32 devices in a mesh: gx: 8 (over y, x, core), gy: 4 (over z).
Axes of the slice: x: 2, y: 2, z: 4, core: 2. Of those that a mesh axis runs over, the one named last changes fastest.
Arguments:
- right_side: float32 [128, 64, 128], P('gx', 'gy'), may hold values from -24 to 24
- material: int32 [128, 64, 128], P('gx', 'gy'), may hold values from 0 to 15
- conductivity: float32 [16], replicated, may hold values from 0.2 to 5
Outputs:
- solution_field: float32 [128, 64, 128], P('gx', 'gy')
The draws below stay inside these ranges and needn't reach their ends.
All inputs are finite; a program needn't handle non-finite values.
Results may differ from the reference program's by a relative error of at most 0.0001.
Values sent between devices are 32-bit elements; how exact they have to be, the bound alone decides.
No kernel may reach another device: no remote copies, remote signals or barrier semaphores. Data moves between devices by JAX's collectives and lax.ppermute only.
A program may use at most 64 MiB of HBM per device.

```python
import math
import jax
import jax.numpy as jnp

CYCLES = 2
COARSE_SWEEPS = 6
NMAT = 16
NX = 128
NY = 64
NZ = 128


def plant(drawn, key, smallest, largest):
    longest = drawn.shape.index(max(drawn.shape))
    spots = []
    for shift in (0, 1):
        where = [jax.random.randint(jax.random.fold_in(key, axis), (), 0, length) for axis, length in enumerate(drawn.shape)]
        where[longest] = (where[longest] + shift) % drawn.shape[longest]
        spots.append(tuple(where))
    return drawn.at[spots[0]].set(smallest).at[spots[1]].set(largest)


def block_levels(own_key, shape, pieces, least, high):
    def one(axis_at, blocks):
        heights = jax.random.uniform(jax.random.fold_in(jax.random.fold_in(own_key, 6), axis_at), (blocks,), jnp.float32, least / len(pieces), high / len(pieces))
        return jnp.repeat(jnp.exp(heights), shape[axis_at] // blocks).reshape((-1,) + (1,) * (len(shape) - axis_at - 1))

    level = one(*pieces[0])
    for cut in pieces[1:]:
        level = level * one(*cut)
    return level


def noise(own_key, extent, deviation, most, pieces=(), dtype=jnp.bfloat16):
    loudness = block_levels(own_key, extent, pieces, -0.22, 0.18) if pieces else 1.0
    values = jax.random.normal(own_key, extent, jnp.float32) * deviation * loudness
    return jnp.minimum(jnp.maximum(values, -most), most).astype(dtype)


def setup_inputs(seed: int = 0) -> dict:
    splits = jax.random.split(jax.random.key(seed), 4)
    return {
        "right_side": noise(splits[0], (NX, NY, NZ), 4.0, 24.0, ((0, 8), (1, 4)), jnp.float32),
        "material": plant(jax.random.randint(splits[1], (NX, NY, NZ), 0, NMAT), jax.random.fold_in(splits[1], 1), 0, NMAT - 1).astype(jnp.int32),
        "conductivity": jnp.clip(jnp.exp(jax.random.uniform(splits[2], (NMAT,), jnp.float32, math.log(0.2), math.log(5.0))), 0.2, 5.0),
    }


OMEGA = 0.8


def neighbours(padded):
    return (padded[2:, 1:-1, 1:-1], padded[:-2, 1:-1, 1:-1],
            padded[1:-1, 2:, 1:-1], padded[1:-1, :-2, 1:-1],
            padded[1:-1, 1:-1, 2:], padded[1:-1, 1:-1, :-2])


def face_set(padded_k, scale):
    centre = padded_k[1:-1, 1:-1, 1:-1]
    faces = tuple(0.5 * scale * (centre + other) for other in neighbours(padded_k))
    total = faces[0] + faces[1] + faces[2] + faces[3] + faces[4] + faces[5]
    return faces, total


def apply_operator(padded_field, faces, total):
    result = total * padded_field[1:-1, 1:-1, 1:-1]
    for weight, other in zip(faces, neighbours(padded_field)):
        result = result - weight * other
    return result


def restrict(field):
    sx, sy, sz = field.shape
    return field.reshape(sx // 2, 2, sy // 2, 2, sz // 2, 2).mean(axis=(1, 3, 5))


def prolong(field):
    return jnp.repeat(jnp.repeat(jnp.repeat(field, 2, 0), 2, 1), 2, 2)


def cycle(levels, level, field, right, first):
    faces, total = levels[level]
    if first:
        field = OMEGA * right / total
    else:
        field = field + OMEGA * (right - apply_operator(jnp.pad(field, 1), faces, total)) / total
    resid = right - apply_operator(jnp.pad(field, 1), faces, total)
    coarse_right = restrict(resid)
    if level == 2:
        cfaces, ctotal = levels[3]
        correction = OMEGA * coarse_right / ctotal
        for sweep in range(COARSE_SWEEPS - 1):
            correction = correction + OMEGA * (coarse_right - apply_operator(jnp.pad(correction, 1), cfaces, ctotal)) / ctotal
    else:
        correction = cycle(levels, level + 1, None, coarse_right, True)
    field = field + prolong(correction)
    field = field + OMEGA * (right - apply_operator(jnp.pad(field, 1), faces, total)) / total
    return field


def reference(right_side, material, conductivity):
    cond = conductivity[material]
    conds = [cond]
    for level in range(3):
        conds.append(restrict(conds[-1]))
    levels = [face_set(jnp.pad(conds[level], 1), 0.25 ** level) for level in range(4)]
    field = jnp.zeros_like(right_side)
    for turn in range(CYCLES):
        field = cycle(levels, 0, field, right_side, turn == 0)
    return field
```

```python
import functools

import jax
import jax.numpy as jnp
from jax import lax
from jax.experimental import pallas as pl
from jax.experimental.pallas import tpu as pltpu
from jax.sharding import PartitionSpec as P

COARSE_SWEEPS = 6
OMEGA = 0.8
KEEP = 1.0 - OMEGA
HALO = 12
SLAB = 4
TRIM = 8
F32 = jnp.float32


def pair_exchange(to_low, to_high, axis):
    count = lax.axis_size(axis)
    odd = lax.axis_index(axis) % 2 == 1
    near = [(i, i ^ 1) for i in range(count) if i ^ 1 < count]
    far = [(i, i + 1) for i in range(1, count - 1, 2)]
    far = far + [(j, i) for i, j in far]
    from_near = lax.ppermute(jnp.where(odd, to_low, to_high), axis, near)
    from_far = lax.ppermute(jnp.where(odd, to_high, to_low), axis, far)
    return jnp.where(odd, from_near, from_far), jnp.where(odd, from_far, from_near)


def everywhere(copies):
    return lax.all_to_all(copies, ("gx", "gy"), 0, 0)


def roll(value, shift, axis):
    return pltpu.roll(value, shift % value.shape[axis], axis=axis)


def lanes_of(value):
    return lax.broadcasted_iota(jnp.int32, value.shape, value.ndim - 1)


def rows_of(value):
    return lax.broadcasted_iota(jnp.int32, value.shape, value.ndim - 2)


def pick_lanes(value, index):
    flat = value.reshape(-1, value.shape[-1])
    index = jnp.broadcast_to(index, flat.shape)
    return jnp.take_along_axis(flat, index, axis=1).reshape(value.shape)


def lane_row(width):
    return lax.broadcasted_iota(jnp.int32, (1, width), 1)


def add_partner(value, apart):
    return value + pick_lanes(value, lane_row(value.shape[-1]) ^ apart)


def local_faces(h, h_next, h_prev, step):
    width = h.shape[-1]
    lane = lanes_of(h)
    wx = h + h_next
    wy = h + roll(h, -1, 1)
    wz = h + jnp.where(lane < width - step, roll(h, -step, 2), 0.0)
    before = jnp.where(lane >= step, roll(h, step, 2), 0.0)
    total = wx + wy + wz + ((h + h_prev) + (h + roll(h, 1, 1)) + (h + before))
    return wx, wy, jnp.where(lane < width - step, wz, 0.0), total


def scaled_inverse(total, h):
    return jnp.where(h > 0.0, OMEGA / total, 0.0)


def local_spread(v, v_next, from_prev, wx, wy, wz, step):
    return (
        (wx * v_next + from_prev)
        + (wy * roll(v, -1, 1) + roll(wy * v, 1, 1))
        + (wz * roll(v, -step, 2) + roll(wz * v, step, 2))
    )


def shift_up(value):
    return jnp.concatenate([value[1:], jnp.zeros_like(value[:1])], axis=0)


def shift_down(value):
    return jnp.concatenate([jnp.zeros_like(value[:1]), value[:-1]], axis=0)


def next_x(value, step):
    turned = roll(value, -step, 2)
    return jnp.where(lanes_of(value) < value.shape[-1] - step, turned, shift_up(turned))


def prev_x(value, step):
    turned = roll(value, step, 2)
    return jnp.where(lanes_of(value) >= step, turned, shift_down(turned))


def whole_faces(h, span, xstep, zstep):
    in_span = lanes_of(h) % span
    row = rows_of(h)
    not_last_z, not_first_z = in_span < span - zstep, in_span >= zstep
    not_last_y, not_first_y = row < h.shape[1] - 1, row >= 1
    wx = h + next_x(h, xstep)
    wy = h + jnp.where(not_last_y, roll(h, -1, 1), 0.0)
    wz = h + jnp.where(not_last_z, roll(h, -zstep, 2), 0.0)
    back = h + prev_x(h, xstep)
    back = back + (h + jnp.where(not_first_y, roll(h, 1, 1), 0.0))
    back = back + (h + jnp.where(not_first_z, roll(h, zstep, 2), 0.0))
    total = wx + wy + wz + back
    return wx, jnp.where(not_last_y, wy, 0.0), jnp.where(not_last_z, wz, 0.0), OMEGA / total


def whole_spread(v, wx, wy, wz, xstep, zstep):
    return (
        (wx * next_x(v, xstep) + prev_x(wx * v, xstep))
        + (wy * roll(v, -1, 1) + roll(wy * v, 1, 1))
        + (wz * roll(v, -zstep, 2) + roll(wz * v, zstep, 2))
    )


def slabs(first, last, body, size=SLAB):
    def step(i, carry):
        body(first + i * size)
        return carry

    lax.fori_loop(0, (last - first) // size, step, 0)


def part(ref, start, size=SLAB, rows=slice(None)):
    return ref[pl.ds(start, size), rows, :]


def halve_rows(value, buffer):
    rows = value.shape[1]
    buffer[...] = value
    return buffer[:, pl.ds(0, rows // 2, stride=2), :] + buffer[:, pl.ds(1, rows // 2, stride=2), :]


def sum_blocks(value, buffer, step):
    pairs = value.reshape((value.shape[0] // 2, 2) + value.shape[1:])
    return add_partner(halve_rows(pairs[:, 0] + pairs[:, 1], buffer), step)


def double_rows(ref, start, size, value):
    rows = value.shape[1]
    ref[pl.ds(start, size), pl.ds(0, rows, stride=2), :] = value
    ref[pl.ds(start, size), pl.ds(1, rows, stride=2), :] = value


def pack_block(values, buffer):
    blocks, rows, width = values[0].shape
    span = width // blocks
    for n, value in enumerate(values):
        buffer[:, n * rows : (n + 1) * rows, :] = value
    used = rows * len(values)
    lane = lane_row(width)
    packed = None
    for x in range(blocks):
        picked = pick_lanes(buffer[x], (lane % span) * blocks)[:used]
        packed = picked if packed is None else jnp.where(lanes_of(picked) // span == x, picked, packed)
    return packed


def coarse_cycle(g2, level2, level3, buffer):
    wx2, wy2, wz2, inv2 = level2
    wx3, wy3, wz3, inv3 = level3
    width = g2.shape[-1]
    span = width // 4
    v2 = inv2 * g2
    r2 = KEEP * g2 + whole_spread(v2, wx2, wy2, wz2, span, 1)
    g3 = 0.125 * halve_rows(add_partner(add_partner(r2, 1), span), buffer)
    v3 = inv3 * g3
    for _ in range(COARSE_SWEEPS - 1):
        v3 = KEEP * v3 + inv3 * (g3 + whole_spread(v3, wx3, wy3, wz3, 2 * span, 2))
    double_rows(buffer, 0, v3.shape[0], v3)
    u2 = v2 + buffer[...]
    return KEEP * u2 + inv2 * (g2 + whole_spread(u2, wx2, wy2, wz2, span, 1))


def spread_out(e2, wide, doubled):
    count, rows, width = e2.shape
    block_rows = rows // lax.axis_size("gy")
    span = width // 4
    wide[...] = jnp.zeros(wide.shape, F32)
    wide[1 : count + 1, 8 : 8 + rows, :] = e2
    gx, gy = lax.axis_index("gx"), lax.axis_index("gy")
    near = wide[pl.ds(gx, 3), pl.ds(gy * block_rows + 8 - block_rows, 16), :]
    lane = lane_row(width)
    kept = 3 * block_rows
    for j in range(1, 11):
        value = pick_lanes(near[j // 4], (j % 4) * span + lane // 4)[:kept]
        doubled[j, pl.ds(0, kept, stride=2), :] = value
        doubled[j, pl.ds(1, kept, stride=2), :] = value


def first_kernel(
    ext, table,
    packed, wx0, wy0, wz0, inv0, tot0, v0, wx1, wy1, wz1, inv1, v1, g1,
    h0, h1, buf0, buf1, buf2, bufp,
):
    planes, rows, width = ext.shape[1:]
    planes1 = planes // 2
    zero = jnp.zeros((1, rows, width), F32)
    for ref in (h0, wx0, v0):
        ref[0:1] = zero
        ref[planes + 1 : planes + 2] = zero
    for ref in (h1, wx1, v1):
        ref[0:1] = zero[:, : rows // 2]
        ref[planes1 + 1 : planes1 + 2] = zero[:, : rows // 2]

    def look_up(i):
        which = part(ext.at[1], i).astype(jnp.int32).reshape(SLAB * rows, width)
        values = jnp.broadcast_to(table[...], which.shape)
        h0[pl.ds(i + 1, SLAB)] = jnp.take_along_axis(values, which, axis=1).reshape(SLAB, rows, width)

    slabs(0, planes, look_up)

    def faces0(i):
        h = part(h0, i + 1)
        wx, wy, wz, total = local_faces(h, part(h0, i + 2), part(h0, i), 1)
        inv = scaled_inverse(total, h)
        wx0[pl.ds(i + 1, SLAB)] = wx
        wy0[pl.ds(i, SLAB)] = wy
        wz0[pl.ds(i, SLAB)] = wz
        tot0[pl.ds(i, SLAB)] = total
        inv0[pl.ds(i, SLAB)] = inv
        v0[pl.ds(i + 1, SLAB)] = inv * part(ext.at[0], i)
        h1[pl.ds(i // 2 + 1, SLAB // 2)] = sum_blocks(h, buf0, 1) * (1.0 / 32.0)

    slabs(0, planes, faces0)

    def resid0(i):
        v = part(v0, i + 1)
        spread = local_spread(
            v, part(v0, i + 2), part(wx0, i) * part(v0, i),
            part(wx0, i + 1), part(wy0, i), part(wz0, i), 1,
        )
        r = KEEP * part(ext.at[0], i) + spread
        g1[pl.ds(i // 2, SLAB // 2)] = sum_blocks(r, buf0, 1) * 0.125

    slabs(0, planes, resid0)

    def faces1(i):
        h = part(h1, i + 1)
        wx, wy, wz, total = local_faces(h, part(h1, i + 2), part(h1, i), 2)
        inv = scaled_inverse(total, h)
        wx1[pl.ds(i + 1, SLAB)] = wx
        wy1[pl.ds(i, SLAB)] = wy
        wz1[pl.ds(i, SLAB)] = wz
        inv1[pl.ds(i, SLAB)] = inv
        v1[pl.ds(i + 1, SLAB)] = inv * part(g1, i)

    slabs(0, planes1, faces1)

    own = slice(8, 16)
    low = HALO // 2
    size = planes1 - HALO
    v = part(v1, low + 1, size)
    r1 = KEEP * part(g1, low, size) + local_spread(
        v, part(v1, low + 2, size), part(wx1, low, size) * part(v1, low, size),
        part(wx1, low + 1, size), part(wy1, low, size), part(wz1, low, size), 2,
    )
    g2 = sum_blocks(r1[:, own], buf1, 2) * 0.125
    h2 = sum_blocks(part(h1, low + 1, size, own), buf2, 2) * (1.0 / 32.0)
    chunk = pack_block([g2, h2], bufp)

    def copy_out(i, carry):
        packed[i] = chunk
        return carry

    lax.fori_loop(0, packed.shape[0], copy_out, 0)


def fine_down(v0, wx0, wy0, wz0, tot0, ext, g1, v1, wx1, wy1, wz1, inv1, buf0, buf1, bufp, rows):
    half = rows.start // 2

    def resid0(i):
        v = part(v0, i + 1)
        spread = local_spread(
            v, part(v0, i + 2), part(wx0, i, rows=rows) * part(v0, i),
            part(wx0, i + 1, rows=rows), part(wy0, i, rows=rows), part(wz0, i, rows=rows), 1,
        )
        r = (part(ext.at[0], i, rows=rows) - part(tot0, i, rows=rows) * v) + spread
        coarse = sum_blocks(r, buf0, 1) * 0.125
        g1[pl.ds(i // 2, SLAB // 2), half : half + coarse.shape[1], :] = coarse

    slabs(HALO - 4, ext.shape[1] - HALO + 4, resid0)
    low = HALO // 2
    size = ext.shape[1] // 2 - HALO
    v1[pl.ds(low - 1, size + 4)] = part(inv1, low - 2, size + 4) * part(g1, low - 2, size + 4)
    v = part(v1, low + 1, size)
    r1 = KEEP * part(g1, low, size) + local_spread(
        v, part(v1, low + 2, size), part(wx1, low, size) * part(v1, low, size),
        part(wx1, low + 1, size), part(wy1, low, size), part(wz1, low, size), 2,
    )
    g2 = sum_blocks(r1[:, 8:16], buf1, 2) * 0.125
    return pack_block([g2], bufp)


def level1_up(first, last, doubled, v1, g1, wx1, wy1, wz1, inv1, u1, e0):
    count = last - first + 2

    def correct(i):
        e = doubled[pl.ds(i // 2 + 1, SLAB // 2)]
        e = jnp.broadcast_to(e[:, None], (SLAB // 2, 2) + e.shape[1:]).reshape((SLAB,) + e.shape[1:])
        u1[pl.ds(i + 1, SLAB)] = part(v1, i + 1) + e

    start = (first - 1) // 2 * 2
    stop = start + -(-(first - 1 - start + count) // SLAB) * SLAB
    slabs(start, stop, correct)

    def sweep(i):
        u = part(u1, i + 1)
        spread = local_spread(
            u, part(u1, i + 2), part(wx1, i) * part(u1, i),
            part(wx1, i + 1), part(wy1, i), part(wz1, i), 2,
        )
        double_rows(e0, i, SLAB, KEEP * u + part(inv1, i) * (part(g1, i) + spread))

    slabs(first, last, sweep)


def second_kernel(
    got, ext, wx0, wy0, wz0, inv0, tot0, v0, wx1, wy1, wz1, inv1, v1, g1,
    packed, v0n, v1n, g1n, wx2, wy2, wz2, inv2, wx3, wy3, wz3, inv3,
    g2, h2, buf2, wide, doubled, u1, e0, u0, v0m, buf0, buf1, bufp,
):
    count, rows2, width = g2.shape
    gy_count = lax.axis_size("gy")
    block = rows2 // gy_count

    def unpack(i, carry):
        for y in range(gy_count):
            both = got[i * gy_count + y]
            g2[i, y * block : (y + 1) * block, :] = both[:block]
            h2[i, y * block : (y + 1) * block, :] = both[block:]
        return carry

    lax.fori_loop(0, count, unpack, 0)

    span = width // 4
    h = h2[...]
    level2 = whole_faces(h, span, span, 1)
    h3 = halve_rows(add_partner(add_partner(h, 1), span), buf2) * (1.0 / 32.0)
    level3 = whole_faces(h3, span, 2 * span, 2)
    for ref, value in zip((wx2, wy2, wz2, inv2, wx3, wy3, wz3, inv3), level2 + level3):
        ref[...] = value
    spread_out(coarse_cycle(g2[...], level2, level3, buf2), wide, doubled)

    planes = ext.shape[1]
    rows = slice(TRIM, ext.shape[2] - TRIM)
    level1_up(2, planes // 2 - 2, doubled, v1, g1, wx1, wy1, wz1, inv1, u1, e0)

    def correct(i):
        e = part(e0, i // 2, SLAB // 2, rows)
        e = jnp.broadcast_to(e[:, None], (SLAB // 2, 2) + e.shape[1:]).reshape((SLAB,) + e.shape[1:])
        u0[pl.ds(i + 1, SLAB)] = part(v0, i + 1, rows=rows) + e

    slabs(HALO - 8, planes - HALO + 8, correct)

    def sweep(source, target):
        def body(i):
            u = part(source, i + 1)
            spread = local_spread(
                u, part(source, i + 2), part(wx0, i, rows=rows) * part(source, i),
                part(wx0, i + 1, rows=rows), part(wy0, i, rows=rows), part(wz0, i, rows=rows), 1,
            )
            target[pl.ds(i + 1, SLAB)] = KEEP * u + part(inv0, i, rows=rows) * (
                part(ext.at[0], i, rows=rows) + spread
            )

        return body

    slabs(HALO - 6, planes - HALO + 6, sweep(u0, v0m))
    slabs(HALO - 6, planes - HALO + 6, sweep(v0m, v0n))
    g1n[...] = jnp.zeros(g1n.shape, F32)
    v1n[...] = jnp.zeros(v1n.shape, F32)
    chunk = fine_down(
        v0n, wx0, wy0, wz0, tot0, ext, g1n, v1n, wx1, wy1, wz1, inv1, buf0, buf1, bufp, rows
    )

    def copy_out(i, carry):
        packed[i] = chunk
        return carry

    lax.fori_loop(0, packed.shape[0], copy_out, 0)


def third_kernel(
    got, ext, wx0, wy0, wz0, inv0, v0, wx1, wy1, wz1, inv1, v1, g1,
    wx2, wy2, wz2, inv2, wx3, wy3, wz3, inv3,
    out,
    g2, buf2, wide, doubled, u1, e0, u0,
):
    count, rows2, width = g2.shape
    gy_count = lax.axis_size("gy")
    block = rows2 // gy_count

    def unpack(i, carry):
        for y in range(gy_count):
            g2[i, y * block : (y + 1) * block, :] = got[i * gy_count + y]
        return carry

    lax.fori_loop(0, count, unpack, 0)
    level2 = (wx2[...], wy2[...], wz2[...], inv2[...])
    level3 = (wx3[...], wy3[...], wz3[...], inv3[...])
    spread_out(coarse_cycle(g2[...], level2, level3, buf2), wide, doubled)

    planes = ext.shape[1]
    rows = slice(TRIM, ext.shape[2] - TRIM)
    level1_up(HALO // 2 - 2, planes // 2 - HALO // 2 + 2, doubled, v1, g1, wx1, wy1, wz1, inv1, u1, e0)

    def correct(i):
        e = part(e0, i // 2, SLAB // 2, rows)
        e = jnp.broadcast_to(e[:, None], (SLAB // 2, 2) + e.shape[1:]).reshape((SLAB,) + e.shape[1:])
        u0[pl.ds(i + 1, SLAB)] = part(v0, i + 1) + e

    slabs(HALO - 2, planes - HALO + 2, correct)
    own = slice(8, 8 + out.shape[1])

    def sweep(i):
        u = part(u0, i + 1)
        spread = local_spread(
            u, part(u0, i + 2), part(wx0, i, rows=rows) * part(u0, i),
            part(wx0, i + 1, rows=rows), part(wy0, i, rows=rows), part(wz0, i, rows=rows), 1,
        )
        result = KEEP * u + part(inv0, i, rows=rows) * (part(ext.at[0], i, rows=rows) + spread)
        out[pl.ds(i - HALO, SLAB)] = result[:, own]

    slabs(HALO, planes - HALO, sweep)


def kernel_call(body, outs, scratch, args):
    def size(shape):
        total = 4
        for length in shape:
            total *= length
        return total

    shapes = [a.shape for a in args] + list(outs) + list(scratch)
    limit = sum(size(s) for s in shapes) + (8 << 20)
    return pl.pallas_call(
        body,
        out_shape=[jax.ShapeDtypeStruct(s, F32) for s in outs],
        in_specs=[pl.BlockSpec(memory_space=pltpu.VMEM)] * len(args),
        out_specs=[pl.BlockSpec(memory_space=pltpu.VMEM)] * len(outs),
        scratch_shapes=[pltpu.VMEM(s, F32) for s in scratch],
        compiler_params=pltpu.CompilerParams(vmem_limit_bytes=limit),
    )(*args)


def local(right_side, material, conductivity):
    bx, by, bz = right_side.shape
    gx_count, gy_count = lax.axis_size("gx"), lax.axis_size("gy")
    devices = gx_count * gy_count

    block = jnp.stack([right_side, (material + 1).astype(F32)])
    below, above = pair_exchange(block, block, "gy")
    block = jnp.concatenate([below, block, above], axis=2)
    below, above = pair_exchange(block[:, :HALO], block[:, bx - HALO :], "gx")
    ext = jnp.concatenate([below, block, above], axis=1)
    table = jnp.pad(0.5 * conductivity, (1, bz - 1 - conductivity.shape[0]))[None]

    X, Y = bx + 2 * HALO, 3 * by
    X1, Y1 = X // 2, Y // 2
    T = Y - 2 * TRIM
    xb, yb = bx // 4, by // 4
    full0, pad0 = (X, Y, bz), (X + 2, Y, bz)
    full1, pad1 = (X1, Y1, bz), (X1 + 2, Y1, bz)
    packed, wx0, wy0, wz0, inv0, tot0, v0, wx1, wy1, wz1, inv1, v1, g1 = kernel_call(
        first_kernel,
        [(devices, 2 * yb, bz), pad0, full0, full0, full0, full0, pad0, pad1, full1, full1, full1, pad1, full1],
        [pad0, pad1, (SLAB // 2, Y, bz), (xb, 2 * yb, bz), (xb, 2 * yb, bz), (xb, 8, bz)],
        [ext, table],
    )
    got = everywhere(packed)
    level2 = (gx_count, gy_count * yb, bz)
    level3 = (gx_count, gy_count * yb // 2, bz)
    coarse_scratch = [
        level2, (gx_count + 2, gy_count * yb + 16, bz), (3 * xb, Y1, bz), pad1, (X1, Y, bz), (X + 2, T, bz),
    ]
    packed, v0, v1, g1, *levels = kernel_call(
        second_kernel,
        [(devices, yb, bz), (X + 2, T, bz), pad1, full1] + [level2] * 4 + [level3] * 4,
        [level2, level2] + coarse_scratch
        + [(X + 2, T, bz), (SLAB // 2, T, bz), (xb, 2 * yb, bz), (xb, 8, bz)],
        [got, ext, wx0, wy0, wz0, inv0, tot0, v0, wx1, wy1, wz1, inv1, v1, g1],
    )
    got = everywhere(packed)
    (out,) = kernel_call(
        third_kernel,
        [(bx, by, bz)],
        [level2] + coarse_scratch,
        [got, ext, wx0, wy0, wz0, inv0, v0, wx1, wy1, wz1, inv1, v1, g1] + levels,
    )
    return out


def solution(mesh):
    return jax.shard_map(
        local,
        mesh=mesh,
        in_specs=(P("gx", "gy", None), P("gx", "gy", None), P()),
        out_specs=P("gx", "gy", None),
        check_vma=False,
    )
```

```python
import jax
import jax.numpy as jnp
from jax import lax
from jax.experimental import pallas as pl
from jax.experimental.pallas import tpu as pltpu
from jax.sharding import PartitionSpec as P

COARSE_SWEEPS = 6
OMEGA = 0.8
KEEP = 1.0 - OMEGA
HALO = 12
NEAR = 8
FAR = HALO - NEAR
BASE = 8
F32 = jnp.float32


def near_partner(index, count):
    return index ^ 1 if index ^ 1 < count else index


def far_partner(index, count):
    return (index - 1 ^ 1) + 1


def route(axis, far):
    gx_count, gy_count = lax.axis_size("gx"), lax.axis_size("gy")
    pairs = []
    for x in range(gx_count):
        for y in range(gy_count):
            if axis == "gx":
                if not far:
                    a, b = near_partner(x, gx_count), y
                elif 0 < x < gx_count - 1:
                    a, b = far_partner(x, gx_count), y
                else:
                    a, b = x, near_partner(y, gy_count)
            else:
                if not far:
                    a, b = x, near_partner(y, gy_count)
                elif 0 < y < gy_count - 1:
                    a, b = x, far_partner(y, gy_count)
                else:
                    a, b = near_partner(x, gx_count), y
            pairs.append((x * gy_count + y, a * gy_count + b))
    return pairs


def trade(to_near, to_far, axis):
    from_far = lax.ppermute(to_far, ("gx", "gy"), route(axis, True))
    from_near = lax.ppermute(to_near, ("gx", "gy"), route(axis, False))
    return from_near, from_far


def everywhere(copies):
    return lax.all_to_all(copies, ("gx", "gy"), 0, 0)


def is_odd(axis):
    return lax.axis_index(axis) % 2 == 1


def has_below(axis):
    return lax.axis_index(axis) > 0


def has_above(axis):
    return lax.axis_index(axis) < lax.axis_size(axis) - 1


def below(near, far, axis):
    return jnp.where(has_below(axis), jnp.where(is_odd(axis), near, far), 0.0)


def above(near, far, axis):
    return jnp.where(has_above(axis), jnp.where(is_odd(axis), far, near), 0.0)


def roll(value, shift, axis):
    return pltpu.roll(value, shift % value.shape[axis], axis=axis)


def lanes_of(value):
    return lax.broadcasted_iota(jnp.int32, value.shape, value.ndim - 1)


def rows_of(value):
    return lax.broadcasted_iota(jnp.int32, value.shape, value.ndim - 2)


def lane_row(width):
    return lax.broadcasted_iota(jnp.int32, (1, width), 1)


def pick_lanes(value, index):
    flat = value.reshape(-1, value.shape[-1])
    index = jnp.broadcast_to(index, flat.shape)
    return jnp.take_along_axis(flat, index, axis=1).reshape(value.shape)


def add_partner(value, apart):
    return value + pick_lanes(value, lane_row(value.shape[-1]) ^ apart)


def shift_up(value):
    return jnp.concatenate([value[1:], jnp.zeros_like(value[:1])], axis=0)


def shift_down(value):
    return jnp.concatenate([jnp.zeros_like(value[:1]), value[:-1]], axis=0)


def next_x(value, step):
    turned = roll(value, -step, 2)
    return jnp.where(lanes_of(value) < value.shape[-1] - step, turned, shift_up(turned))


def prev_x(value, step):
    turned = roll(value, step, 2)
    return jnp.where(lanes_of(value) >= step, turned, shift_down(turned))


def whole_faces(h, span, xstep, zstep):
    in_span = lanes_of(h) % span
    row = rows_of(h)
    not_last_z, not_first_z = in_span < span - zstep, in_span >= zstep
    not_last_y, not_first_y = row < h.shape[1] - 1, row >= 1
    wx = h + next_x(h, xstep)
    wy = h + jnp.where(not_last_y, roll(h, -1, 1), 0.0)
    wz = h + jnp.where(not_last_z, roll(h, -zstep, 2), 0.0)
    back = h + prev_x(h, xstep)
    back = back + (h + jnp.where(not_first_y, roll(h, 1, 1), 0.0))
    back = back + (h + jnp.where(not_first_z, roll(h, zstep, 2), 0.0))
    total = wx + wy + wz + back
    return wx, jnp.where(not_last_y, wy, 0.0), jnp.where(not_last_z, wz, 0.0), OMEGA / total


def whole_spread(v, wx, wy, wz, xstep, zstep):
    return (
        (wx * next_x(v, xstep) + prev_x(wx * v, xstep))
        + (wy * roll(v, -1, 1) + roll(wy * v, 1, 1))
        + (wz * roll(v, -zstep, 2) + roll(wz * v, zstep, 2))
    )


def read(array, start, size, top, rows, dx=0, dy=0):
    ref, planes_off, rows_off = array
    return ref[pl.ds(start + planes_off + dx, size), pl.ds(top + rows_off + dy, rows), :]


def write(array, start, top, value):
    ref, planes_off, rows_off = array
    ref[pl.ds(start + planes_off, value.shape[0]), pl.ds(top + rows_off, value.shape[1]), :] = value


def slabs(first, last, size, body):
    if first + size == last:
        body(first)
        return

    def step(i, carry):
        body(first + i * size)
        return carry

    lax.fori_loop(0, (last - first) // size, step, 0)


def faces(h, window, step):
    here = read(h, *window)
    lane = lanes_of(here)
    width = here.shape[-1]
    not_last = lane < width - step
    wx = here + read(h, *window, dx=1)
    wy = here + read(h, *window, dy=1)
    wz = here + jnp.where(not_last, roll(here, -step, 2), 0.0)
    back = (here + read(h, *window, dx=-1)) + (here + read(h, *window, dy=-1))
    back = back + (here + jnp.where(lane >= step, roll(here, step, 2), 0.0))
    total = (wx + wy + wz) + back
    inverse = jnp.where(here > 0.0, OMEGA / total, 0.0)
    return here, wx, wy, jnp.where(not_last, wz, 0.0), total, inverse


def spread(v, weights, window, step):
    wx, wy, wz = weights
    here = read(v, *window)
    wz = read(wz, *window)
    return here, (
        (read(wx, *window) * read(v, *window, dx=1) + read(wx, *window, dx=-1) * read(v, *window, dx=-1))
        + (read(wy, *window) * read(v, *window, dy=1) + read(wy, *window, dy=-1) * read(v, *window, dy=-1))
        + (wz * roll(here, -step, 2) + roll(wz * here, step, 2))
    )


def halve_rows(value, buffer):
    count, rows, _ = value.shape
    buffer[0:count, 0:rows, :] = value
    return (
        buffer[0:count, pl.ds(0, rows // 2, stride=2), :] + buffer[0:count, pl.ds(1, rows // 2, stride=2), :]
    )


def sum_blocks(value, buffer, step):
    pairs = value.reshape((value.shape[0] // 2, 2) + value.shape[1:])
    return add_partner(halve_rows(pairs[:, 0] + pairs[:, 1], buffer), step)


def double_rows(ref, start, value):
    count, rows, _ = value.shape
    ref[pl.ds(start, count), pl.ds(0, rows, stride=2), :] = value
    ref[pl.ds(start, count), pl.ds(1, rows, stride=2), :] = value


def double_planes(value):
    wide = jnp.broadcast_to(value[:, None], (value.shape[0], 2) + value.shape[1:])
    return wide.reshape((2 * value.shape[0],) + value.shape[1:])


def pack_block(values, buffer):
    blocks, rows, width = values[0].shape
    span = width // blocks
    for n, value in enumerate(values):
        buffer[:, n * rows : (n + 1) * rows, :] = value
    used = rows * len(values)
    lane = lane_row(width)
    packed = None
    for x in range(blocks):
        picked = pick_lanes(buffer[x], (lane % span) * blocks)[:used]
        packed = picked if packed is None else jnp.where(lanes_of(picked) // span == x, picked, packed)
    return packed


def send_to_all(packed, chunk):
    def copy_out(i, carry):
        packed[i] = chunk
        return carry

    lax.fori_loop(0, packed.shape[0], copy_out, 0)


def coarse_cycle(g2, level2, level3, buffer):
    wx2, wy2, wz2, inv2 = level2
    wx3, wy3, wz3, inv3 = level3
    width = g2.shape[-1]
    span = width // 4
    v2 = inv2 * g2
    r2 = KEEP * g2 + whole_spread(v2, wx2, wy2, wz2, span, 1)
    g3 = 0.125 * halve_rows(add_partner(add_partner(r2, 1), span), buffer)
    v3 = inv3 * g3
    for _ in range(COARSE_SWEEPS - 1):
        v3 = KEEP * v3 + inv3 * (g3 + whole_spread(v3, wx3, wy3, wz3, 2 * span, 2))
    double_rows(buffer, 0, v3)
    u2 = v2 + buffer[...]
    return KEEP * u2 + inv2 * (g2 + whole_spread(u2, wx2, wy2, wz2, span, 1))


def spread_out(e2, wide, doubled, planes):
    count, rows, width = e2.shape
    block = rows // lax.axis_size("gy")
    span = width // 4
    wide[0:1] = jnp.zeros((1,) + wide.shape[1:], F32)
    wide[count + 1 : count + 2] = jnp.zeros((1,) + wide.shape[1:], F32)
    wide[1 : count + 1, 0:8, :] = jnp.zeros((count, 8, width), F32)
    wide[1 : count + 1, rows + 8 : rows + 16, :] = jnp.zeros((count, 8, width), F32)
    wide[1 : count + 1, 8 : 8 + rows, :] = e2
    gx, gy = lax.axis_index("gx"), lax.axis_index("gy")
    around = wide[pl.ds(gx, 3), pl.ds(gy * block + 8 - block, 16), :]
    lane = lane_row(width)
    kept = 3 * block
    for j in planes:
        value = pick_lanes(around[j // 4], (j % 4) * span + lane // 4)[:kept]
        doubled[j, pl.ds(0, kept, stride=2), :] = value
        doubled[j, pl.ds(1, kept, stride=2), :] = value


def row_starts(axis, block):
    odd = is_odd(axis)
    low = (0, NEAR)
    high = (block - NEAR, block - HALO)
    to_near = [jnp.where(odd, a, b) for a, b in zip(low, high)]
    to_far = [jnp.where(odd, b, a) for a, b in zip(low, high)]
    return to_near, to_far


def pack_rows(source, starts, first, last, target):
    count = source.shape[0]
    half = (last - first) // 2
    target[0:count] = source[:, pl.ds(starts[0], NEAR), :]
    target[count : count + half, 0:FAR, :] = source[first : first + half, pl.ds(starts[1], FAR), :]
    target[count : count + half, FAR:NEAR, :] = source[first + half : last, pl.ds(starts[1], FAR), :]


def unpack_rows(target, planes_off, top, bottom, count, first, last, near, far):
    half = (last - first) // 2
    for choose, at, edge in ((below, top - NEAR, top - HALO), (above, bottom, bottom + NEAR)):
        target[planes_off : planes_off + count, at : at + NEAR, :] = choose(near[0:count], far[0:count], "gy")
        strips = choose(near[count : count + half], far[count : count + half], "gy")
        target[planes_off + first : planes_off + first + half, edge : edge + FAR, :] = strips[:, 0:FAR]
        target[planes_off + first + half : planes_off + last, edge : edge + FAR, :] = strips[:, FAR:NEAR]


def start_kernel(right, material, cond, h, k_near, k_far, g_near, g_far, table):
    planes, rows, width = material.shape
    table[0:1, 0 : cond.shape[1]] = cond[...]
    which = material[...].reshape(planes * rows, width)
    values = jnp.broadcast_to(0.5 * table[0:1, :], which.shape)
    h[...] = jnp.take_along_axis(values, which, axis=1).reshape(material.shape)
    odd = is_odd("gx")
    k_near[...] = h[pl.ds(jnp.where(odd, 0, planes - HALO), HALO)]
    k_far[...] = h[pl.ds(jnp.where(odd, planes - HALO, 0), HALO)]
    to_near, to_far = row_starts("gy", rows)
    pack_rows(right, to_near, 0, planes, g_near)
    pack_rows(right, to_far, 0, planes, g_far)


def far_planes(planes):
    return HALO - FAR + 1, planes - HALO + FAR - 1


def k_kernel(h, near, far, wide, k_near, k_far):
    block = h.shape[0]
    wide[0:HALO] = below(near[...], far[...], "gx")
    wide[HALO : HALO + block] = h[...]
    wide[HALO + block :] = above(near[...], far[...], "gx")
    first, last = far_planes(wide.shape[0])
    to_near, to_far = row_starts("gy", h.shape[1])
    pack_rows(wide, to_near, first, last, k_near)
    pack_rows(wide, to_far, first, last, k_far)


def plane_strips(rows):
    strips, at = [], 0
    for distance in range(1, HALO):
        cut = (distance // 4) * 4
        tiles = (rows - 2 * cut) // 8
        strips.append((distance, cut, tiles, at))
        at += tiles
    return strips, at


def g_kernel(right, near, far, wide, g_near, g_far):
    block, rows, _ = right.shape
    top = BASE // 2
    wide[:, top + HALO : top + HALO + rows, :] = right[...]
    unpack_rows(wide, 0, top + HALO, top + HALO + rows, block, 0, block, near, far)
    odd = is_odd("gx")
    strips, _ = plane_strips(rows + 2 * HALO)
    for distance, cut, tiles, at in strips:
        low, high = distance - 1, block - distance
        for target, plane in ((g_near, jnp.where(odd, low, high)), (g_far, jnp.where(odd, high, low))):
            for tile in range(tiles):
                target[at + tile] = wide[plane, top + cut + 8 * tile : top + cut + 8 * tile + 8, :]


def first_kernel(
    k_wide, k_near, k_far, g_wide, g_near, g_far,
    packed, g0, wx0, wy0, wz0, inv0, tot0, v0, wx1, wy1, wz1, inv1, v1, g1,
    h0, h1, buf0, bufp,
):
    top = BASE // 2
    planes, rows, width = k_wide.shape
    own = slice(HALO, planes - HALO)
    h0[1 : planes + 1, top + HALO : top + HALO + rows, :] = k_wide[...]
    first, last = far_planes(planes)
    unpack_rows(h0, 1, top + HALO, top + HALO + rows, planes, first, last, k_near, k_far)
    g0[own] = g_wide[...]
    rows = rows + 2 * HALO
    strips, _ = plane_strips(rows)
    for distance, cut, tiles, at in strips:
        for choose, plane in ((below, HALO - distance), (above, planes - HALO - 1 + distance)):
            value = choose(g_near[at : at + tiles], g_far[at : at + tiles], "gx")
            g0[plane, top + cut : top + cut + 8 * tiles, :] = value.reshape(8 * tiles, width)

    aH0, aG0 = (h0, 1, top), (g0, 0, top)
    aWX0, aV0 = (wx0, 1, BASE), (v0, 1, BASE)
    aWY0, aWZ0, aINV0, aTOT0 = ((ref, 0, BASE) for ref in (wy0, wz0, inv0, tot0))
    aH1, aWX1, aV1 = (h1, 1, BASE), (wx1, 1, BASE), (v1, 1, BASE)
    aWY1, aWZ1, aINV1, aG1 = ((ref, 0, BASE) for ref in (wy1, wz1, inv1, g1))
    size = planes // 4

    def faces0(i):
        window = (i, size, 0, rows)
        here, wx, wy, wz, total, inverse = faces(aH0, window, 1)
        write(aWX0, i, 0, wx)
        write(aWY0, i, 0, wy)
        write(aWZ0, i, 0, wz)
        write(aTOT0, i, 0, total)
        write(aINV0, i, 0, inverse)
        write(aV0, i, 0, inverse * read(aG0, *window))
        write(aH1, i // 2, 0, sum_blocks(here, buf0, 1) * (1.0 / 32.0))

    slabs(0, planes, size, faces0)

    def resid0(i):
        window = (i, size, 0, rows)
        _, around = spread(aV0, (aWX0, aWY0, aWZ0), window, 1)
        write(aG1, i // 2, 0, sum_blocks(KEEP * read(aG0, *window) + around, buf0, 1) * 0.125)

    slabs(0, planes, size, resid0)

    planes1, rows1 = planes // 2, -(-rows // 16) * 8

    def faces1(i):
        window = (i, planes1, 0, rows1)
        _, wx, wy, wz, total, inverse = faces(aH1, window, 2)
        write(aWX1, i, 0, wx)
        write(aWY1, i, 0, wy)
        write(aWZ1, i, 0, wz)
        write(aINV1, i, 0, inverse)
        write(aV1, i, 0, inverse * read(aG1, *window))

    slabs(0, planes1, planes1, faces1)

    low = HALO // 2
    window = (low, planes1 - HALO, low, rows // 2 - HALO)
    _, around = spread(aV1, (aWX1, aWY1, aWZ1), window, 2)
    g2 = sum_blocks(KEEP * read(aG1, *window) + around, buf0, 2) * 0.125
    h2 = sum_blocks(read(aH1, *window), buf0, 2) * (1.0 / 32.0)
    send_to_all(packed, pack_block([g2, h2], bufp))


def second_kernel(
    got, g0, wx0, wy0, wz0, inv0, tot0, v0, wx1, wy1, wz1, inv1, v1, g1,
    packed, v0n, v1n, g1n, wx2, wy2, wz2, inv2, wx3, wy3, wz3, inv3,
    g2, h2, buf2, wide, doubled, u1, e0, u0, v0m, buf0, bufp,
):
    count, rows2, width = g2.shape
    gy_count = lax.axis_size("gy")
    block2 = rows2 // gy_count

    def unpack(i, carry):
        for y in range(gy_count):
            both = got[i * gy_count + y]
            g2[i, y * block2 : (y + 1) * block2, :] = both[:block2]
            h2[i, y * block2 : (y + 1) * block2, :] = both[block2:]
        return carry

    lax.fori_loop(0, count, unpack, 0)

    span = width // 4
    h = h2[...]
    level2 = whole_faces(h, span, span, 1)
    h3 = halve_rows(add_partner(add_partner(h, 1), span), buf2) * (1.0 / 32.0)
    level3 = whole_faces(h3, span, 2 * span, 2)
    for ref, value in zip((wx2, wy2, wz2, inv2, wx3, wy3, wz3, inv3), level2 + level3):
        ref[...] = value
    spread_out(coarse_cycle(g2[...], level2, level3, buf2), wide, doubled, range(1, 11))

    top = BASE // 2
    planes = g0.shape[0]
    block = planes - 2 * HALO
    aG0 = (g0, 0, top)
    w0 = (wx0, 1, BASE), (wy0, 0, BASE), (wz0, 0, BASE)
    aINV0, aTOT0, aV0 = (inv0, 0, BASE), (tot0, 0, BASE), (v0, 1, BASE)
    w1 = (wx1, 1, BASE), (wy1, 0, BASE), (wz1, 0, BASE)
    aINV1, aG1, aV1 = (inv1, 0, BASE), (g1, 0, BASE), (v1, 1, BASE)

    low, block1 = HALO // 2, block // 2
    aU1 = (u1, 1, BASE)
    window = (0, planes // 2, 0, planes // 4 // 8 * 8 + 16)
    e1 = doubled[1 : 1 + planes // 4, 2 : 2 + window[3], :]
    write(aU1, 0, 0, read(aV1, *window) + double_planes(e1))
    window = (low - 4, block1 + 8, low - 4, block1 + 8)
    here, around = spread(aU1, w1, window, 2)
    swept = KEEP * here + read(aINV1, *window) * (read(aG1, *window) + around)
    double_rows(e0, low - 4, swept)

    rows = block + 16
    aU0 = (u0, 1, BASE - (HALO - 7))
    aE0 = (e0, 0, -(2 * low - 8))
    aV0M = (v0m, 1, BASE - (HALO - 6))
    aV0N = (v0n, 1, BASE - (HALO - 5))
    size = (block + 16) // 4

    def correct(i):
        window = (i, size, HALO - 7, rows)
        e = double_planes(read(aE0, i // 2, size // 2, HALO - 7, rows))
        write(aU0, i, HALO - 7, read(aV0, *window) + e)

    slabs(HALO - 8, planes - HALO + 8, size, correct)

    def sweep(source, target, margin, size):
        def body(i):
            window = (i, size, HALO - margin, rows)
            here, around = spread(source, w0, window, 1)
            value = KEEP * here + read(aINV0, *window) * (read(aG0, *window) + around)
            write(target, i, HALO - margin, value)

        slabs(HALO - margin, planes - HALO + margin, size, body)

    sweep(aU0, aV0M, 6, (block + 12) // 2)
    sweep(aV0M, aV0N, 5, (block + 10) // 2)

    aG1N, aV1N = (g1n, 0, BASE - (low - 2)), (v1n, 1, BASE - (low - 2))
    size = (block + 8) // 2

    def resid(i):
        window = (i, size, HALO - 4, block + 8)
        here, around = spread(aV0N, w0, window, 1)
        r = (read(aG0, *window) - read(aTOT0, *window) * here) + around
        write(aG1N, i // 2, low - 2, sum_blocks(r, buf0, 1) * 0.125)

    slabs(HALO - 4, planes - HALO + 4, size, resid)

    window = (low - 2, block1 + 4, low - 2, block1 + 4)
    write(aV1N, low - 2, low - 2, read(aINV1, *window) * read(aG1N, *window))
    window = (low, block1, low, block1)
    _, around = spread(aV1N, w1, window, 2)
    send_to_all(packed, pack_block([sum_blocks(KEEP * read(aG1N, *window) + around, buf0, 2) * 0.125], bufp))


def third_kernel(
    got, g0, wx0, wy0, wz0, inv0, v0n, wx1, wy1, wz1, inv1, v1n, g1n,
    wx2, wy2, wz2, inv2, wx3, wy3, wz3, inv3,
    out,
    g2, buf2, wide, doubled, u1, e0, u0,
):
    count, rows2, width = g2.shape
    gy_count = lax.axis_size("gy")
    block2 = rows2 // gy_count

    def unpack(i, carry):
        for y in range(gy_count):
            g2[i, y * block2 : (y + 1) * block2, :] = got[i * gy_count + y]
        return carry

    lax.fori_loop(0, count, unpack, 0)
    level2 = (wx2[...], wy2[...], wz2[...], inv2[...])
    level3 = (wx3[...], wy3[...], wz3[...], inv3[...])
    spread_out(coarse_cycle(g2[...], level2, level3, buf2), wide, doubled, range(3, 9))

    top = BASE // 2
    planes = g0.shape[0]
    block = planes - 2 * HALO
    aG0, aINV0 = (g0, 0, top), (inv0, 0, BASE)
    w0 = (wx0, 1, BASE), (wy0, 0, BASE), (wz0, 0, BASE)
    w1 = (wx1, 1, BASE), (wy1, 0, BASE), (wz1, 0, BASE)
    low, block1 = HALO // 2, block // 2
    aINV1 = (inv1, 0, BASE)
    aG1N, aV1N = (g1n, 0, BASE - (low - 2)), (v1n, 1, BASE - (low - 2))
    aV0N = (v0n, 1, BASE - (HALO - 5))

    aU1 = (u1, 1, BASE - (low - 2))
    window = (low - 2, block1 + 4, low - 2, block1 + 4)
    e1 = doubled[low // 2 : low // 2 + block1 // 2 + 2, low : low + block1 + 4, :]
    write(aU1, low - 2, low - 2, read(aV1N, *window) + double_planes(e1))
    window = (low - 1, block1 + 2, low - 1, block1 + 2)
    here, around = spread(aU1, w1, window, 2)
    swept = KEEP * here + read(aINV1, *window) * (read(aG1N, *window) + around)
    double_rows(e0, low - 1, swept)

    aU0 = (u0, 1, BASE - (HALO - 1))
    aE0 = (e0, 0, -(2 * low - 2))
    size = (block + 4) // 2
    rows = block + 2

    def correct(i):
        window = (i, size, HALO - 1, rows)
        e = double_planes(read(aE0, i // 2, size // 2, HALO - 1, rows))
        write(aU0, i, HALO - 1, read(aV0N, *window) + e)

    slabs(HALO - 2, planes - HALO + 2, size, correct)

    def sweep(i):
        window = (i, size, HALO, block)
        here, around = spread(aU0, w0, window, 1)
        out[pl.ds(i - HALO, size)] = KEEP * here + read(aINV0, *window) * (read(aG0, *window) + around)

    size = block // 2
    slabs(HALO, planes - HALO, size, sweep)


def kernel_call(body, outs, scratch, args):
    def size(shape):
        total = 4
        for length in shape:
            total *= length
        return total

    shapes = [a.shape for a in args] + list(outs) + list(scratch)
    limit = sum(size(s) for s in shapes) + (8 << 20)
    return pl.pallas_call(
        body,
        out_shape=[jax.ShapeDtypeStruct(s, F32) for s in outs],
        in_specs=[pl.BlockSpec(memory_space=pltpu.VMEM)] * len(args),
        out_specs=[pl.BlockSpec(memory_space=pltpu.VMEM)] * len(outs),
        scratch_shapes=[pltpu.VMEM(s, F32) for s in scratch],
        compiler_params=pltpu.CompilerParams(vmem_limit_bytes=limit),
    )(*args)


def local(right_side, material, conductivity):
    bx, by, bz = right_side.shape
    gx_count, gy_count = lax.axis_size("gx"), lax.axis_size("gy")
    devices = gx_count * gy_count

    X, Y = bx + 2 * HALO, by + 2 * HALO
    YA = Y + BASE
    YB = Y + 2 * BASE
    X1, Y1 = X // 2, -(-Y // 16) * 8 + 2 * BASE
    xb, yb = bx // 4, by // 4

    strip = (bx + bx // 2, NEAR, bz)
    h, k_near, k_far, g_near, g_far = kernel_call(
        start_kernel,
        [(bx, by, bz), (HALO, by, bz), (HALO, by, bz), strip, strip],
        [(8, bz)],
        [right_side, material, conductivity[None]],
    )
    k_near, k_far = trade(k_near, k_far, "gx")
    g_near, g_far = trade(g_near, g_far, "gy")
    first, last = far_planes(X)
    strip = (X + (last - first) // 2, NEAR, bz)
    k_wide, k_near, k_far = kernel_call(
        k_kernel, [(X, by, bz), strip, strip], [], [h, k_near, k_far]
    )
    k_near, k_far = trade(k_near, k_far, "gy")
    strip = (plane_strips(Y)[1], 8, bz)
    g_wide, g_near, g_far = kernel_call(
        g_kernel, [(bx, YA, bz), strip, strip], [], [right_side, g_near, g_far]
    )
    g_near, g_far = trade(g_near, g_far, "gx")

    pad0, full0, pad1, full1 = (X + 2, YB, bz), (X, YB, bz), (X1 + 2, Y1, bz), (X1, Y1, bz)
    packed, g0, wx0, wy0, wz0, inv0, tot0, v0, wx1, wy1, wz1, inv1, v1, g1 = kernel_call(
        first_kernel,
        [(devices, 2 * yb, bz), (X, YA, bz), pad0, full0, full0, full0, full0, pad0]
        + [pad1, full1, full1, full1, pad1, full1],
        [(X + 2, YA, bz), pad1, (X // 4, Y, bz), (xb, 8, bz)],
        [k_wide, k_near, k_far, g_wide, g_near, g_far],
    )
    got = everywhere(packed)
    level2 = (gx_count, gy_count * yb, bz)
    level3 = (gx_count, gy_count * yb // 2, bz)
    coarse_scratch = [
        level2, (gx_count + 2, gy_count * yb + 16, bz), (3 * xb, 32, bz), pad1, (X1, by + 24, bz), pad0,
    ]
    packed, v0n, v1n, g1n, *levels = kernel_call(
        second_kernel,
        [(devices, yb, bz), pad0, pad1, full1] + [level2] * 4 + [level3] * 4,
        [level2, level2] + coarse_scratch + [pad0, (X // 4, Y, bz), (xb, 8, bz)],
        [got, g0, wx0, wy0, wz0, inv0, tot0, v0, wx1, wy1, wz1, inv1, v1, g1],
    )
    got = everywhere(packed)
    (out,) = kernel_call(
        third_kernel,
        [(bx, by, bz)],
        [level2] + coarse_scratch,
        [got, g0, wx0, wy0, wz0, inv0, v0n, wx1, wy1, wz1, inv1, v1n, g1n] + levels,
    )
    return out


def solution(mesh):
    return jax.shard_map(
        local,
        mesh=mesh,
        in_specs=(P("gx", "gy", None), P("gx", "gy", None), P()),
        out_specs=P("gx", "gy", None),
        check_vma=False,
    )
```

```python
import jax
import jax.numpy as jnp
from jax import lax
from jax.experimental import pallas as pl
from jax.experimental.pallas import tpu as pltpu
from jax.sharding import PartitionSpec as P

COARSE_SWEEPS = 6
OMEGA = 0.8
KEEP = 1.0 - OMEGA
HALO = 12
NEAR = 8
FAR = HALO - NEAR
BASE = 8
F32 = jnp.float32
START_LIMIT = int(53.25 * 2**20)


def near_partner(index, count):
    return index ^ 1 if index ^ 1 < count else index


def far_partner(index, count):
    return (index - 1 ^ 1) + 1


def route(axis, far):
    gx_count, gy_count = lax.axis_size("gx"), lax.axis_size("gy")
    pairs = []
    for x in range(gx_count):
        for y in range(gy_count):
            if axis == "gx":
                if not far:
                    a, b = near_partner(x, gx_count), y
                elif 0 < x < gx_count - 1:
                    a, b = far_partner(x, gx_count), y
                else:
                    a, b = x, near_partner(y, gy_count)
            else:
                if not far:
                    a, b = x, near_partner(y, gy_count)
                elif 0 < y < gy_count - 1:
                    a, b = x, far_partner(y, gy_count)
                else:
                    a, b = near_partner(x, gx_count), y
            pairs.append((x * gy_count + y, a * gy_count + b))
    return pairs


def trade(to_near, to_far, axis):
    from_far = lax.ppermute(to_far, ("gx", "gy"), route(axis, True))
    from_near = lax.ppermute(to_near, ("gx", "gy"), route(axis, False))
    return from_near, from_far


def everywhere(copies):
    return lax.all_to_all(copies, ("gx", "gy"), 0, 0)


def is_odd(axis):
    return lax.axis_index(axis) % 2 == 1


def has_below(axis):
    return lax.axis_index(axis) > 0


def has_above(axis):
    return lax.axis_index(axis) < lax.axis_size(axis) - 1


def below(near, far, axis):
    return jnp.where(has_below(axis), jnp.where(is_odd(axis), near, far), 0.0)


def above(near, far, axis):
    return jnp.where(has_above(axis), jnp.where(is_odd(axis), far, near), 0.0)


def roll(value, shift, axis):
    return pltpu.roll(value, shift % value.shape[axis], axis=axis)


def lanes_of(value):
    return lax.broadcasted_iota(jnp.int32, value.shape, value.ndim - 1)


def rows_of(value):
    return lax.broadcasted_iota(jnp.int32, value.shape, value.ndim - 2)


def lane_row(width):
    return lax.broadcasted_iota(jnp.int32, (1, width), 1)


def pick_lanes(value, index):
    flat = value.reshape(-1, value.shape[-1])
    index = jnp.broadcast_to(index, flat.shape)
    return jnp.take_along_axis(flat, index, axis=1).reshape(value.shape)


def add_partner(value, apart):
    return value + pick_lanes(value, lane_row(value.shape[-1]) ^ apart)


def shift_up(value):
    return jnp.concatenate([value[1:], jnp.zeros_like(value[:1])], axis=0)


def shift_down(value):
    return jnp.concatenate([jnp.zeros_like(value[:1]), value[:-1]], axis=0)


def next_x(value, step):
    turned = roll(value, -step, 2)
    return jnp.where(lanes_of(value) < value.shape[-1] - step, turned, shift_up(turned))


def prev_x(value, step):
    turned = roll(value, step, 2)
    return jnp.where(lanes_of(value) >= step, turned, shift_down(turned))


def whole_faces(h, span, xstep, zstep):
    in_span = lanes_of(h) % span
    row = rows_of(h)
    not_last_z, not_first_z = in_span < span - zstep, in_span >= zstep
    not_last_y, not_first_y = row < h.shape[1] - 1, row >= 1
    wx = h + next_x(h, xstep)
    wy = h + jnp.where(not_last_y, roll(h, -1, 1), 0.0)
    wz = h + jnp.where(not_last_z, roll(h, -zstep, 2), 0.0)
    back = h + prev_x(h, xstep)
    back = back + (h + jnp.where(not_first_y, roll(h, 1, 1), 0.0))
    back = back + (h + jnp.where(not_first_z, roll(h, zstep, 2), 0.0))
    total = wx + wy + wz + back
    return wx, jnp.where(not_last_y, wy, 0.0), jnp.where(not_last_z, wz, 0.0), OMEGA / total


def whole_spread(v, wx, wy, wz, xstep, zstep):
    return (
        (wx * next_x(v, xstep) + prev_x(wx * v, xstep))
        + (wy * roll(v, -1, 1) + roll(wy * v, 1, 1))
        + (wz * roll(v, -zstep, 2) + roll(wz * v, zstep, 2))
    )


def read(array, start, size, top, rows, dx=0, dy=0):
    ref, planes_off, rows_off = array
    return ref[pl.ds(start + planes_off + dx, size), pl.ds(top + rows_off + dy, rows), :]


def write(array, start, top, value):
    ref, planes_off, rows_off = array
    ref[pl.ds(start + planes_off, value.shape[0]), pl.ds(top + rows_off, value.shape[1]), :] = value


def slabs(first, last, size, body):
    if first + size == last:
        body(first)
        return

    def step(i, carry):
        body(first + i * size)
        return carry

    lax.fori_loop(0, (last - first) // size, step, 0)


def faces(h, window, step):
    here = read(h, *window)
    lane = lanes_of(here)
    width = here.shape[-1]
    not_last = lane < width - step
    wx = here + read(h, *window, dx=1)
    wy = here + read(h, *window, dy=1)
    wz = here + jnp.where(not_last, roll(here, -step, 2), 0.0)
    back = (here + read(h, *window, dx=-1)) + (here + read(h, *window, dy=-1))
    back = back + (here + jnp.where(lane >= step, roll(here, step, 2), 0.0))
    total = (wx + wy + wz) + back
    inverse = jnp.where(here > 0.0, OMEGA / total, 0.0)
    return here, wx, wy, jnp.where(not_last, wz, 0.0), total, inverse


def spread(v, weights, window, step):
    wx, wy, wz = weights
    here = read(v, *window)
    wz = read(wz, *window)
    return here, (
        (read(wx, *window) * read(v, *window, dx=1) + read(wx, *window, dx=-1) * read(v, *window, dx=-1))
        + (read(wy, *window) * read(v, *window, dy=1) + read(wy, *window, dy=-1) * read(v, *window, dy=-1))
        + (wz * roll(here, -step, 2) + roll(wz * here, step, 2))
    )


def halve_rows(value, buffer):
    count, rows, _ = value.shape
    buffer[0:count, 0:rows, :] = value
    return (
        buffer[0:count, pl.ds(0, rows // 2, stride=2), :] + buffer[0:count, pl.ds(1, rows // 2, stride=2), :]
    )


def halve_planes(value):
    pairs = value.reshape((value.shape[0] // 2, 2) + value.shape[1:])
    return pairs[:, 0] + pairs[:, 1]


def sum_blocks(value, buffer, step):
    return add_partner(halve_rows(halve_planes(value), buffer), step)


def double_rows(ref, start, value):
    count, rows, _ = value.shape
    ref[pl.ds(start, count), pl.ds(0, rows, stride=2), :] = value
    ref[pl.ds(start, count), pl.ds(1, rows, stride=2), :] = value


def double_planes(value):
    wide = jnp.broadcast_to(value[:, None], (value.shape[0], 2) + value.shape[1:])
    return wide.reshape((2 * value.shape[0],) + value.shape[1:])


def pack_block(values, buffer):
    blocks, rows, width = values[0].shape
    span = width // blocks
    for n, value in enumerate(values):
        buffer[:, n * rows : (n + 1) * rows, :] = value
    used = rows * len(values)
    lane = lane_row(width)
    packed = None
    for x in range(blocks):
        picked = pick_lanes(buffer[x], (lane % span) * blocks)[:used]
        packed = picked if packed is None else jnp.where(lanes_of(picked) // span == x, picked, packed)
    return packed


def send_to_all(packed, chunk):
    copies = min(packed.shape[0], 32)

    def copy_out(i):
        packed[pl.ds(i, copies)] = jnp.broadcast_to(chunk[None], (copies,) + chunk.shape)

    slabs(0, packed.shape[0], copies, copy_out)


def coarse_cycle(g2, level2, level3, buffer):
    wx2, wy2, wz2, inv2 = level2
    wx3, wy3, wz3, inv3 = level3
    width = g2.shape[-1]
    span = width // 4
    v2 = inv2 * g2
    r2 = KEEP * g2 + whole_spread(v2, wx2, wy2, wz2, span, 1)
    g3 = 0.125 * halve_rows(add_partner(add_partner(r2, 1), span), buffer)
    v3 = inv3 * g3
    for _ in range(COARSE_SWEEPS - 1):
        v3 = KEEP * v3 + inv3 * (g3 + whole_spread(v3, wx3, wy3, wz3, 2 * span, 2))
    double_rows(buffer, 0, v3)
    u2 = v2 + buffer[...]
    return KEEP * u2 + inv2 * (g2 + whole_spread(u2, wx2, wy2, wz2, span, 1))


def spread_out(e2, wide, doubled, planes):
    count, rows, width = e2.shape
    block = rows // lax.axis_size("gy")
    span = width // 4
    wide[0:1] = jnp.zeros((1,) + wide.shape[1:], F32)
    wide[count + 1 : count + 2] = jnp.zeros((1,) + wide.shape[1:], F32)
    wide[1 : count + 1, 0:8, :] = jnp.zeros((count, 8, width), F32)
    wide[1 : count + 1, rows + 8 : rows + 16, :] = jnp.zeros((count, 8, width), F32)
    wide[1 : count + 1, 8 : 8 + rows, :] = e2
    gx, gy = lax.axis_index("gx"), lax.axis_index("gy")
    around = wide[pl.ds(gx, 3), pl.ds(gy * block + 8 - block, 16), :]
    lane = lane_row(width)
    kept = 3 * block
    for j in planes:
        value = pick_lanes(around[j // 4], (j % 4) * span + lane // 4)[:kept]
        doubled[j, pl.ds(0, kept, stride=2), :] = value
        doubled[j, pl.ds(1, kept, stride=2), :] = value


def row_starts(axis, block):
    odd = is_odd(axis)
    low = (0, NEAR)
    high = (block - NEAR, block - HALO)
    to_near = [jnp.where(odd, a, b) for a, b in zip(low, high)]
    to_far = [jnp.where(odd, b, a) for a, b in zip(low, high)]
    return to_near, to_far


def pack_rows(source, starts, first, last, target):
    count = source.shape[0]
    half = (last - first) // 2
    target[0:count] = source[:, pl.ds(starts[0], NEAR), :]
    target[count : count + half, 0:FAR, :] = source[first : first + half, pl.ds(starts[1], FAR), :]
    target[count : count + half, FAR:NEAR, :] = source[first + half : last, pl.ds(starts[1], FAR), :]


def unpack_rows(target, planes_off, top, bottom, count, first, last, near, far):
    half = (last - first) // 2
    for choose, at, edge in ((below, top - NEAR, top - HALO), (above, bottom, bottom + NEAR)):
        target[planes_off : planes_off + count, at : at + NEAR, :] = choose(near[0:count], far[0:count], "gy")
        strips = choose(near[count : count + half], far[count : count + half], "gy")
        target[planes_off + first : planes_off + first + half, edge : edge + FAR, :] = strips[:, 0:FAR]
        target[planes_off + first + half : planes_off + last, edge : edge + FAR, :] = strips[:, FAR:NEAR]


def start_kernel(
    right_hbm, material_hbm, cond, h, right, k_near, k_far, g_near, g_far, material, table, arrived,
):
    planes, rows, width = h.shape
    copies = [
        pltpu.make_async_copy(right_hbm, right, arrived.at[0]),
        pltpu.make_async_copy(material_hbm, material, arrived.at[1]),
    ]
    for copy in copies:
        copy.start()
    table[0:1, 0 : cond.shape[1]] = cond[...]
    copies[0].wait()
    to_near, to_far = row_starts("gy", rows)
    pack_rows(right, to_near, 0, planes, g_near)
    pack_rows(right, to_far, 0, planes, g_far)
    copies[1].wait()
    which = material[...].reshape(planes * rows, width)
    values = jnp.broadcast_to(0.5 * table[0:1, :], which.shape)
    h[...] = jnp.take_along_axis(values, which, axis=1).reshape(planes, rows, width)
    odd = is_odd("gx")
    k_near[...] = h[pl.ds(jnp.where(odd, 0, planes - HALO), HALO)]
    k_far[...] = h[pl.ds(jnp.where(odd, planes - HALO, 0), HALO)]


def far_planes(planes):
    return HALO - FAR + 1, planes - HALO + FAR - 1


def k_kernel(h, near, far, wide, k_near, k_far):
    block = h.shape[0]
    wide[0:HALO] = below(near[...], far[...], "gx")
    wide[HALO : HALO + block] = h[...]
    wide[HALO + block :] = above(near[...], far[...], "gx")
    first, last = far_planes(wide.shape[0])
    to_near, to_far = row_starts("gy", h.shape[1])
    pack_rows(wide, to_near, first, last, k_near)
    pack_rows(wide, to_far, first, last, k_far)


def plane_strips(rows):
    strips, at = [], 0
    for distance in range(1, HALO):
        cut = (distance // 4) * 4
        tiles = (rows - 2 * cut) // 8
        strips.append((distance, cut, tiles, at))
        at += tiles
    return strips, at


def g_kernel(right, near, far, wide, g_near, g_far):
    block, rows, _ = right.shape
    top = BASE // 2
    wide[:, top + HALO : top + HALO + rows, :] = right[...]
    unpack_rows(wide, 0, top + HALO, top + HALO + rows, block, 0, block, near, far)
    odd = is_odd("gx")
    strips, _ = plane_strips(rows + 2 * HALO)
    for distance, cut, tiles, at in strips:
        low, high = distance - 1, block - distance
        for target, plane in ((g_near, jnp.where(odd, low, high)), (g_far, jnp.where(odd, high, low))):
            for tile in range(tiles):
                target[at + tile] = wide[plane, top + cut + 8 * tile : top + cut + 8 * tile + 8, :]


def first_kernel(
    k_wide, k_near, k_far, g_wide, g_near, g_far,
    packed, g0, wx0, wy0, wz0, inv0, tot0, v0, wx1, wy1, wz1, inv1, v1, g1,
    h0, h1, buf0, bufp,
):
    top = BASE // 2
    planes, rows, width = k_wide.shape
    own = slice(HALO, planes - HALO)
    h0[1 : planes + 1, top + HALO : top + HALO + rows, :] = k_wide[...]
    first, last = far_planes(planes)
    unpack_rows(h0, 1, top + HALO, top + HALO + rows, planes, first, last, k_near, k_far)
    g0[own] = g_wide[...]
    rows = rows + 2 * HALO
    strips, _ = plane_strips(rows)
    for distance, cut, tiles, at in strips:
        for choose, plane in ((below, HALO - distance), (above, planes - HALO - 1 + distance)):
            value = choose(g_near[at : at + tiles], g_far[at : at + tiles], "gx")
            g0[plane, top + cut : top + cut + 8 * tiles, :] = value.reshape(8 * tiles, width)

    aH0, aG0 = (h0, 1, top), (g0, 0, top)
    aWX0, aV0 = (wx0, 1, BASE), (v0, 1, BASE)
    aWY0, aWZ0, aINV0, aTOT0 = ((ref, 0, BASE) for ref in (wy0, wz0, inv0, tot0))
    aH1, aWX1, aV1 = (h1, 1, BASE), (wx1, 1, BASE), (v1, 1, BASE)
    aWY1, aWZ1, aINV1, aG1 = ((ref, 0, BASE) for ref in (wy1, wz1, inv1, g1))
    size = planes

    def faces0(i):
        window = (i, size, 0, rows)
        here, wx, wy, wz, total, inverse = faces(aH0, window, 1)
        write(aWX0, i, 0, wx)
        write(aWY0, i, 0, wy)
        write(aWZ0, i, 0, wz)
        write(aTOT0, i, 0, total)
        write(aINV0, i, 0, inverse)
        write(aV0, i, 0, inverse * read(aG0, *window))

    slabs(0, planes, size, faces0)
    write(aH1, 0, 0, sum_blocks(read(aH0, 0, planes, 0, rows), buf0, 1) * (1.0 / 32.0))

    def resid0(i):
        window = (i, size, 0, rows)
        _, around = spread(aV0, (aWX0, aWY0, aWZ0), window, 1)
        buf0[pl.ds(i // 2, size // 2)] = halve_planes(KEEP * read(aG0, *window) + around)

    slabs(0, planes, size, resid0)
    r = buf0[:, pl.ds(0, rows // 2, stride=2), :] + buf0[:, pl.ds(1, rows // 2, stride=2), :]
    write(aG1, 0, 0, add_partner(r, 1) * 0.125)

    planes1, rows1 = planes // 2, -(-rows // 16) * 8

    def faces1(i):
        window = (i, planes1, 0, rows1)
        _, wx, wy, wz, total, inverse = faces(aH1, window, 2)
        write(aWX1, i, 0, wx)
        write(aWY1, i, 0, wy)
        write(aWZ1, i, 0, wz)
        write(aINV1, i, 0, inverse)
        write(aV1, i, 0, inverse * read(aG1, *window))

    slabs(0, planes1, planes1, faces1)

    low = HALO // 2
    window = (low, planes1 - HALO, low, rows // 2 - HALO)
    _, around = spread(aV1, (aWX1, aWY1, aWZ1), window, 2)
    g2 = sum_blocks(KEEP * read(aG1, *window) + around, buf0, 2) * 0.125
    h2 = sum_blocks(read(aH1, *window), buf0, 2) * (1.0 / 32.0)
    send_to_all(packed, pack_block([g2, h2], bufp))


def second_kernel(
    got, g0, wx0, wy0, wz0, inv0, tot0, v0, wx1, wy1, wz1, inv1, v1, g1,
    packed, v0n, v1n, g1n, wx2, wy2, wz2, inv2, wx3, wy3, wz3, inv3,
    g2, h2, buf2, wide, doubled, u1, e0, u0, v0m, buf0, bufp,
):
    count, rows2, width = g2.shape
    gy_count = lax.axis_size("gy")
    block2 = rows2 // gy_count

    def unpack(i, carry):
        for y in range(gy_count):
            both = got[i * gy_count + y]
            g2[i, y * block2 : (y + 1) * block2, :] = both[:block2]
            h2[i, y * block2 : (y + 1) * block2, :] = both[block2:]
        return carry

    lax.fori_loop(0, count, unpack, 0)

    span = width // 4
    h = h2[...]
    level2 = whole_faces(h, span, span, 1)
    h3 = halve_rows(add_partner(add_partner(h, 1), span), buf2) * (1.0 / 32.0)
    level3 = whole_faces(h3, span, 2 * span, 2)
    for ref, value in zip((wx2, wy2, wz2, inv2, wx3, wy3, wz3, inv3), level2 + level3):
        ref[...] = value
    spread_out(coarse_cycle(g2[...], level2, level3, buf2), wide, doubled, range(1, 11))

    top = BASE // 2
    planes = g0.shape[0]
    block = planes - 2 * HALO
    aG0 = (g0, 0, top)
    w0 = (wx0, 1, BASE), (wy0, 0, BASE), (wz0, 0, BASE)
    aINV0, aTOT0, aV0 = (inv0, 0, BASE), (tot0, 0, BASE), (v0, 1, BASE)
    w1 = (wx1, 1, BASE), (wy1, 0, BASE), (wz1, 0, BASE)
    aINV1, aG1, aV1 = (inv1, 0, BASE), (g1, 0, BASE), (v1, 1, BASE)

    low, block1 = HALO // 2, block // 2
    aU1 = (u1, 1, BASE)
    window = (0, planes // 2, 0, planes // 4 // 8 * 8 + 16)
    e1 = doubled[1 : 1 + planes // 4, 2 : 2 + window[3], :]
    write(aU1, 0, 0, read(aV1, *window) + double_planes(e1))
    window = (low - 4, block1 + 8, low - 4, block1 + 8)
    here, around = spread(aU1, w1, window, 2)
    swept = KEEP * here + read(aINV1, *window) * (read(aG1, *window) + around)
    double_rows(e0, low - 4, swept)

    rows = block + 16
    aU0 = (u0, 1, BASE - (HALO - 7))
    aE0 = (e0, 0, -(2 * low - 8))
    aV0M = (v0m, 1, BASE - (HALO - 6))
    aV0N = (v0n, 1, BASE - (HALO - 5))
    size = block + 16

    def correct(i):
        window = (i, size, HALO - 7, rows)
        e = double_planes(read(aE0, i // 2, size // 2, HALO - 7, rows))
        write(aU0, i, HALO - 7, read(aV0, *window) + e)

    slabs(HALO - 8, planes - HALO + 8, size, correct)

    def sweep(source, target, margin, size):
        def body(i):
            window = (i, size, HALO - margin, rows)
            here, around = spread(source, w0, window, 1)
            value = KEEP * here + read(aINV0, *window) * (read(aG0, *window) + around)
            write(target, i, HALO - margin, value)

        slabs(HALO - margin, planes - HALO + margin, size, body)

    sweep(aU0, aV0M, 6, block + 12)
    sweep(aV0M, aV0N, 5, block + 10)

    aG1N, aV1N = (g1n, 0, BASE - (low - 2)), (v1n, 1, BASE - (low - 2))
    window = (HALO - 4, block + 8, HALO - 4, block + 8)
    here, around = spread(aV0N, w0, window, 1)
    r = (read(aG0, *window) - read(aTOT0, *window) * here) + around
    write(aG1N, low - 2, low - 2, sum_blocks(r, buf0, 1) * 0.125)

    window = (low - 2, block1 + 4, low - 2, block1 + 4)
    write(aV1N, low - 2, low - 2, read(aINV1, *window) * read(aG1N, *window))
    window = (low, block1, low, block1)
    _, around = spread(aV1N, w1, window, 2)
    send_to_all(packed, pack_block([sum_blocks(KEEP * read(aG1N, *window) + around, buf0, 2) * 0.125], bufp))


def third_kernel(
    got, g0, wx0, wy0, wz0, inv0, v0n, wx1, wy1, wz1, inv1, v1n, g1n,
    wx2, wy2, wz2, inv2, wx3, wy3, wz3, inv3,
    out,
    g2, buf2, wide, doubled, u1, e0, u0,
):
    count, rows2, width = g2.shape
    gy_count = lax.axis_size("gy")
    block2 = rows2 // gy_count

    def unpack(i, carry):
        for y in range(gy_count):
            g2[i, y * block2 : (y + 1) * block2, :] = got[i * gy_count + y]
        return carry

    lax.fori_loop(0, count, unpack, 0)
    level2 = (wx2[...], wy2[...], wz2[...], inv2[...])
    level3 = (wx3[...], wy3[...], wz3[...], inv3[...])
    spread_out(coarse_cycle(g2[...], level2, level3, buf2), wide, doubled, range(3, 9))

    top = BASE // 2
    planes = g0.shape[0]
    block = planes - 2 * HALO
    aG0, aINV0 = (g0, 0, top), (inv0, 0, BASE)
    w0 = (wx0, 1, BASE), (wy0, 0, BASE), (wz0, 0, BASE)
    w1 = (wx1, 1, BASE), (wy1, 0, BASE), (wz1, 0, BASE)
    low, block1 = HALO // 2, block // 2
    aINV1 = (inv1, 0, BASE)
    aG1N, aV1N = (g1n, 0, BASE - (low - 2)), (v1n, 1, BASE - (low - 2))
    aV0N = (v0n, 1, BASE - (HALO - 5))

    aU1 = (u1, 1, BASE - (low - 2))
    window = (low - 2, block1 + 4, low - 2, block1 + 4)
    e1 = doubled[low // 2 : low // 2 + block1 // 2 + 2, low : low + block1 + 4, :]
    write(aU1, low - 2, low - 2, read(aV1N, *window) + double_planes(e1))
    window = (low - 1, block1 + 2, low - 1, block1 + 2)
    here, around = spread(aU1, w1, window, 2)
    swept = KEEP * here + read(aINV1, *window) * (read(aG1N, *window) + around)
    double_rows(e0, low - 1, swept)

    aU0 = (u0, 1, BASE - (HALO - 1))
    aE0 = (e0, 0, -(2 * low - 2))
    size = block + 4
    rows = block + 2

    def correct(i):
        window = (i, size, HALO - 1, rows)
        e = double_planes(read(aE0, i // 2, size // 2, HALO - 1, rows))
        write(aU0, i, HALO - 1, read(aV0N, *window) + e)

    slabs(HALO - 2, planes - HALO + 2, size, correct)

    def sweep(i):
        window = (i, size, HALO, block)
        here, around = spread(aU0, w0, window, 1)
        out[pl.ds(i - HALO, size)] = KEEP * here + read(aINV0, *window) * (read(aG0, *window) + around)

    size = block
    slabs(HALO, planes - HALO, size, sweep)


def kernel_call(body, outs, scratch, args):
    def size(shape):
        total = 4
        for length in shape:
            total *= length
        return total

    shapes = [a.shape for a in args] + list(outs) + list(scratch)
    limit = sum(size(s) for s in shapes) + (8 << 20)
    return pl.pallas_call(
        body,
        out_shape=[jax.ShapeDtypeStruct(s, F32) for s in outs],
        in_specs=[pl.BlockSpec(memory_space=pltpu.VMEM)] * len(args),
        out_specs=[pl.BlockSpec(memory_space=pltpu.VMEM)] * len(outs),
        scratch_shapes=[pltpu.VMEM(s, F32) for s in scratch],
        compiler_params=pltpu.CompilerParams(vmem_limit_bytes=limit),
    )(*args)


def local(right_side, material, conductivity):
    bx, by, bz = right_side.shape
    gx_count, gy_count = lax.axis_size("gx"), lax.axis_size("gy")
    devices = gx_count * gy_count

    X, Y = bx + 2 * HALO, by + 2 * HALO
    YA = Y + BASE
    YB = Y + 2 * BASE
    X1, Y1 = X // 2, -(-Y // 16) * 8 + 2 * BASE
    xb, yb = bx // 4, by // 4

    strip = (bx + bx // 2, NEAR, bz)
    outs = [(bx, by, bz), (bx, by, bz), (HALO, by, bz), (HALO, by, bz), strip, strip]
    h, right, k_near, k_far, g_near, g_far = pl.pallas_call(
        start_kernel,
        out_shape=[jax.ShapeDtypeStruct(s, F32) for s in outs],
        in_specs=[pl.BlockSpec(memory_space=pl.ANY)] * 2 + [pl.BlockSpec(memory_space=pltpu.VMEM)],
        out_specs=[pl.BlockSpec(memory_space=pltpu.VMEM)] * len(outs),
        scratch_shapes=[
            pltpu.VMEM((bx, by, bz), jnp.int32),
            pltpu.VMEM((8, bz), F32),
            pltpu.SemaphoreType.DMA((2,)),
        ],
        compiler_params=pltpu.CompilerParams(vmem_limit_bytes=START_LIMIT),
    )(right_side, material, conductivity[None])
    k_near, k_far = trade(k_near, k_far, "gx")
    g_near, g_far = trade(g_near, g_far, "gy")
    strip = (plane_strips(Y)[1], 8, bz)
    g_wide, g_near, g_far = kernel_call(
        g_kernel, [(bx, YA, bz), strip, strip], [], [right, g_near, g_far]
    )
    first, last = far_planes(X)
    strip = (X + (last - first) // 2, NEAR, bz)
    k_wide, k_near, k_far = kernel_call(
        k_kernel, [(X, by, bz), strip, strip], [], [h, k_near, k_far]
    )
    g_near, g_far = trade(g_near, g_far, "gx")
    k_near, k_far = trade(k_near, k_far, "gy")

    pad0, full0, pad1, full1 = (X + 2, YB, bz), (X, YB, bz), (X1 + 2, Y1, bz), (X1, Y1, bz)
    packed, g0, wx0, wy0, wz0, inv0, tot0, v0, wx1, wy1, wz1, inv1, v1, g1 = kernel_call(
        first_kernel,
        [(devices, 2 * yb, bz), (X, YA, bz), pad0, full0, full0, full0, full0, pad0]
        + [pad1, full1, full1, full1, pad1, full1],
        [(X + 2, YA, bz), pad1, (X1, Y, bz), (xb, 8, bz)],
        [k_wide, k_near, k_far, g_wide, g_near, g_far],
    )
    got = everywhere(packed)
    level2 = (gx_count, gy_count * yb, bz)
    level3 = (gx_count, gy_count * yb // 2, bz)
    coarse_scratch = [
        level2, (gx_count + 2, gy_count * yb + 16, bz), (3 * xb, 32, bz), pad1, (X1, by + 24, bz), pad0,
    ]
    packed, v0n, v1n, g1n, *levels = kernel_call(
        second_kernel,
        [(devices, yb, bz), pad0, pad1, full1] + [level2] * 4 + [level3] * 4,
        [level2, level2] + coarse_scratch + [pad0, (X1, Y, bz), (xb, 8, bz)],
        [got, g0, wx0, wy0, wz0, inv0, tot0, v0, wx1, wy1, wz1, inv1, v1, g1],
    )
    got = everywhere(packed)
    (out,) = kernel_call(
        third_kernel,
        [(bx, by, bz)],
        [level2] + coarse_scratch,
        [got, g0, wx0, wy0, wz0, inv0, v0n, wx1, wy1, wz1, inv1, v1n, g1n] + levels,
    )
    return out


def solution(mesh):
    return jax.shard_map(
        local,
        mesh=mesh,
        in_specs=(P("gx", "gy", None), P("gx", "gy", None), P()),
        out_specs=P("gx", "gy", None),
        check_vma=False,
    )
```

```python
import jax
import jax.numpy as jnp
from jax import lax
from jax.experimental import pallas as pl
from jax.experimental.pallas import tpu as pltpu
from jax.sharding import PartitionSpec as P

COARSE_SWEEPS = 6
OMEGA = 0.8
KEEP = 1.0 - OMEGA
HALO = 12
NEAR = 8
FAR = HALO - NEAR
BASE = 8
F32 = jnp.float32
START_LIMIT = int(53.25 * 2**20)


def near_partner(index, count):
    return index ^ 1 if index ^ 1 < count else index


def far_partner(index, count):
    return (index - 1 ^ 1) + 1


def route(axis, far):
    gx_count, gy_count = lax.axis_size("gx"), lax.axis_size("gy")
    pairs = []
    for x in range(gx_count):
        for y in range(gy_count):
            if axis == "gx":
                if not far:
                    a, b = near_partner(x, gx_count), y
                elif 0 < x < gx_count - 1:
                    a, b = far_partner(x, gx_count), y
                else:
                    a, b = x, near_partner(y, gy_count)
            else:
                if not far:
                    a, b = x, near_partner(y, gy_count)
                elif 0 < y < gy_count - 1:
                    a, b = x, far_partner(y, gy_count)
                else:
                    a, b = near_partner(x, gx_count), y
            pairs.append((x * gy_count + y, a * gy_count + b))
    return pairs


def trade(to_near, to_far, axis):
    from_far = lax.ppermute(to_far, ("gx", "gy"), route(axis, True))
    from_near = lax.ppermute(to_near, ("gx", "gy"), route(axis, False))
    return from_near, from_far


def everywhere(copies):
    return lax.all_to_all(copies, ("gx", "gy"), 0, 0)


def is_odd(axis):
    return lax.axis_index(axis) % 2 == 1


def has_below(axis):
    return lax.axis_index(axis) > 0


def has_above(axis):
    return lax.axis_index(axis) < lax.axis_size(axis) - 1


def below(near, far, axis):
    return jnp.where(has_below(axis), jnp.where(is_odd(axis), near, far), 0.0)


def above(near, far, axis):
    return jnp.where(has_above(axis), jnp.where(is_odd(axis), far, near), 0.0)


def roll(value, shift, axis):
    return pltpu.roll(value, shift % value.shape[axis], axis=axis)


def lanes_of(value):
    return lax.broadcasted_iota(jnp.int32, value.shape, value.ndim - 1)


def rows_of(value):
    return lax.broadcasted_iota(jnp.int32, value.shape, value.ndim - 2)


def lane_row(width):
    return lax.broadcasted_iota(jnp.int32, (1, width), 1)


def pick_lanes(value, index):
    flat = value.reshape(-1, value.shape[-1])
    index = jnp.broadcast_to(index, flat.shape)
    return jnp.take_along_axis(flat, index, axis=1).reshape(value.shape)


def add_partner(value, apart):
    return value + pick_lanes(value, lane_row(value.shape[-1]) ^ apart)


def shift_up(value):
    return jnp.concatenate([value[1:], jnp.zeros_like(value[:1])], axis=0)


def shift_down(value):
    return jnp.concatenate([jnp.zeros_like(value[:1]), value[:-1]], axis=0)


def next_x(value, step):
    turned = roll(value, -step, 2)
    return jnp.where(lanes_of(value) < value.shape[-1] - step, turned, shift_up(turned))


def prev_x(value, step):
    turned = roll(value, step, 2)
    return jnp.where(lanes_of(value) >= step, turned, shift_down(turned))


def whole_faces(h, span, xstep, zstep):
    in_span = lanes_of(h) % span
    row = rows_of(h)
    not_last_z, not_first_z = in_span < span - zstep, in_span >= zstep
    not_last_y, not_first_y = row < h.shape[1] - 1, row >= 1
    wx = h + next_x(h, xstep)
    wy = h + jnp.where(not_last_y, roll(h, -1, 1), 0.0)
    wz = h + jnp.where(not_last_z, roll(h, -zstep, 2), 0.0)
    back = h + prev_x(h, xstep)
    back = back + (h + jnp.where(not_first_y, roll(h, 1, 1), 0.0))
    back = back + (h + jnp.where(not_first_z, roll(h, zstep, 2), 0.0))
    total = wx + wy + wz + back
    return wx, jnp.where(not_last_y, wy, 0.0), jnp.where(not_last_z, wz, 0.0), OMEGA / total


def whole_spread(v, wx, wy, wz, xstep, zstep):
    return (
        (wx * next_x(v, xstep) + prev_x(wx * v, xstep))
        + (wy * roll(v, -1, 1) + roll(wy * v, 1, 1))
        + (wz * roll(v, -zstep, 2) + roll(wz * v, zstep, 2))
    )


def coarse_faces(h, span, xstep, zstep):
    wx, wy, wz, inverse = whole_faces(h, span, xstep, zstep)
    return wx, prev_x(wx, xstep), wy, roll(wy, 1, 1), wz, roll(wz, zstep, 2), inverse


def coarse_spread(v, wx, wx_back, wy, wy_back, wz, wz_back, zstep):
    turned = roll(v, v.shape[-1] // 2, 2)
    low = lanes_of(v) < v.shape[-1] // 2
    after = jnp.where(low, turned, shift_up(turned))
    before = jnp.where(low, shift_down(turned), turned)
    return (
        (wx * after + wx_back * before)
        + (wy * roll(v, -1, 1) + wy_back * roll(v, 1, 1))
        + (wz * roll(v, -zstep, 2) + wz_back * roll(v, zstep, 2))
    )


def read(array, start, size, top, rows, dx=0, dy=0):
    ref, planes_off, rows_off = array
    return ref[pl.ds(start + planes_off + dx, size), pl.ds(top + rows_off + dy, rows), :]


def write(array, start, top, value):
    ref, planes_off, rows_off = array
    ref[pl.ds(start + planes_off, value.shape[0]), pl.ds(top + rows_off, value.shape[1]), :] = value


def slabs(first, last, size, body):
    if first + size == last:
        body(first)
        return

    def step(i, carry):
        body(first + i * size)
        return carry

    lax.fori_loop(0, (last - first) // size, step, 0)


def faces(h, window, step):
    here = read(h, *window)
    lane = lanes_of(here)
    width = here.shape[-1]
    not_last = lane < width - step
    wx = here + read(h, *window, dx=1)
    wy = here + read(h, *window, dy=1)
    wz = here + jnp.where(not_last, roll(here, -step, 2), 0.0)
    back = (here + read(h, *window, dx=-1)) + (here + read(h, *window, dy=-1))
    back = back + (here + jnp.where(lane >= step, roll(here, step, 2), 0.0))
    total = (wx + wy + wz) + back
    inverse = jnp.where(here > 0.0, OMEGA / total, 0.0)
    return here, wx, wy, jnp.where(not_last, wz, 0.0), total, inverse


def spread(v, weights, window, step):
    wx, wy, wz = weights
    here = read(v, *window)
    wz = read(wz, *window)
    return here, (
        (read(wx, *window) * read(v, *window, dx=1) + read(wx, *window, dx=-1) * read(v, *window, dx=-1))
        + (read(wy, *window) * read(v, *window, dy=1) + read(wy, *window, dy=-1) * read(v, *window, dy=-1))
        + (wz * roll(here, -step, 2) + roll(wz * here, step, 2))
    )


def halve_rows(value, buffer):
    count, rows, _ = value.shape
    buffer[0:count, 0:rows, :] = value
    return (
        buffer[0:count, pl.ds(0, rows // 2, stride=2), :] + buffer[0:count, pl.ds(1, rows // 2, stride=2), :]
    )


def halve_planes(value):
    pairs = value.reshape((value.shape[0] // 2, 2) + value.shape[1:])
    return pairs[:, 0] + pairs[:, 1]


def sum_blocks(value, buffer, step):
    return add_partner(halve_rows(halve_planes(value), buffer), step)


def double_rows(ref, start, value):
    count, rows, _ = value.shape
    ref[pl.ds(start, count), pl.ds(0, rows, stride=2), :] = value
    ref[pl.ds(start, count), pl.ds(1, rows, stride=2), :] = value


def double_planes(value):
    wide = jnp.broadcast_to(value[:, None], (value.shape[0], 2) + value.shape[1:])
    return wide.reshape((2 * value.shape[0],) + value.shape[1:])


def pack_block(values, buffer):
    blocks, rows, width = values[0].shape
    span = width // blocks
    for n, value in enumerate(values):
        buffer[:, n * rows : (n + 1) * rows, :] = value
    used = rows * len(values)
    lane = lane_row(width)
    packed = None
    for x in range(blocks):
        picked = pick_lanes(buffer[x], (lane % span) * blocks)[:used]
        packed = picked if packed is None else jnp.where(lanes_of(picked) // span == x, picked, packed)
    return packed


def send_to_all(packed, chunk):
    copies = min(packed.shape[0], 32)

    def copy_out(i):
        packed[pl.ds(i, copies)] = jnp.broadcast_to(chunk[None], (copies,) + chunk.shape)

    slabs(0, packed.shape[0], copies, copy_out)


def sum_whole_blocks(value, buffer):
    halved = halve_rows(value, buffer)
    lane = lane_row(value.shape[-1])
    span = value.shape[-1] // 4
    return (halved + pick_lanes(halved, lane ^ 1)) + (
        pick_lanes(halved, lane ^ span) + pick_lanes(halved, lane ^ span ^ 1)
    )


def coarse_cycle(g2, level2, level3, buffer):
    wx2, wy2, wz2, inv2 = level2
    *w3, inv3 = level3
    span = g2.shape[-1] // 4
    v2 = inv2 * g2
    r2 = KEEP * g2 + whole_spread(v2, wx2, wy2, wz2, span, 1)
    g3 = 0.125 * sum_whole_blocks(r2, buffer)
    v3 = inv3 * g3
    for _ in range(COARSE_SWEEPS - 1):
        v3 = KEEP * v3 + inv3 * (g3 + coarse_spread(v3, *w3, 2))
    double_rows(buffer, 0, v3)
    u2 = v2 + buffer[...]
    return KEEP * u2 + inv2 * (g2 + whole_spread(u2, wx2, wy2, wz2, span, 1))


def spread_out(e2, wide, around, doubled, planes):
    count, rows, width = e2.shape
    blocks = lax.axis_size("gy")
    block = rows // blocks
    span = width // 4
    for edge in (0, count + 1):
        wide[edge] = jnp.zeros(wide.shape[1:], F32)
    for edge in (0, blocks + 1):
        wide[:, edge] = jnp.zeros((count + 2,) + wide.shape[2:], F32)
    for y in range(blocks):
        wide[1 : count + 1, y + 1] = e2[:, y * block : (y + 1) * block]
    gx, gy = lax.axis_index("gx"), lax.axis_index("gy")
    for x in range(3):
        for y in range(3):
            around[x, y * block : (y + 1) * block, :] = wide[gx + x, gy + y]
    lane = lane_row(width)
    kept = 3 * block
    for j in planes:
        value = pick_lanes(around[j // 4], (j % 4) * span + lane // 4)[:kept]
        doubled[j, pl.ds(0, kept, stride=2), :] = value
        doubled[j, pl.ds(1, kept, stride=2), :] = value


def row_starts(axis, block):
    odd = is_odd(axis)
    low = (0, 0, NEAR)
    high = (block - NEAR, block - FAR, block - HALO)
    to_near = [jnp.where(odd, a, b) for a, b in zip(low, high)]
    to_far = [jnp.where(odd, b, a) for a, b in zip(low, high)]
    return to_near, to_far


def whole_strips(planes):
    return (0, planes), (0, 0, 0), (0, planes // 2, planes // 2)


def diamond_strips(planes):
    full = (HALO - NEAR + 1, planes - HALO + NEAR - 1)
    far = HALO - FAR + 1
    half = planes // 2 - far
    return full, (1, full[1], full[0] - 1), (far, far + half, half)


def strip_tiles(strips):
    (first, last), (_, _, edge), (_, _, half) = strips
    return last - first + edge + half


def pack_rows(source, starts, strips, target):
    (first, last), *halves = strips
    at = last - first
    target[0:at] = source[first:last, pl.ds(starts[0], NEAR), :]
    for start, (one, two, count) in zip(starts[1:], halves):
        if count:
            target[at : at + count, 0:FAR, :] = source[one : one + count, pl.ds(start, FAR), :]
            target[at : at + count, FAR:NEAR, :] = source[two : two + count, pl.ds(start, FAR), :]
        at += count


def unpack_rows(target, planes_off, top, bottom, strips, near, far):
    (first, last), *halves = strips
    for choose, rows in ((below, (top - NEAR, top - FAR, top - HALO)), (above, (bottom, bottom, bottom + NEAR))):
        at = last - first
        target[planes_off + first : planes_off + last, rows[0] : rows[0] + NEAR, :] = choose(
            near[0:at], far[0:at], "gy"
        )
        for row, (one, two, count) in zip(rows[1:], halves):
            if count:
                both = choose(near[at : at + count], far[at : at + count], "gy")
                for plane, value in ((planes_off + one, both[:, 0:FAR]), (planes_off + two, both[:, FAR:NEAR])):
                    target[plane : plane + count, row : row + FAR, :] = value
            at += count


def start_kernel(
    right_hbm, material_hbm, right, material, k_near, k_far, g_near, g_far, arrived,
):
    planes, rows, _ = right.shape
    copies = [
        pltpu.make_async_copy(material_hbm, material, arrived.at[0]),
        pltpu.make_async_copy(right_hbm, right, arrived.at[1]),
    ]
    for copy in copies:
        copy.start()
    copies[0].wait()
    odd = is_odd("gx")
    k_near[...] = material[pl.ds(jnp.where(odd, 0, planes - HALO), HALO)]
    k_far[...] = material[pl.ds(jnp.where(odd, planes - HALO, 0), HALO)]
    copies[1].wait()
    to_near, to_far = row_starts("gy", rows)
    strips = whole_strips(planes)
    pack_rows(right, to_near, strips, g_near)
    pack_rows(right, to_far, strips, g_far)


def table_kernel(cond, material, near, table, h, h_near):
    table[...] = jnp.zeros(table.shape, F32)
    table[0:1, 0 : cond.shape[1]] = 0.5 * cond[...]
    h[...] = look_up(material[...], table)
    h_near[...] = look_up(near[...], table)


def look_up(ids, table):
    planes, rows, width = ids.shape
    ids = ids.reshape(planes * rows, width)
    values = jnp.broadcast_to(table[0:1, :], ids.shape)
    return jnp.take_along_axis(values, ids, axis=1).reshape(planes, rows, width)


def k_kernel(h, h_near, far, table, wide, k_near, k_far):
    block = h.shape[0]
    h_far = look_up(far[...], table)
    wide[0:HALO] = below(h_near[...], h_far, "gx")
    wide[HALO : HALO + block] = h[...]
    wide[HALO + block :] = above(h_near[...], h_far, "gx")
    strips = diamond_strips(wide.shape[0])
    to_near, to_far = row_starts("gy", wide.shape[1])
    pack_rows(wide, to_near, strips, k_near)
    pack_rows(wide, to_far, strips, k_far)


def plane_strips(rows):
    strips, at = [], 0
    for distance in range(1, HALO):
        cut = HALO - -(-(HALO - 1 - distance) // 4) * 4
        tiles = (rows - 2 * cut) // 8
        strips.append((distance, cut, tiles, at))
        at += tiles
    return strips, at


def g_kernel(right, near, far, wide, g_near, g_far):
    block, rows, _ = right.shape
    top = BASE // 2
    wide[:, top + HALO : top + HALO + rows, :] = right[...]
    unpack_rows(wide, 0, top + HALO, top + HALO + rows, whole_strips(block), near, far)
    odd = is_odd("gx")
    strips, _ = plane_strips(rows + 2 * HALO)
    for distance, cut, tiles, at in strips:
        low, high = distance - 1, block - distance
        for target, plane in ((g_near, jnp.where(odd, low, high)), (g_far, jnp.where(odd, high, low))):
            for tile in range(tiles):
                target[at + tile] = wide[plane, top + cut + 8 * tile : top + cut + 8 * tile + 8, :]


def faces_kernel(
    k_wide, k_near, k_far,
    wx0, wy0, wz0, inv0, tot0, wx1, wy1, wz1, inv1, h2,
    h0, h1, buf0,
):
    top = BASE // 2
    planes, rows, _ = k_wide.shape
    h0[1 : planes + 1, top + HALO : top + HALO + rows, :] = k_wide[...]
    unpack_rows(h0, 1, top + HALO, top + HALO + rows, diamond_strips(planes), k_near, k_far)
    rows = rows + 2 * HALO

    aH0, aWX0, aH1, aWX1 = (h0, 1, top), (wx0, 1, BASE), (h1, 1, BASE), (wx1, 1, BASE)
    _, wx, wy, wz, total, inverse = faces(aH0, (0, planes, 0, rows), 1)
    write(aWX0, 0, 0, wx)
    for ref, value in ((wy0, wy), (wz0, wz), (tot0, total), (inv0, inverse)):
        write((ref, 0, BASE), 0, 0, value)
    write(aH1, 0, 0, sum_blocks(read(aH0, 0, planes, 0, rows), buf0, 1) * (1.0 / 32.0))

    planes1, rows1 = planes // 2, -(-rows // 16) * 8
    _, wx, wy, wz, _, inverse = faces(aH1, (0, planes1, 0, rows1), 2)
    write(aWX1, 0, 0, wx)
    for ref, value in ((wy1, wy), (wz1, wz), (inv1, inverse)):
        write((ref, 0, BASE), 0, 0, value)
    low = HALO // 2
    own = read(aH1, low, planes1 - HALO, low, rows // 2 - HALO)
    h2[...] = sum_blocks(own, buf0, 2) * (1.0 / 32.0)


def first_kernel(
    g_wide, g_near, g_far, wx0, wy0, wz0, inv0, wx1, wy1, wz1, inv1, h2,
    packed, g0, v0, v1, g1,
    buf0, bufp,
):
    top = BASE // 2
    planes, _, width = g0.shape
    block, rows = g_wide.shape[0], g_wide.shape[1] - BASE
    g0[HALO : HALO + block] = g_wide[...]
    strips, _ = plane_strips(rows)
    for distance, cut, tiles, at in strips:
        for choose, plane in ((below, HALO - distance), (above, planes - HALO - 1 + distance)):
            value = choose(g_near[at : at + tiles], g_far[at : at + tiles], "gx")
            g0[plane, top + cut : top + cut + 8 * tiles, :] = value.reshape(8 * tiles, width)

    aG0, aV0, aV1, aG1 = (g0, 0, top), (v0, 1, BASE), (v1, 1, BASE), (g1, 0, BASE)
    w0 = (wx0, 1, BASE), (wy0, 0, BASE), (wz0, 0, BASE)
    w1 = (wx1, 1, BASE), (wy1, 0, BASE), (wz1, 0, BASE)
    window = (0, planes, 0, rows)
    write(aV0, 0, 0, read((inv0, 0, BASE), *window) * read(aG0, *window))
    _, around = spread(aV0, w0, window, 1)
    write(aG1, 0, 0, sum_blocks(KEEP * read(aG0, *window) + around, buf0, 1) * 0.125)

    planes1, rows1 = planes // 2, -(-rows // 16) * 8
    window = (0, planes1, 0, rows1)
    write(aV1, 0, 0, read((inv1, 0, BASE), *window) * read(aG1, *window))
    low = HALO // 2
    window = (low, planes1 - HALO, low, rows // 2 - HALO)
    _, around = spread(aV1, w1, window, 2)
    g2 = sum_blocks(KEEP * read(aG1, *window) + around, buf0, 2) * 0.125
    send_to_all(packed, pack_block([g2, h2[...]], bufp))


def second_kernel(
    got, g0, wx0, wy0, wz0, inv0, tot0, v0, wx1, wy1, wz1, inv1, v1, g1,
    packed, v0n, v1n, g1n, *rest,
):
    levels, (g2, h2, buf2, wide, around, doubled, u1, e0, u0, v0m, buf0, bufp) = rest[:11], rest[11:]
    count, rows2, width = g2.shape
    gy_count = lax.axis_size("gy")
    block2 = rows2 // gy_count

    def unpack(i, carry):
        for y in range(gy_count):
            both = got[i * gy_count + y]
            g2[i, y * block2 : (y + 1) * block2, :] = both[:block2]
            h2[i, y * block2 : (y + 1) * block2, :] = both[block2:]
        return carry

    lax.fori_loop(0, count, unpack, 0)

    span = width // 4
    h = h2[...]
    level2 = whole_faces(h, span, span, 1)
    h3 = sum_whole_blocks(h, buf2) * (1.0 / 32.0)
    level3 = coarse_faces(h3, span, 2 * span, 2)
    for ref, value in zip(levels, level2 + level3):
        ref[...] = value
    spread_out(coarse_cycle(g2[...], level2, level3, buf2), wide, around, doubled, range(1, 11))

    top = BASE // 2
    planes = g0.shape[0]
    block = planes - 2 * HALO
    aG0 = (g0, 0, top)
    w0 = (wx0, 1, BASE), (wy0, 0, BASE), (wz0, 0, BASE)
    aINV0, aTOT0, aV0 = (inv0, 0, BASE), (tot0, 0, BASE), (v0, 1, BASE)
    w1 = (wx1, 1, BASE), (wy1, 0, BASE), (wz1, 0, BASE)
    aINV1, aG1, aV1 = (inv1, 0, BASE), (g1, 0, BASE), (v1, 1, BASE)

    low, block1 = HALO // 2, block // 2
    aU1 = (u1, 1, BASE)
    window = (0, planes // 2, 0, planes // 4 // 8 * 8 + 16)
    e1 = doubled[1 : 1 + planes // 4, 2 : 2 + window[3], :]
    write(aU1, 0, 0, read(aV1, *window) + double_planes(e1))
    window = (low - 4, block1 + 8, low - 4, block1 + 8)
    here, around = spread(aU1, w1, window, 2)
    swept = KEEP * here + read(aINV1, *window) * (read(aG1, *window) + around)
    double_rows(e0, low - 4, swept)

    rows = block + 16
    aU0 = (u0, 1, BASE - (HALO - 7))
    aE0 = (e0, 0, -(2 * low - 8))
    aV0M = (v0m, 1, BASE - (HALO - 6))
    aV0N = (v0n, 1, BASE - (HALO - 5))
    size = block + 16

    def correct(i):
        window = (i, size, HALO - 7, rows)
        e = double_planes(read(aE0, i // 2, size // 2, HALO - 7, rows))
        write(aU0, i, HALO - 7, read(aV0, *window) + e)

    slabs(HALO - 8, planes - HALO + 8, size, correct)

    def sweep(source, target, margin, size):
        def body(i):
            window = (i, size, HALO - margin, rows)
            here, around = spread(source, w0, window, 1)
            value = KEEP * here + read(aINV0, *window) * (read(aG0, *window) + around)
            write(target, i, HALO - margin, value)

        slabs(HALO - margin, planes - HALO + margin, size, body)

    sweep(aU0, aV0M, 6, block + 12)
    sweep(aV0M, aV0N, 5, block + 10)

    aG1N, aV1N = (g1n, 0, BASE - (low - 2)), (v1n, 1, BASE - (low - 2))
    window = (HALO - 4, block + 8, HALO - 4, block + 8)
    here, around = spread(aV0N, w0, window, 1)
    r = (read(aG0, *window) - read(aTOT0, *window) * here) + around
    write(aG1N, low - 2, low - 2, sum_blocks(r, buf0, 1) * 0.125)

    window = (low - 2, block1 + 4, low - 2, block1 + 4)
    write(aV1N, low - 2, low - 2, read(aINV1, *window) * read(aG1N, *window))
    window = (low, block1, low, block1)
    _, around = spread(aV1N, w1, window, 2)
    send_to_all(packed, pack_block([sum_blocks(KEEP * read(aG1N, *window) + around, buf0, 2) * 0.125], bufp))


def third_kernel(
    got, g0, wx0, wy0, wz0, inv0, v0n, wx1, wy1, wz1, inv1, v1n, g1n, *rest,
):
    levels, (out, g2, buf2, wide, around, doubled, u1, e0, u0) = rest[:11], rest[11:]
    count, rows2, width = g2.shape
    gy_count = lax.axis_size("gy")
    block2 = rows2 // gy_count

    def unpack(i, carry):
        for y in range(gy_count):
            g2[i, y * block2 : (y + 1) * block2, :] = got[i * gy_count + y]
        return carry

    lax.fori_loop(0, count, unpack, 0)
    values = [ref[...] for ref in levels]
    spread_out(coarse_cycle(g2[...], values[:4], values[4:], buf2), wide, around, doubled, range(3, 9))

    top = BASE // 2
    planes = g0.shape[0]
    block = planes - 2 * HALO
    aG0, aINV0 = (g0, 0, top), (inv0, 0, BASE)
    w0 = (wx0, 1, BASE), (wy0, 0, BASE), (wz0, 0, BASE)
    w1 = (wx1, 1, BASE), (wy1, 0, BASE), (wz1, 0, BASE)
    low, block1 = HALO // 2, block // 2
    aINV1 = (inv1, 0, BASE)
    aG1N, aV1N = (g1n, 0, BASE - (low - 2)), (v1n, 1, BASE - (low - 2))
    aV0N = (v0n, 1, BASE - (HALO - 5))

    aU1 = (u1, 1, BASE - (low - 2))
    window = (low - 2, block1 + 4, low - 2, block1 + 4)
    e1 = doubled[low // 2 : low // 2 + block1 // 2 + 2, low : low + block1 + 4, :]
    write(aU1, low - 2, low - 2, read(aV1N, *window) + double_planes(e1))
    window = (low - 1, block1 + 2, low - 1, block1 + 2)
    here, around = spread(aU1, w1, window, 2)
    swept = KEEP * here + read(aINV1, *window) * (read(aG1N, *window) + around)
    double_rows(e0, low - 1, swept)

    aU0 = (u0, 1, BASE - (HALO - 1))
    aE0 = (e0, 0, -(2 * low - 2))
    size = block + 4
    rows = block + 2

    def correct(i):
        window = (i, size, HALO - 1, rows)
        e = double_planes(read(aE0, i // 2, size // 2, HALO - 1, rows))
        write(aU0, i, HALO - 1, read(aV0N, *window) + e)

    slabs(HALO - 2, planes - HALO + 2, size, correct)

    def sweep(i):
        window = (i, size, HALO, block)
        here, around = spread(aU0, w0, window, 1)
        out[pl.ds(i - HALO, size)] = KEEP * here + read(aINV0, *window) * (read(aG0, *window) + around)

    size = block
    slabs(HALO, planes - HALO, size, sweep)


def kernel_call(body, outs, scratch, args, cost=None):
    def size(shape):
        total = 4
        for length in shape:
            total *= length
        return total

    shapes = [a.shape for a in args] + list(outs) + list(scratch)
    limit = sum(size(s) for s in shapes) + (8 << 20)
    return pl.pallas_call(
        body,
        out_shape=[jax.ShapeDtypeStruct(s, F32) for s in outs],
        in_specs=[pl.BlockSpec(memory_space=pltpu.VMEM)] * len(args),
        out_specs=[pl.BlockSpec(memory_space=pltpu.VMEM)] * len(outs),
        scratch_shapes=[pltpu.VMEM(s, F32) for s in scratch],
        compiler_params=pltpu.CompilerParams(vmem_limit_bytes=limit),
        cost_estimate=cost,
    )(*args)


def local(right_side, material, conductivity):
    bx, by, bz = right_side.shape
    gx_count, gy_count = lax.axis_size("gx"), lax.axis_size("gy")
    devices = gx_count * gy_count

    X, Y = bx + 2 * HALO, by + 2 * HALO
    YA = Y + BASE
    YB = Y + 2 * BASE
    X1, Y1 = X // 2, -(-Y // 16) * 8 + 2 * BASE
    xb, yb = bx // 4, by // 4

    strip = (strip_tiles(whole_strips(bx)), NEAR, bz)
    def ints(*shape):
        return jax.ShapeDtypeStruct(shape, jnp.int32)

    def floats(*shape):
        return jax.ShapeDtypeStruct(shape, F32)

    outs = [floats(bx, by, bz), ints(bx, by, bz), ints(HALO, by, bz), ints(HALO, by, bz), floats(*strip), floats(*strip)]
    right, material, k_near, k_far, g_near, g_far = pl.pallas_call(
        start_kernel,
        out_shape=outs,
        in_specs=[pl.BlockSpec(memory_space=pl.ANY)] * 2,
        out_specs=[pl.BlockSpec(memory_space=pltpu.VMEM)] * len(outs),
        scratch_shapes=[pltpu.SemaphoreType.DMA((2,))],
        compiler_params=pltpu.CompilerParams(vmem_limit_bytes=START_LIMIT),
    )(right_side, material)
    k_near, k_far = trade(k_near, k_far, "gx")
    g_near, g_far = trade(g_near, g_far, "gy")
    table, h, h_near = kernel_call(
        table_kernel, [(8, bz), (bx, by, bz), (HALO, by, bz)], [], [conductivity[None], material, k_near]
    )
    strip = (plane_strips(Y)[1], 8, bz)
    g_wide, g_near, g_far = kernel_call(
        g_kernel, [(bx, YA, bz), strip, strip], [], [right, g_near, g_far]
    )
    strip = (strip_tiles(diamond_strips(X)), NEAR, bz)
    k_wide, k_near, k_far = kernel_call(
        k_kernel, [(X, by, bz), strip, strip], [], [h, h_near, k_far, table]
    )
    g_near, g_far = trade(g_near, g_far, "gx")
    k_near, k_far = trade(k_near, k_far, "gy")

    pad0, full0, pad1, full1 = (X + 2, YB, bz), (X, YB, bz), (X1 + 2, Y1, bz), (X1, Y1, bz)
    wx0, wy0, wz0, inv0, tot0, wx1, wy1, wz1, inv1, h2 = kernel_call(
        faces_kernel,
        [pad0, full0, full0, full0, full0, pad1, full1, full1, full1, (xb, yb, bz)],
        [(X + 2, YA, bz), pad1, (X1, Y, bz)],
        [k_wide, k_near, k_far],
        pl.CostEstimate(flops=0, bytes_accessed=8 << 20, transcendentals=0),
    )
    packed, g0, v0, v1, g1 = kernel_call(
        first_kernel,
        [(devices, 2 * yb, bz), (X, YA, bz), pad0, pad1, full1],
        [(X1, Y, bz), (xb, 8, bz)],
        [g_wide, g_near, g_far, wx0, wy0, wz0, inv0, wx1, wy1, wz1, inv1, h2],
    )
    got = everywhere(packed)
    level2 = (gx_count, gy_count * yb, bz)
    level3 = (gx_count, gy_count * yb // 2, bz)
    coarse_scratch = [
        level2, (gx_count + 2, gy_count + 2, yb, bz), (3, 16, bz), (3 * xb, 32, bz), pad1, (X1, by + 24, bz), pad0,
    ]
    packed, v0n, v1n, g1n, *levels = kernel_call(
        second_kernel,
        [(devices, yb, bz), pad0, pad1, full1] + [level2] * 4 + [level3] * 7,
        [level2, level2] + coarse_scratch + [pad0, (X1, Y, bz), (xb, 8, bz)],
        [got, g0, wx0, wy0, wz0, inv0, tot0, v0, wx1, wy1, wz1, inv1, v1, g1],
    )
    got = everywhere(packed)
    (out,) = kernel_call(
        third_kernel,
        [(bx, by, bz)],
        [level2] + coarse_scratch,
        [got, g0, wx0, wy0, wz0, inv0, v0n, wx1, wy1, wz1, inv1, v1n, g1n] + levels,
    )
    return out


def solution(mesh):
    return jax.shard_map(
        local,
        mesh=mesh,
        in_specs=(P("gx", "gy", None), P("gx", "gy", None), P()),
        out_specs=P("gx", "gy", None),
        check_vma=False,
    )
```

```python
import jax
import jax.numpy as jnp
from jax import lax
from jax.experimental import pallas as pl
from jax.experimental.pallas import tpu as pltpu
from jax.sharding import PartitionSpec as P

COARSE_SWEEPS = 6
OMEGA = 0.8
KEEP = 1.0 - OMEGA
HALO = 12
NEAR = 8
FAR = HALO - NEAR
BASE = 8
UNPACK = 8
F32 = jnp.float32
START_LIMIT = int(53.25 * 2**20)


def near_partner(index, count):
    return index ^ 1 if index ^ 1 < count else index


def far_partner(index, count):
    return (index - 1 ^ 1) + 1


def route(axis, far):
    gx_count, gy_count = lax.axis_size("gx"), lax.axis_size("gy")
    pairs = []
    for x in range(gx_count):
        for y in range(gy_count):
            if axis == "gx":
                if not far:
                    a, b = near_partner(x, gx_count), y
                elif 0 < x < gx_count - 1:
                    a, b = far_partner(x, gx_count), y
                else:
                    a, b = x, near_partner(y, gy_count)
            else:
                if not far:
                    a, b = x, near_partner(y, gy_count)
                elif 0 < y < gy_count - 1:
                    a, b = x, far_partner(y, gy_count)
                else:
                    a, b = near_partner(x, gx_count), y
            pairs.append((x * gy_count + y, a * gy_count + b))
    return pairs


def trade(to_near, to_far, axis):
    from_far = lax.ppermute(to_far, ("gx", "gy"), route(axis, True))
    from_near = lax.ppermute(to_near, ("gx", "gy"), route(axis, False))
    return from_near, from_far


def everywhere(copies):
    return lax.all_to_all(copies, ("gx", "gy"), 0, 0)


def is_odd(axis):
    return lax.axis_index(axis) % 2 == 1


def has_below(axis):
    return lax.axis_index(axis) > 0


def has_above(axis):
    return lax.axis_index(axis) < lax.axis_size(axis) - 1


def below(near, far, axis):
    return jnp.where(has_below(axis), jnp.where(is_odd(axis), near, far), 0.0)


def above(near, far, axis):
    return jnp.where(has_above(axis), jnp.where(is_odd(axis), far, near), 0.0)


def roll(value, shift, axis):
    return pltpu.roll(value, shift % value.shape[axis], axis=axis)


def lanes_of(value):
    return lax.broadcasted_iota(jnp.int32, value.shape, value.ndim - 1)


def rows_of(value):
    return lax.broadcasted_iota(jnp.int32, value.shape, value.ndim - 2)


def lane_row(width):
    return lax.broadcasted_iota(jnp.int32, (1, width), 1)


def pick_lanes(value, index):
    flat = value.reshape(-1, value.shape[-1])
    index = jnp.broadcast_to(index, flat.shape)
    return jnp.take_along_axis(flat, index, axis=1).reshape(value.shape)


def add_partner(value, apart):
    return value + pick_lanes(value, lane_row(value.shape[-1]) ^ apart)


def shift_up(value):
    return jnp.concatenate([value[1:], jnp.zeros_like(value[:1])], axis=0)


def shift_down(value):
    return jnp.concatenate([jnp.zeros_like(value[:1]), value[:-1]], axis=0)


def next_x(value, step):
    turned = roll(value, -step, 2)
    return jnp.where(lanes_of(value) < value.shape[-1] - step, turned, shift_up(turned))


def prev_x(value, step):
    turned = roll(value, step, 2)
    return jnp.where(lanes_of(value) >= step, turned, shift_down(turned))


def whole_faces(h, span, xstep, zstep):
    in_span = lanes_of(h) % span
    row = rows_of(h)
    not_last_z, not_first_z = in_span < span - zstep, in_span >= zstep
    not_last_y, not_first_y = row < h.shape[1] - 1, row >= 1
    wx = h + next_x(h, xstep)
    wy = h + jnp.where(not_last_y, roll(h, -1, 1), 0.0)
    wz = h + jnp.where(not_last_z, roll(h, -zstep, 2), 0.0)
    back = h + prev_x(h, xstep)
    back = back + (h + jnp.where(not_first_y, roll(h, 1, 1), 0.0))
    back = back + (h + jnp.where(not_first_z, roll(h, zstep, 2), 0.0))
    total = wx + wy + wz + back
    return wx, jnp.where(not_last_y, wy, 0.0), jnp.where(not_last_z, wz, 0.0), OMEGA / total


def whole_spread(v, wx, wy, wz, xstep, zstep):
    return (
        (wx * next_x(v, xstep) + prev_x(wx * v, xstep))
        + (wy * roll(v, -1, 1) + roll(wy * v, 1, 1))
        + (wz * roll(v, -zstep, 2) + roll(wz * v, zstep, 2))
    )


def coarse_faces(h, span, xstep, zstep):
    wx, wy, wz, inverse = whole_faces(h, span, xstep, zstep)
    return wx, prev_x(wx, xstep), wy, roll(wy, 1, 1), wz, roll(wz, zstep, 2), inverse


def coarse_spread(v, wx, wx_back, wy, wy_back, wz, wz_back, zstep):
    turned = roll(v, v.shape[-1] // 2, 2)
    low = lanes_of(v) < v.shape[-1] // 2
    after = jnp.where(low, turned, shift_up(turned))
    before = jnp.where(low, shift_down(turned), turned)
    return (
        (wx * after + wx_back * before)
        + (wy * roll(v, -1, 1) + wy_back * roll(v, 1, 1))
        + (wz * roll(v, -zstep, 2) + wz_back * roll(v, zstep, 2))
    )


def read(array, start, size, top, rows, dx=0, dy=0):
    ref, planes_off, rows_off = array
    return ref[pl.ds(start + planes_off + dx, size), pl.ds(top + rows_off + dy, rows), :]


def write(array, start, top, value):
    ref, planes_off, rows_off = array
    ref[pl.ds(start + planes_off, value.shape[0]), pl.ds(top + rows_off, value.shape[1]), :] = value


def slabs(first, last, size, body):
    if first + size == last:
        body(first)
        return

    def step(i, carry):
        body(first + i * size)
        return carry

    lax.fori_loop(0, (last - first) // size, step, 0)


def faces(h, window, step):
    here = read(h, *window)
    lane = lanes_of(here)
    width = here.shape[-1]
    not_last = lane < width - step
    wx = here + read(h, *window, dx=1)
    wy = here + read(h, *window, dy=1)
    wz = here + jnp.where(not_last, roll(here, -step, 2), 0.0)
    back = (here + read(h, *window, dx=-1)) + (here + read(h, *window, dy=-1))
    back = back + (here + jnp.where(lane >= step, roll(here, step, 2), 0.0))
    total = (wx + wy + wz) + back
    inverse = jnp.where(here > 0.0, OMEGA / total, 0.0)
    return here, wx, wy, jnp.where(not_last, wz, 0.0), total, inverse


def spread(v, weights, window, step):
    wx, wy, wz = weights
    here = read(v, *window)
    wz = read(wz, *window)
    return here, (
        (read(wx, *window) * read(v, *window, dx=1) + read(wx, *window, dx=-1) * read(v, *window, dx=-1))
        + (read(wy, *window) * read(v, *window, dy=1) + read(wy, *window, dy=-1) * read(v, *window, dy=-1))
        + (wz * roll(here, -step, 2) + roll(wz * here, step, 2))
    )


def diamond(planes, rows, reach):
    groups = {}
    for distance in range(0, reach + 2, 2):
        rest = reach - max(distance - 1, 0)
        wide = -(-(rows - 2 * HALO + 2 * rest) // 8) * 8
        top = HALO - (wide - (rows - 2 * HALO)) // 2
        first, last = groups.get((top, wide), (distance, distance))
        groups[(top, wide)] = (first, distance)
    found = []
    for (top, wide), (first, last) in groups.items():
        if first == 0:
            found.append((HALO - last, planes - 2 * HALO + 2 * last, top, wide))
        else:
            size = last - first + 2
            found.append((HALO - last, size, top, wide))
            found.append((planes - HALO + first - 2, size, top, wide))
    return found


def halve_rows(value, buffer):
    count, rows, _ = value.shape
    buffer[0:count, 0:rows, :] = value
    return (
        buffer[0:count, pl.ds(0, rows // 2, stride=2), :] + buffer[0:count, pl.ds(1, rows // 2, stride=2), :]
    )


def halve_planes(value):
    pairs = value.reshape((value.shape[0] // 2, 2) + value.shape[1:])
    return pairs[:, 0] + pairs[:, 1]


def sum_blocks(value, buffer, step):
    return add_partner(halve_rows(halve_planes(value), buffer), step)


def double_rows(ref, start, value):
    count, rows, _ = value.shape
    ref[pl.ds(start, count), pl.ds(0, rows, stride=2), :] = value
    ref[pl.ds(start, count), pl.ds(1, rows, stride=2), :] = value


def double_planes(value):
    wide = jnp.broadcast_to(value[:, None], (value.shape[0], 2) + value.shape[1:])
    return wide.reshape((2 * value.shape[0],) + value.shape[1:])


def pack_block(values, buffer):
    blocks, rows, width = values[0].shape
    span = width // blocks
    for n, value in enumerate(values):
        buffer[:, n * rows : (n + 1) * rows, :] = value
    used = rows * len(values)
    lane = lane_row(width)
    first = (lane % span) * blocks
    packed = None
    for x in range(blocks):
        picked = (pick_lanes(buffer[x], first) + pick_lanes(buffer[x], first + blocks // 2))[:used]
        packed = picked if packed is None else jnp.where(lanes_of(picked) // span == x, picked, packed)
    return packed


def send_to_all(packed, chunk):
    copies = min(packed.shape[0], 32)

    def copy_out(i):
        packed[pl.ds(i, copies)] = jnp.broadcast_to(chunk[None], (copies,) + chunk.shape)

    slabs(0, packed.shape[0], copies, copy_out)


def sum_whole_blocks(value, buffer):
    halved = halve_rows(value, buffer)
    lane = lane_row(value.shape[-1])
    span = value.shape[-1] // 4
    return (halved + pick_lanes(halved, lane ^ 1)) + (
        pick_lanes(halved, lane ^ span) + pick_lanes(halved, lane ^ span ^ 1)
    )


def coarse_cycle(g2, level2, level3, buffer):
    wx2, wy2, wz2, inv2 = level2
    *w3, inv3 = level3
    span = g2.shape[-1] // 4
    v2 = inv2 * g2
    r2 = KEEP * g2 + whole_spread(v2, wx2, wy2, wz2, span, 1)
    g3 = 0.125 * sum_whole_blocks(r2, buffer)
    v3 = inv3 * g3
    for _ in range(COARSE_SWEEPS - 1):
        v3 = KEEP * v3 + inv3 * (g3 + coarse_spread(v3, *w3, 2))
    double_rows(buffer, 0, v3)
    u2 = v2 + buffer[...]
    return KEEP * u2 + inv2 * (g2 + whole_spread(u2, wx2, wy2, wz2, span, 1))


def spread_out(e2, wide, around, doubled, planes):
    count, rows, width = e2.shape
    blocks = lax.axis_size("gy")
    block = rows // blocks
    span = width // 4
    for edge in (0, count + 1):
        wide[edge] = jnp.zeros(wide.shape[1:], F32)
    for edge in (0, blocks + 1):
        wide[:, edge] = jnp.zeros((count + 2,) + wide.shape[2:], F32)
    for y in range(blocks):
        wide[1 : count + 1, y + 1] = e2[:, y * block : (y + 1) * block]
    gx, gy = lax.axis_index("gx"), lax.axis_index("gy")
    for x in range(3):
        for y in range(3):
            around[x, y * block : (y + 1) * block, :] = wide[gx + x, gy + y]
    lane = lane_row(width)
    kept = 3 * block
    for j in planes:
        value = pick_lanes(around[j // 4], (j % 4) * span + lane // 4)[:kept]
        doubled[j, pl.ds(0, kept, stride=2), :] = value
        doubled[j, pl.ds(1, kept, stride=2), :] = value


def row_starts(axis, block):
    odd = is_odd(axis)
    low = (0, 0, NEAR)
    high = (block - NEAR, block - FAR, block - HALO)
    to_near = [jnp.where(odd, a, b) for a, b in zip(low, high)]
    to_far = [jnp.where(odd, b, a) for a, b in zip(low, high)]
    return to_near, to_far


def whole_strips(planes):
    return (0, planes), (0, 0, 0), (0, planes // 2, planes // 2)


def diamond_strips(planes):
    full = (HALO - NEAR + 1, planes - HALO + NEAR - 1)
    far = HALO - FAR + 1
    half = planes // 2 - far
    return full, (1, full[1], full[0] - 1), (far, far + half, half)


def strip_tiles(strips):
    (first, last), (_, _, edge), (_, _, half) = strips
    return last - first + edge + half


def pack_rows(source, starts, strips, target):
    (first, last), *halves = strips
    at = last - first
    target[0:at] = source[first:last, pl.ds(starts[0], NEAR), :]
    for start, (one, two, count) in zip(starts[1:], halves):
        if count:
            target[at : at + count, 0:FAR, :] = source[one : one + count, pl.ds(start, FAR), :]
            target[at : at + count, FAR:NEAR, :] = source[two : two + count, pl.ds(start, FAR), :]
        at += count


def unpack_rows(target, planes_off, top, bottom, strips, near, far):
    (first, last), *halves = strips
    for choose, rows in ((below, (top - NEAR, top - FAR, top - HALO)), (above, (bottom, bottom, bottom + NEAR))):
        at = last - first
        target[planes_off + first : planes_off + last, rows[0] : rows[0] + NEAR, :] = choose(
            near[0:at], far[0:at], "gy"
        )
        for row, (one, two, count) in zip(rows[1:], halves):
            if count:
                both = choose(near[at : at + count], far[at : at + count], "gy")
                for plane, value in ((planes_off + one, both[:, 0:FAR]), (planes_off + two, both[:, FAR:NEAR])):
                    target[plane : plane + count, row : row + FAR, :] = value
            at += count


def start_kernel(
    right_hbm, material_hbm, right, material, k_near, k_far, g_near, g_far, arrived,
):
    planes, rows, _ = right.shape
    copies = [
        pltpu.make_async_copy(material_hbm, material, arrived.at[0]),
        pltpu.make_async_copy(right_hbm, right, arrived.at[1]),
    ]
    for copy in copies:
        copy.start()
    copies[0].wait()
    odd = is_odd("gx")
    k_near[...] = material[pl.ds(jnp.where(odd, 0, planes - HALO), HALO)]
    k_far[...] = material[pl.ds(jnp.where(odd, planes - HALO, 0), HALO)]
    copies[1].wait()
    to_near, to_far = row_starts("gy", rows)
    strips = whole_strips(planes)
    pack_rows(right, to_near, strips, g_near)
    pack_rows(right, to_far, strips, g_far)


def table_kernel(cond, material, near, table, h, h_near):
    table[...] = jnp.zeros(table.shape, F32)
    table[0:1, 0 : cond.shape[1]] = 0.5 * cond[...]
    h[...] = look_up(material[...], table)
    h_near[...] = look_up(near[...], table)


def look_up(ids, table):
    planes, rows, width = ids.shape
    ids = ids.reshape(planes * rows, width)
    values = jnp.broadcast_to(table[0:1, :], ids.shape)
    return jnp.take_along_axis(values, ids, axis=1).reshape(planes, rows, width)


def k_kernel(h, h_near, far, table, wide, k_near, k_far):
    block = h.shape[0]
    h_far = look_up(far[...], table)
    wide[0:HALO] = below(h_near[...], h_far, "gx")
    wide[HALO : HALO + block] = h[...]
    wide[HALO + block :] = above(h_near[...], h_far, "gx")
    strips = diamond_strips(wide.shape[0])
    to_near, to_far = row_starts("gy", wide.shape[1])
    pack_rows(wide, to_near, strips, k_near)
    pack_rows(wide, to_far, strips, k_far)


def plane_strips(rows):
    strips, at = [], 0
    for distance in range(1, HALO):
        cut = HALO - -(-(HALO - 1 - distance) // 4) * 4
        tiles = (rows - 2 * cut) // 8
        strips.append((distance, cut, tiles, at))
        at += tiles
    return strips, at


def g_kernel(right, near, far, wide, g_near, g_far):
    block, rows, _ = right.shape
    top = BASE // 2
    wide[:, top + HALO : top + HALO + rows, :] = right[...]
    unpack_rows(wide, 0, top + HALO, top + HALO + rows, whole_strips(block), near, far)
    odd = is_odd("gx")
    strips, _ = plane_strips(rows + 2 * HALO)
    for distance, cut, tiles, at in strips:
        low, high = distance - 1, block - distance
        for target, plane in ((g_near, jnp.where(odd, low, high)), (g_far, jnp.where(odd, high, low))):
            for tile in range(tiles):
                target[at + tile] = wide[plane, top + cut + 8 * tile : top + cut + 8 * tile + 8, :]


def faces_kernel(
    k_wide, k_near, k_far,
    wx0, wy0, wz0, inv0, tot0, wx1, wy1, wz1, inv1, h2,
    h0, h1, buf0,
):
    top = BASE // 2
    planes, rows, _ = k_wide.shape
    h0[1 : planes + 1, top + HALO : top + HALO + rows, :] = k_wide[...]
    unpack_rows(h0, 1, top + HALO, top + HALO + rows, diamond_strips(planes), k_near, k_far)
    rows = rows + 2 * HALO

    aH0, aWX0, aH1, aWX1 = (h0, 1, top), (wx0, 1, BASE), (h1, 1, BASE), (wx1, 1, BASE)
    for window in diamond(planes, rows, HALO - 1):
        start, _, above_rows, _ = window
        _, wx, wy, wz, total, inverse = faces(aH0, window, 1)
        write(aWX0, start, above_rows, wx)
        for ref, value in ((wy0, wy), (wz0, wz), (tot0, total), (inv0, inverse)):
            write((ref, 0, BASE), start, above_rows, value)
    write(aH1, 0, 0, sum_blocks(read(aH0, 0, planes, 0, rows), buf0, 1) * (1.0 / 32.0))

    planes1, rows1 = planes // 2, -(-rows // 16) * 8
    _, wx, wy, wz, _, inverse = faces(aH1, (0, planes1, 0, rows1), 2)
    write(aWX1, 0, 0, wx)
    for ref, value in ((wy1, wy), (wz1, wz), (inv1, inverse)):
        write((ref, 0, BASE), 0, 0, value)
    low = HALO // 2
    own = read(aH1, low, planes1 - HALO, low, rows // 2 - HALO)
    h2[...] = halve_rows(halve_planes(own), buf0) * (1.0 / 32.0)


def first_kernel(
    g_wide, g_near, g_far, wx0, wy0, wz0, inv0, wx1, wy1, wz1, inv1, h2,
    packed, g0, v0, v1, g1,
    buf0, bufp,
):
    top = BASE // 2
    planes, _, width = g0.shape
    block, rows = g_wide.shape[0], g_wide.shape[1] - BASE
    g0[HALO : HALO + block] = g_wide[...]
    strips, _ = plane_strips(rows)
    for distance, cut, tiles, at in strips:
        for choose, plane in ((below, HALO - distance), (above, planes - HALO - 1 + distance)):
            value = choose(g_near[at : at + tiles], g_far[at : at + tiles], "gx")
            g0[plane, top + cut : top + cut + 8 * tiles, :] = value.reshape(8 * tiles, width)

    aG0, aV0, aV1, aG1 = (g0, 0, top), (v0, 1, BASE), (v1, 1, BASE), (g1, 0, BASE)
    w0 = (wx0, 1, BASE), (wy0, 0, BASE), (wz0, 0, BASE)
    w1 = (wx1, 1, BASE), (wy1, 0, BASE), (wz1, 0, BASE)
    for window in diamond(planes, rows, HALO - 1):
        write(aV0, window[0], window[2], read((inv0, 0, BASE), *window) * read(aG0, *window))
    for window in diamond(planes, rows, HALO - 2):
        start, _, above_rows, _ = window
        _, around = spread(aV0, w0, window, 1)
        r = KEEP * read(aG0, *window) + around
        write(aG1, start // 2, above_rows // 2, sum_blocks(r, buf0.at[start // 2 :], 1) * 0.125)

    planes1, rows1 = planes // 2, -(-rows // 16) * 8
    window = (0, planes1, 0, rows1)
    write(aV1, 0, 0, read((inv1, 0, BASE), *window) * read(aG1, *window))
    low = HALO // 2
    window = (low, planes1 - HALO, low, rows // 2 - HALO)
    _, around = spread(aV1, w1, window, 2)
    g2 = halve_rows(halve_planes(KEEP * read(aG1, *window) + around), buf0) * 0.125
    send_to_all(packed, pack_block([g2, h2[...]], bufp))


def second_kernel(
    got, g0, wx0, wy0, wz0, inv0, tot0, v0, wx1, wy1, wz1, inv1, v1, g1,
    packed, v0n, v1n, g1n, *rest,
):
    levels, (g2, h2, buf2, wide, around, doubled, u1, e0, u0, v0m, buf0, bufp) = rest[:11], rest[11:]
    count, rows2, width = g2.shape
    gy_count = lax.axis_size("gy")
    block2 = rows2 // gy_count

    def unpack(i):
        for x in range(UNPACK):
            for y in range(gy_count):
                both = got[(i + x) * gy_count + y]
                g2[i + x, y * block2 : (y + 1) * block2, :] = both[:block2]
                h2[i + x, y * block2 : (y + 1) * block2, :] = both[block2:]

    slabs(0, count, UNPACK, unpack)

    span = width // 4
    h = h2[...]
    level2 = whole_faces(h, span, span, 1)
    h3 = sum_whole_blocks(h, buf2) * (1.0 / 32.0)
    level3 = coarse_faces(h3, span, 2 * span, 2)
    for ref, value in zip(levels, level2 + level3):
        ref[...] = value
    spread_out(coarse_cycle(g2[...], level2, level3, buf2), wide, around, doubled, range(1, 11))

    top = BASE // 2
    planes = g0.shape[0]
    block = planes - 2 * HALO
    aG0 = (g0, 0, top)
    w0 = (wx0, 1, BASE), (wy0, 0, BASE), (wz0, 0, BASE)
    aINV0, aTOT0, aV0 = (inv0, 0, BASE), (tot0, 0, BASE), (v0, 1, BASE)
    w1 = (wx1, 1, BASE), (wy1, 0, BASE), (wz1, 0, BASE)
    aINV1, aG1, aV1 = (inv1, 0, BASE), (g1, 0, BASE), (v1, 1, BASE)

    low, block1 = HALO // 2, block // 2
    aU1 = (u1, 1, BASE)
    window = (0, planes // 2, 0, planes // 4 // 8 * 8 + 16)
    e1 = doubled[1 : 1 + planes // 4, 2 : 2 + window[3], :]
    write(aU1, 0, 0, read(aV1, *window) + double_planes(e1))
    window = (low - 4, block1 + 8, low - 4, block1 + 8)
    here, around = spread(aU1, w1, window, 2)
    swept = KEEP * here + read(aINV1, *window) * (read(aG1, *window) + around)
    double_rows(e0, low - 4, swept)

    rows = block + 16
    aU0 = (u0, 1, BASE - (HALO - 7))
    aE0 = (e0, 0, -(2 * low - 8))
    aV0M = (v0m, 1, BASE - (HALO - 6))
    aV0N = (v0n, 1, BASE - (HALO - 5))
    size = block + 16

    def correct(i):
        window = (i, size, HALO - 7, rows)
        e = double_planes(read(aE0, i // 2, size // 2, HALO - 7, rows))
        write(aU0, i, HALO - 7, read(aV0, *window) + e)

    slabs(HALO - 8, planes - HALO + 8, size, correct)

    def sweep(source, target, margin, size):
        def body(i):
            window = (i, size, HALO - margin, rows)
            here, around = spread(source, w0, window, 1)
            value = KEEP * here + read(aINV0, *window) * (read(aG0, *window) + around)
            write(target, i, HALO - margin, value)

        slabs(HALO - margin, planes - HALO + margin, size, body)

    sweep(aU0, aV0M, 6, block + 12)
    sweep(aV0M, aV0N, 5, block + 10)

    aG1N, aV1N = (g1n, 0, BASE - (low - 2)), (v1n, 1, BASE - (low - 2))
    window = (HALO - 4, block + 8, HALO - 4, block + 8)
    here, around = spread(aV0N, w0, window, 1)
    r = (read(aG0, *window) - read(aTOT0, *window) * here) + around
    write(aG1N, low - 2, low - 2, sum_blocks(r, buf0, 1) * 0.125)

    window = (low - 2, block1 + 4, low - 2, block1 + 4)
    write(aV1N, low - 2, low - 2, read(aINV1, *window) * read(aG1N, *window))
    window = (low, block1, low, block1)
    _, around = spread(aV1N, w1, window, 2)
    g2 = halve_rows(halve_planes(KEEP * read(aG1N, *window) + around), buf0) * 0.125
    send_to_all(packed, pack_block([g2], bufp))


def third_kernel(
    got, g0, wx0, wy0, wz0, inv0, v0n, wx1, wy1, wz1, inv1, v1n, g1n, *rest,
):
    levels, (out, g2, buf2, wide, around, doubled, u1, e0, u0) = rest[:11], rest[11:]
    count, rows2, width = g2.shape
    gy_count = lax.axis_size("gy")
    block2 = rows2 // gy_count

    def unpack(i):
        for x in range(UNPACK):
            for y in range(gy_count):
                g2[i + x, y * block2 : (y + 1) * block2, :] = got[(i + x) * gy_count + y]

    slabs(0, count, UNPACK, unpack)
    values = [ref[...] for ref in levels]
    spread_out(coarse_cycle(g2[...], values[:4], values[4:], buf2), wide, around, doubled, range(3, 9))

    top = BASE // 2
    planes = g0.shape[0]
    block = planes - 2 * HALO
    aG0, aINV0 = (g0, 0, top), (inv0, 0, BASE)
    w0 = (wx0, 1, BASE), (wy0, 0, BASE), (wz0, 0, BASE)
    w1 = (wx1, 1, BASE), (wy1, 0, BASE), (wz1, 0, BASE)
    low, block1 = HALO // 2, block // 2
    aINV1 = (inv1, 0, BASE)
    aG1N, aV1N = (g1n, 0, BASE - (low - 2)), (v1n, 1, BASE - (low - 2))
    aV0N = (v0n, 1, BASE - (HALO - 5))

    aU1 = (u1, 1, BASE - (low - 2))
    window = (low - 2, block1 + 4, low - 2, block1 + 4)
    e1 = doubled[low // 2 : low // 2 + block1 // 2 + 2, low : low + block1 + 4, :]
    write(aU1, low - 2, low - 2, read(aV1N, *window) + double_planes(e1))
    window = (low - 1, block1 + 2, low - 1, block1 + 2)
    here, around = spread(aU1, w1, window, 2)
    swept = KEEP * here + read(aINV1, *window) * (read(aG1N, *window) + around)
    double_rows(e0, low - 1, swept)

    aU0 = (u0, 1, BASE - (HALO - 1))
    aE0 = (e0, 0, -(2 * low - 2))
    size = block + 4
    rows = block + 2

    def correct(i):
        window = (i, size, HALO - 1, rows)
        e = double_planes(read(aE0, i // 2, size // 2, HALO - 1, rows))
        write(aU0, i, HALO - 1, read(aV0N, *window) + e)

    slabs(HALO - 2, planes - HALO + 2, size, correct)

    def sweep(i):
        window = (i, size, HALO, block)
        here, around = spread(aU0, w0, window, 1)
        out[pl.ds(i - HALO, size)] = KEEP * here + read(aINV0, *window) * (read(aG0, *window) + around)

    size = block
    slabs(HALO, planes - HALO, size, sweep)


def kernel_call(body, outs, scratch, args, cost=None):
    def size(shape):
        total = 4
        for length in shape:
            total *= length
        return total

    shapes = [a.shape for a in args] + list(outs) + list(scratch)
    limit = sum(size(s) for s in shapes) + (8 << 20)
    return pl.pallas_call(
        body,
        out_shape=[jax.ShapeDtypeStruct(s, F32) for s in outs],
        in_specs=[pl.BlockSpec(memory_space=pltpu.VMEM)] * len(args),
        out_specs=[pl.BlockSpec(memory_space=pltpu.VMEM)] * len(outs),
        scratch_shapes=[pltpu.VMEM(s, F32) for s in scratch],
        compiler_params=pltpu.CompilerParams(vmem_limit_bytes=limit),
        cost_estimate=cost,
    )(*args)


def local(right_side, material, conductivity):
    bx, by, bz = right_side.shape
    gx_count, gy_count = lax.axis_size("gx"), lax.axis_size("gy")
    devices = gx_count * gy_count

    X, Y = bx + 2 * HALO, by + 2 * HALO
    YA = Y + BASE
    YB = Y + 2 * BASE
    X1, Y1 = X // 2, -(-Y // 16) * 8 + 2 * BASE
    xb, yb = bx // 4, by // 4

    strip = (strip_tiles(whole_strips(bx)), NEAR, bz)
    def ints(*shape):
        return jax.ShapeDtypeStruct(shape, jnp.int32)

    def floats(*shape):
        return jax.ShapeDtypeStruct(shape, F32)

    outs = [floats(bx, by, bz), ints(bx, by, bz), ints(HALO, by, bz), ints(HALO, by, bz), floats(*strip), floats(*strip)]
    right, material, k_near, k_far, g_near, g_far = pl.pallas_call(
        start_kernel,
        out_shape=outs,
        in_specs=[pl.BlockSpec(memory_space=pl.ANY)] * 2,
        out_specs=[pl.BlockSpec(memory_space=pltpu.VMEM)] * len(outs),
        scratch_shapes=[pltpu.SemaphoreType.DMA((2,))],
        compiler_params=pltpu.CompilerParams(vmem_limit_bytes=START_LIMIT),
    )(right_side, material)
    k_near, k_far = trade(k_near, k_far, "gx")
    g_near, g_far = trade(g_near, g_far, "gy")
    table, h, h_near = kernel_call(
        table_kernel, [(8, bz), (bx, by, bz), (HALO, by, bz)], [], [conductivity[None], material, k_near]
    )
    strip = (plane_strips(Y)[1], 8, bz)
    g_wide, g_near, g_far = kernel_call(
        g_kernel, [(bx, YA, bz), strip, strip], [], [right, g_near, g_far]
    )
    strip = (strip_tiles(diamond_strips(X)), NEAR, bz)
    k_wide, k_near, k_far = kernel_call(
        k_kernel, [(X, by, bz), strip, strip], [], [h, h_near, k_far, table]
    )
    g_near, g_far = trade(g_near, g_far, "gx")
    k_near, k_far = trade(k_near, k_far, "gy")

    pad0, full0, pad1, full1 = (X + 2, YB, bz), (X, YB, bz), (X1 + 2, Y1, bz), (X1, Y1, bz)
    wx0, wy0, wz0, inv0, tot0, wx1, wy1, wz1, inv1, h2 = kernel_call(
        faces_kernel,
        [pad0, full0, full0, full0, full0, pad1, full1, full1, full1, (xb, yb, bz)],
        [(X + 2, YA, bz), pad1, (X1, Y, bz)],
        [k_wide, k_near, k_far],
        pl.CostEstimate(flops=0, bytes_accessed=8 << 20, transcendentals=0),
    )
    packed, g0, v0, v1, g1 = kernel_call(
        first_kernel,
        [(devices, 2 * yb, bz), (X, YA, bz), pad0, pad1, full1],
        [(X1, Y, bz), (xb, 8, bz)],
        [g_wide, g_near, g_far, wx0, wy0, wz0, inv0, wx1, wy1, wz1, inv1, h2],
    )
    got = everywhere(packed)
    level2 = (gx_count, gy_count * yb, bz)
    level3 = (gx_count, gy_count * yb // 2, bz)
    coarse_scratch = [
        level2, (gx_count + 2, gy_count + 2, yb, bz), (3, 16, bz), (3 * xb, 32, bz), pad1, (X1, by + 24, bz), pad0,
    ]
    packed, v0n, v1n, g1n, *levels = kernel_call(
        second_kernel,
        [(devices, yb, bz), pad0, pad1, full1] + [level2] * 4 + [level3] * 7,
        [level2, level2] + coarse_scratch + [pad0, (X1, Y, bz), (xb, 8, bz)],
        [got, g0, wx0, wy0, wz0, inv0, tot0, v0, wx1, wy1, wz1, inv1, v1, g1],
    )
    got = everywhere(packed)
    (out,) = kernel_call(
        third_kernel,
        [(bx, by, bz)],
        [level2] + coarse_scratch,
        [got, g0, wx0, wy0, wz0, inv0, v0n, wx1, wy1, wz1, inv1, v1n, g1n] + levels,
    )
    return out


def solution(mesh):
    return jax.shard_map(
        local,
        mesh=mesh,
        in_specs=(P("gx", "gy", None), P("gx", "gy", None), P()),
        out_specs=P("gx", "gy", None),
        check_vma=False,
    )
```

```python
import jax
import jax.numpy as jnp
from jax import lax
from jax.experimental import pallas as pl
from jax.experimental.pallas import tpu as pltpu
from jax.sharding import PartitionSpec as P

COARSE_SWEEPS = 6
OMEGA = 0.8
KEEP = 1.0 - OMEGA
HALO = 12
NEAR = 8
FAR = HALO - NEAR
BASE = 8
UNPACK = 8
F32 = jnp.float32


def near_partner(index, count):
    return index ^ 1 if index ^ 1 < count else index


def far_partner(index, count):
    return (index - 1 ^ 1) + 1


def route(axis, far):
    gx_count, gy_count = lax.axis_size("gx"), lax.axis_size("gy")
    pairs = []
    for x in range(gx_count):
        for y in range(gy_count):
            if axis == "gx":
                if not far:
                    a, b = near_partner(x, gx_count), y
                elif 0 < x < gx_count - 1:
                    a, b = far_partner(x, gx_count), y
                else:
                    a, b = x, near_partner(y, gy_count)
            else:
                if not far:
                    a, b = x, near_partner(y, gy_count)
                elif 0 < y < gy_count - 1:
                    a, b = x, far_partner(y, gy_count)
                else:
                    a, b = near_partner(x, gx_count), y
            pairs.append((x * gy_count + y, a * gy_count + b))
    return pairs


def trade(to_near, to_far, axis):
    from_far = lax.ppermute(to_far, ("gx", "gy"), route(axis, True))
    from_near = lax.ppermute(to_near, ("gx", "gy"), route(axis, False))
    return from_near, from_far


def everywhere(copies):
    return lax.all_to_all(copies, ("gx", "gy"), 0, 0)


def is_odd(axis):
    return lax.axis_index(axis) % 2 == 1


def has_below(axis):
    return lax.axis_index(axis) > 0


def has_above(axis):
    return lax.axis_index(axis) < lax.axis_size(axis) - 1


def below(near, far, axis):
    return jnp.where(has_below(axis), jnp.where(is_odd(axis), near, far), 0.0)


def above(near, far, axis):
    return jnp.where(has_above(axis), jnp.where(is_odd(axis), far, near), 0.0)


def roll(value, shift, axis):
    return pltpu.roll(value, shift % value.shape[axis], axis=axis)


def lanes_of(value):
    return lax.broadcasted_iota(jnp.int32, value.shape, value.ndim - 1)


def rows_of(value):
    return lax.broadcasted_iota(jnp.int32, value.shape, value.ndim - 2)


def lane_row(width):
    return lax.broadcasted_iota(jnp.int32, (1, width), 1)


def pick_lanes(value, index):
    flat = value.reshape(-1, value.shape[-1])
    index = jnp.broadcast_to(index, flat.shape)
    return jnp.take_along_axis(flat, index, axis=1).reshape(value.shape)


def add_partner(value, apart):
    return value + pick_lanes(value, lane_row(value.shape[-1]) ^ apart)


def shift_up(value):
    return jnp.concatenate([value[1:], jnp.zeros_like(value[:1])], axis=0)


def shift_down(value):
    return jnp.concatenate([jnp.zeros_like(value[:1]), value[:-1]], axis=0)


def next_x(value, step):
    turned = roll(value, -step, 2)
    return jnp.where(lanes_of(value) < value.shape[-1] - step, turned, shift_up(turned))


def prev_x(value, step):
    turned = roll(value, step, 2)
    return jnp.where(lanes_of(value) >= step, turned, shift_down(turned))


def whole_faces(h, span, xstep, zstep):
    in_span = lanes_of(h) % span
    row = rows_of(h)
    not_last_z, not_first_z = in_span < span - zstep, in_span >= zstep
    not_last_y, not_first_y = row < h.shape[1] - 1, row >= 1
    wx = h + next_x(h, xstep)
    wy = h + jnp.where(not_last_y, roll(h, -1, 1), 0.0)
    wz = h + jnp.where(not_last_z, roll(h, -zstep, 2), 0.0)
    back = h + prev_x(h, xstep)
    back = back + (h + jnp.where(not_first_y, roll(h, 1, 1), 0.0))
    back = back + (h + jnp.where(not_first_z, roll(h, zstep, 2), 0.0))
    total = wx + wy + wz + back
    return wx, jnp.where(not_last_y, wy, 0.0), jnp.where(not_last_z, wz, 0.0), OMEGA / total


def whole_spread(v, wx, wy, wz, xstep, zstep):
    return (
        (wx * next_x(v, xstep) + prev_x(wx * v, xstep))
        + (wy * roll(v, -1, 1) + roll(wy * v, 1, 1))
        + (wz * roll(v, -zstep, 2) + roll(wz * v, zstep, 2))
    )


def coarse_faces(h, span, xstep, zstep):
    wx, wy, wz, inverse = whole_faces(h, span, xstep, zstep)
    return wx, prev_x(wx, xstep), wy, roll(wy, 1, 1), wz, roll(wz, zstep, 2), inverse


def coarse_spread(v, wx, wx_back, wy, wy_back, wz, wz_back, zstep):
    turned = roll(v, v.shape[-1] // 2, 2)
    low = lanes_of(v) < v.shape[-1] // 2
    after = jnp.where(low, turned, shift_up(turned))
    before = jnp.where(low, shift_down(turned), turned)
    return (
        (wx * after + wx_back * before)
        + (wy * roll(v, -1, 1) + wy_back * roll(v, 1, 1))
        + (wz * roll(v, -zstep, 2) + wz_back * roll(v, zstep, 2))
    )


def read(array, start, size, top, rows, dx=0, dy=0):
    ref, planes_off, rows_off = array
    return ref[pl.ds(start + planes_off + dx, size), pl.ds(top + rows_off + dy, rows), :]


def write(array, start, top, value):
    ref, planes_off, rows_off = array
    ref[pl.ds(start + planes_off, value.shape[0]), pl.ds(top + rows_off, value.shape[1]), :] = value


def slabs(first, last, size, body):
    if first + size == last:
        body(first)
        return

    def step(i, carry):
        body(first + i * size)
        return carry

    lax.fori_loop(0, (last - first) // size, step, 0)


def faces(h, window, step):
    here = read(h, *window)
    lane = lanes_of(here)
    width = here.shape[-1]
    not_last = lane < width - step
    wx = here + read(h, *window, dx=1)
    wy = here + read(h, *window, dy=1)
    wz = here + jnp.where(not_last, roll(here, -step, 2), 0.0)
    back = (here + read(h, *window, dx=-1)) + (here + read(h, *window, dy=-1))
    back = back + (here + jnp.where(lane >= step, roll(here, step, 2), 0.0))
    total = (wx + wy + wz) + back
    inverse = jnp.where(here > 0.0, OMEGA / total, 0.0)
    return here, wx, wy, jnp.where(not_last, wz, 0.0), total, inverse


def spread(v, weights, window, step):
    wx, wy, wz = weights
    here = read(v, *window)
    wz = read(wz, *window)
    return here, (
        (read(wx, *window) * read(v, *window, dx=1) + read(wx, *window, dx=-1) * read(v, *window, dx=-1))
        + (read(wy, *window) * read(v, *window, dy=1) + read(wy, *window, dy=-1) * read(v, *window, dy=-1))
        + (wz * roll(here, -step, 2) + roll(wz * here, step, 2))
    )


def diamond(planes, rows, reach):
    groups = {}
    for distance in range(0, reach + 2, 2):
        rest = reach - max(distance - 1, 0)
        wide = -(-(rows - 2 * HALO + 2 * rest) // 8) * 8
        top = HALO - (wide - (rows - 2 * HALO)) // 2
        first, last = groups.get((top, wide), (distance, distance))
        groups[(top, wide)] = (first, distance)
    found = []
    for (top, wide), (first, last) in groups.items():
        if first == 0:
            found.append((HALO - last, planes - 2 * HALO + 2 * last, top, wide))
        else:
            size = last - first + 2
            found.append((HALO - last, size, top, wide))
            found.append((planes - HALO + first - 2, size, top, wide))
    return found


def halve_rows(value, buffer):
    count, rows, _ = value.shape
    buffer[0:count, 0:rows, :] = value
    return (
        buffer[0:count, pl.ds(0, rows // 2, stride=2), :] + buffer[0:count, pl.ds(1, rows // 2, stride=2), :]
    )


def halve_planes(value):
    pairs = value.reshape((value.shape[0] // 2, 2) + value.shape[1:])
    return pairs[:, 0] + pairs[:, 1]


def sum_blocks(value, buffer, step):
    return add_partner(halve_rows(halve_planes(value), buffer), step)


def double_rows(ref, start, value):
    count, rows, _ = value.shape
    ref[pl.ds(start, count), pl.ds(0, rows, stride=2), :] = value
    ref[pl.ds(start, count), pl.ds(1, rows, stride=2), :] = value


def double_planes(value):
    wide = jnp.broadcast_to(value[:, None], (value.shape[0], 2) + value.shape[1:])
    return wide.reshape((2 * value.shape[0],) + value.shape[1:])


def pack_block(values, buffer):
    blocks, rows, width = values[0].shape
    span = width // blocks
    for n, value in enumerate(values):
        buffer[:, n * rows : (n + 1) * rows, :] = value
    used = rows * len(values)
    lane = lane_row(width)
    first = (lane % span) * blocks
    packed = None
    for x in range(blocks):
        picked = (pick_lanes(buffer[x], first) + pick_lanes(buffer[x], first + blocks // 2))[:used]
        packed = picked if packed is None else jnp.where(lanes_of(picked) // span == x, picked, packed)
    return packed


def send_to_all(packed, chunk):
    copies = min(packed.shape[0], 32)

    def copy_out(i):
        packed[pl.ds(i, copies)] = jnp.broadcast_to(chunk[None], (copies,) + chunk.shape)

    slabs(0, packed.shape[0], copies, copy_out)


def sum_whole_blocks(value, buffer):
    halved = halve_rows(value, buffer)
    lane = lane_row(value.shape[-1])
    span = value.shape[-1] // 4
    return (halved + pick_lanes(halved, lane ^ 1)) + (
        pick_lanes(halved, lane ^ span) + pick_lanes(halved, lane ^ span ^ 1)
    )


def coarse_cycle(g2, level2, level3, buffer):
    wx2, wy2, wz2, inv2 = level2
    *w3, inv3 = level3
    span = g2.shape[-1] // 4
    v2 = inv2 * g2
    r2 = KEEP * g2 + whole_spread(v2, wx2, wy2, wz2, span, 1)
    g3 = 0.125 * sum_whole_blocks(r2, buffer)
    v3 = inv3 * g3
    for _ in range(COARSE_SWEEPS - 1):
        v3 = KEEP * v3 + inv3 * (g3 + coarse_spread(v3, *w3, 2))
    double_rows(buffer, 0, v3)
    u2 = v2 + buffer[...]
    return KEEP * u2 + inv2 * (g2 + whole_spread(u2, wx2, wy2, wz2, span, 1))


def spread_out(e2, wide, around, doubled, planes):
    count, rows, width = e2.shape
    blocks = lax.axis_size("gy")
    block = rows // blocks
    span = width // 4
    for edge in (0, count + 1):
        wide[edge] = jnp.zeros(wide.shape[1:], F32)
    for edge in (0, blocks + 1):
        wide[:, edge] = jnp.zeros((count + 2,) + wide.shape[2:], F32)
    for y in range(blocks):
        wide[1 : count + 1, y + 1] = e2[:, y * block : (y + 1) * block]
    gx, gy = lax.axis_index("gx"), lax.axis_index("gy")
    for x in range(3):
        for y in range(3):
            around[x, y * block : (y + 1) * block, :] = wide[gx + x, gy + y]
    lane = lane_row(width)
    kept = 3 * block
    for j in planes:
        value = pick_lanes(around[j // 4], (j % 4) * span + lane // 4)[:kept]
        doubled[j, pl.ds(0, kept, stride=2), :] = value
        doubled[j, pl.ds(1, kept, stride=2), :] = value


def row_starts(axis, block):
    odd = is_odd(axis)
    low = (0, 0, NEAR)
    high = (block - NEAR, block - FAR, block - HALO)
    to_near = [jnp.where(odd, a, b) for a, b in zip(low, high)]
    to_far = [jnp.where(odd, b, a) for a, b in zip(low, high)]
    return to_near, to_far


def diamond_strips(planes):
    full = (HALO - NEAR + 1, planes - HALO + NEAR - 1)
    far = HALO - FAR + 1
    half = planes // 2 - far
    return full, (1, full[1], full[0] - 1), (far, far + half, half)


def strip_tiles(strips):
    (first, last), (_, _, edge), (_, _, half) = strips
    return last - first + edge + half


def pack_rows(source, starts, strips, target):
    (first, last), *halves = strips
    at = last - first
    target[0:at] = source[first:last, pl.ds(starts[0], NEAR), :]
    for start, (one, two, count) in zip(starts[1:], halves):
        if count:
            target[at : at + count, 0:FAR, :] = source[one : one + count, pl.ds(start, FAR), :]
            target[at : at + count, FAR:NEAR, :] = source[two : two + count, pl.ds(start, FAR), :]
        at += count


def unpack_rows(target, planes_off, top, bottom, strips, near, far):
    (first, last), *halves = strips
    for choose, rows in ((below, (top - NEAR, top - FAR, top - HALO)), (above, (bottom, bottom, bottom + NEAR))):
        at = last - first
        target[planes_off + first : planes_off + last, rows[0] : rows[0] + NEAR, :] = choose(
            near[0:at], far[0:at], "gy"
        )
        for row, (one, two, count) in zip(rows[1:], halves):
            if count:
                both = choose(near[at : at + count], far[at : at + count], "gy")
                for plane, value in ((planes_off + one, both[:, 0:FAR]), (planes_off + two, both[:, FAR:NEAR])):
                    target[plane : plane + count, row : row + FAR, :] = value
            at += count


def own_kernel(cond, material, right_in, near, table, h, h_near, right):
    table[...] = jnp.zeros(table.shape, F32)
    table[0:1, 0 : cond.shape[1]] = 0.5 * cond[...]
    h[...] = look_up(material[...], table)
    first = jnp.where(is_odd("gx"), near.shape[0] - HALO, 0)
    h_near[...] = look_up(near[pl.ds(first, HALO)], table)
    right[...] = right_in[...]


def look_up(ids, table):
    planes, rows, width = ids.shape
    ids = ids.reshape(planes * rows, width)
    values = jnp.broadcast_to(table[0:1, :], ids.shape)
    return jnp.take_along_axis(values, ids, axis=1).reshape(planes, rows, width)


def k_kernel(h, h_near, far, table, wide, k_near, k_far):
    block = h.shape[0]
    first = jnp.where(is_odd("gx"), 0, block - HALO)
    h_far = look_up(far[pl.ds(first, HALO)], table)
    wide[0:HALO] = below(h_near[...], h_far, "gx")
    wide[HALO : HALO + block] = h[...]
    wide[HALO + block :] = above(h_near[...], h_far, "gx")
    strips = diamond_strips(wide.shape[0])
    to_near, to_far = row_starts("gy", wide.shape[1])
    pack_rows(wide, to_near, strips, k_near)
    pack_rows(wide, to_far, strips, k_far)


def plane_strips(rows):
    strips, at = [], 0
    for distance in range(1, HALO):
        cut = HALO - -(-(HALO - 1 - distance) // 4) * 4
        tiles = (rows - 2 * cut) // 8
        strips.append((distance, cut, tiles, at))
        at += tiles
    return strips, at


def g_kernel(right, near, far, wide, g_near, g_far):
    block, rows, _ = right.shape
    top = BASE // 2
    wide[:, top + HALO : top + HALO + rows, :] = right[...]
    wide[:, top : top + HALO, :] = below(near[:, rows - HALO :], far[:, rows - HALO :], "gy")
    wide[:, top + HALO + rows : top + 2 * HALO + rows, :] = above(near[:, :HALO], far[:, :HALO], "gy")
    odd = is_odd("gx")
    strips, _ = plane_strips(rows + 2 * HALO)
    for distance, cut, tiles, at in strips:
        low, high = distance - 1, block - distance
        for target, plane in ((g_near, jnp.where(odd, low, high)), (g_far, jnp.where(odd, high, low))):
            for tile in range(tiles):
                target[at + tile] = wide[plane, top + cut + 8 * tile : top + cut + 8 * tile + 8, :]


def faces_kernel(
    k_wide, k_near, k_far,
    wx0, wy0, wz0, inv0, tot0, wx1, wy1, wz1, inv1, h2,
    h0, h1, buf0,
):
    top = BASE // 2
    planes, rows, _ = k_wide.shape
    h0[1 : planes + 1, top + HALO : top + HALO + rows, :] = k_wide[...]
    unpack_rows(h0, 1, top + HALO, top + HALO + rows, diamond_strips(planes), k_near, k_far)
    rows = rows + 2 * HALO

    aH0, aWX0, aH1, aWX1 = (h0, 1, top), (wx0, 1, BASE), (h1, 1, BASE), (wx1, 1, BASE)
    for window in diamond(planes, rows, HALO - 1):
        start, _, above_rows, _ = window
        _, wx, wy, wz, total, inverse = faces(aH0, window, 1)
        write(aWX0, start, above_rows, wx)
        for ref, value in ((wy0, wy), (wz0, wz), (tot0, total), (inv0, inverse)):
            write((ref, 0, BASE), start, above_rows, value)
    write(aH1, 0, 0, sum_blocks(read(aH0, 0, planes, 0, rows), buf0, 1) * (1.0 / 32.0))

    planes1, rows1 = planes // 2, -(-rows // 16) * 8
    _, wx, wy, wz, _, inverse = faces(aH1, (0, planes1, 0, rows1), 2)
    write(aWX1, 0, 0, wx)
    for ref, value in ((wy1, wy), (wz1, wz), (inv1, inverse)):
        write((ref, 0, BASE), 0, 0, value)
    low = HALO // 2
    own = read(aH1, low, planes1 - HALO, low, rows // 2 - HALO)
    h2[...] = halve_rows(halve_planes(own), buf0) * (1.0 / 32.0)


def first_kernel(
    g_wide, g_near, g_far, wx0, wy0, wz0, inv0, wx1, wy1, wz1, inv1, h2,
    packed, g0, v0, v1, g1,
    buf0, bufp,
):
    top = BASE // 2
    planes, _, width = g0.shape
    block, rows = g_wide.shape[0], g_wide.shape[1] - BASE
    g0[HALO : HALO + block] = g_wide[...]
    strips, _ = plane_strips(rows)
    for distance, cut, tiles, at in strips:
        for choose, plane in ((below, HALO - distance), (above, planes - HALO - 1 + distance)):
            value = choose(g_near[at : at + tiles], g_far[at : at + tiles], "gx")
            g0[plane, top + cut : top + cut + 8 * tiles, :] = value.reshape(8 * tiles, width)

    aG0, aV0, aV1, aG1 = (g0, 0, top), (v0, 1, BASE), (v1, 1, BASE), (g1, 0, BASE)
    w0 = (wx0, 1, BASE), (wy0, 0, BASE), (wz0, 0, BASE)
    w1 = (wx1, 1, BASE), (wy1, 0, BASE), (wz1, 0, BASE)
    for window in diamond(planes, rows, HALO - 1):
        write(aV0, window[0], window[2], read((inv0, 0, BASE), *window) * read(aG0, *window))
    for window in diamond(planes, rows, HALO - 2):
        start, _, above_rows, _ = window
        _, around = spread(aV0, w0, window, 1)
        r = KEEP * read(aG0, *window) + around
        write(aG1, start // 2, above_rows // 2, sum_blocks(r, buf0.at[start // 2 :], 1) * 0.125)

    planes1, rows1 = planes // 2, -(-rows // 16) * 8
    window = (0, planes1, 0, rows1)
    write(aV1, 0, 0, read((inv1, 0, BASE), *window) * read(aG1, *window))
    low = HALO // 2
    window = (low, planes1 - HALO, low, rows // 2 - HALO)
    _, around = spread(aV1, w1, window, 2)
    g2 = halve_rows(halve_planes(KEEP * read(aG1, *window) + around), buf0) * 0.125
    send_to_all(packed, pack_block([g2, h2[...]], bufp))


def second_kernel(
    got, g0, wx0, wy0, wz0, inv0, tot0, v0, wx1, wy1, wz1, inv1, v1, g1,
    packed, v0n, v1n, g1n, *rest,
):
    levels, (g2, h2, buf2, wide, around, doubled, u1, e0, u0, v0m, buf0, bufp) = rest[:11], rest[11:]
    count, rows2, width = g2.shape
    gy_count = lax.axis_size("gy")
    block2 = rows2 // gy_count

    def unpack(i):
        for x in range(UNPACK):
            for y in range(gy_count):
                both = got[(i + x) * gy_count + y]
                g2[i + x, y * block2 : (y + 1) * block2, :] = both[:block2]
                h2[i + x, y * block2 : (y + 1) * block2, :] = both[block2:]

    slabs(0, count, UNPACK, unpack)

    span = width // 4
    h = h2[...]
    level2 = whole_faces(h, span, span, 1)
    h3 = sum_whole_blocks(h, buf2) * (1.0 / 32.0)
    level3 = coarse_faces(h3, span, 2 * span, 2)
    for ref, value in zip(levels, level2 + level3):
        ref[...] = value
    spread_out(coarse_cycle(g2[...], level2, level3, buf2), wide, around, doubled, range(1, 11))

    top = BASE // 2
    planes = g0.shape[0]
    block = planes - 2 * HALO
    aG0 = (g0, 0, top)
    w0 = (wx0, 1, BASE), (wy0, 0, BASE), (wz0, 0, BASE)
    aINV0, aTOT0, aV0 = (inv0, 0, BASE), (tot0, 0, BASE), (v0, 1, BASE)
    w1 = (wx1, 1, BASE), (wy1, 0, BASE), (wz1, 0, BASE)
    aINV1, aG1, aV1 = (inv1, 0, BASE), (g1, 0, BASE), (v1, 1, BASE)

    low, block1 = HALO // 2, block // 2
    aU1 = (u1, 1, BASE)
    window = (0, planes // 2, 0, planes // 4 // 8 * 8 + 16)
    e1 = doubled[1 : 1 + planes // 4, 2 : 2 + window[3], :]
    write(aU1, 0, 0, read(aV1, *window) + double_planes(e1))
    window = (low - 4, block1 + 8, low - 4, block1 + 8)
    here, around = spread(aU1, w1, window, 2)
    swept = KEEP * here + read(aINV1, *window) * (read(aG1, *window) + around)
    double_rows(e0, low - 4, swept)

    rows = block + 16
    aU0 = (u0, 1, BASE - (HALO - 7))
    aE0 = (e0, 0, -(2 * low - 8))
    aV0M = (v0m, 1, BASE - (HALO - 6))
    aV0N = (v0n, 1, BASE - (HALO - 5))
    size = block + 16

    def correct(i):
        window = (i, size, HALO - 7, rows)
        e = double_planes(read(aE0, i // 2, size // 2, HALO - 7, rows))
        write(aU0, i, HALO - 7, read(aV0, *window) + e)

    slabs(HALO - 8, planes - HALO + 8, size, correct)

    def sweep(source, target, margin, size):
        def body(i):
            window = (i, size, HALO - margin, rows)
            here, around = spread(source, w0, window, 1)
            value = KEEP * here + read(aINV0, *window) * (read(aG0, *window) + around)
            write(target, i, HALO - margin, value)

        slabs(HALO - margin, planes - HALO + margin, size, body)

    sweep(aU0, aV0M, 6, block + 12)
    sweep(aV0M, aV0N, 5, block + 10)

    aG1N, aV1N = (g1n, 0, BASE - (low - 2)), (v1n, 1, BASE - (low - 2))
    window = (HALO - 4, block + 8, HALO - 4, block + 8)
    here, around = spread(aV0N, w0, window, 1)
    r = (read(aG0, *window) - read(aTOT0, *window) * here) + around
    write(aG1N, low - 2, low - 2, sum_blocks(r, buf0, 1) * 0.125)

    window = (low - 2, block1 + 4, low - 2, block1 + 4)
    write(aV1N, low - 2, low - 2, read(aINV1, *window) * read(aG1N, *window))
    window = (low, block1, low, block1)
    _, around = spread(aV1N, w1, window, 2)
    g2 = halve_rows(halve_planes(KEEP * read(aG1N, *window) + around), buf0) * 0.125
    send_to_all(packed, pack_block([g2], bufp))


def third_kernel(
    got, g0, wx0, wy0, wz0, inv0, v0n, wx1, wy1, wz1, inv1, v1n, g1n, *rest,
):
    levels, (out, g2, buf2, wide, around, doubled, u1, e0, u0) = rest[:11], rest[11:]
    count, rows2, width = g2.shape
    gy_count = lax.axis_size("gy")
    block2 = rows2 // gy_count

    def unpack(i):
        for x in range(UNPACK):
            for y in range(gy_count):
                g2[i + x, y * block2 : (y + 1) * block2, :] = got[(i + x) * gy_count + y]

    slabs(0, count, UNPACK, unpack)
    values = [ref[...] for ref in levels]
    spread_out(coarse_cycle(g2[...], values[:4], values[4:], buf2), wide, around, doubled, range(3, 9))

    top = BASE // 2
    planes = g0.shape[0]
    block = planes - 2 * HALO
    aG0, aINV0 = (g0, 0, top), (inv0, 0, BASE)
    w0 = (wx0, 1, BASE), (wy0, 0, BASE), (wz0, 0, BASE)
    w1 = (wx1, 1, BASE), (wy1, 0, BASE), (wz1, 0, BASE)
    low, block1 = HALO // 2, block // 2
    aINV1 = (inv1, 0, BASE)
    aG1N, aV1N = (g1n, 0, BASE - (low - 2)), (v1n, 1, BASE - (low - 2))
    aV0N = (v0n, 1, BASE - (HALO - 5))

    aU1 = (u1, 1, BASE - (low - 2))
    window = (low - 2, block1 + 4, low - 2, block1 + 4)
    e1 = doubled[low // 2 : low // 2 + block1 // 2 + 2, low : low + block1 + 4, :]
    write(aU1, low - 2, low - 2, read(aV1N, *window) + double_planes(e1))
    window = (low - 1, block1 + 2, low - 1, block1 + 2)
    here, around = spread(aU1, w1, window, 2)
    swept = KEEP * here + read(aINV1, *window) * (read(aG1N, *window) + around)
    double_rows(e0, low - 1, swept)

    aU0 = (u0, 1, BASE - (HALO - 1))
    aE0 = (e0, 0, -(2 * low - 2))
    size = block + 4
    rows = block + 2

    def correct(i):
        window = (i, size, HALO - 1, rows)
        e = double_planes(read(aE0, i // 2, size // 2, HALO - 1, rows))
        write(aU0, i, HALO - 1, read(aV0N, *window) + e)

    slabs(HALO - 2, planes - HALO + 2, size, correct)

    def sweep(i):
        window = (i, size, HALO, block)
        here, around = spread(aU0, w0, window, 1)
        out[pl.ds(i - HALO, size)] = KEEP * here + read(aINV0, *window) * (read(aG0, *window) + around)

    size = block
    slabs(HALO, planes - HALO, size, sweep)


def kernel_call(body, outs, scratch, args):
    def size(shape):
        total = 4
        for length in shape:
            total *= length
        return total

    shapes = [a.shape for a in args] + list(outs) + list(scratch)
    limit = sum(size(s) for s in shapes) + (8 << 20)
    return pl.pallas_call(
        body,
        out_shape=[jax.ShapeDtypeStruct(s, F32) for s in outs],
        in_specs=[pl.BlockSpec(memory_space=pltpu.VMEM)] * len(args),
        out_specs=[pl.BlockSpec(memory_space=pltpu.VMEM)] * len(outs),
        scratch_shapes=[pltpu.VMEM(s, F32) for s in scratch],
        compiler_params=pltpu.CompilerParams(vmem_limit_bytes=limit),
    )(*args)


def local(right_side, material, conductivity):
    bx, by, bz = right_side.shape
    gx_count, gy_count = lax.axis_size("gx"), lax.axis_size("gy")
    devices = gx_count * gy_count

    X, Y = bx + 2 * HALO, by + 2 * HALO
    YA = Y + BASE
    YB = Y + 2 * BASE
    X1, Y1 = X // 2, -(-Y // 16) * 8 + 2 * BASE
    xb, yb = bx // 4, by // 4

    k_near, k_far = trade(material, material, "gx")
    g_near, g_far = trade(right_side, right_side, "gy")
    table, h, h_near, right = kernel_call(
        own_kernel,
        [(8, bz), (bx, by, bz), (HALO, by, bz), (bx, by, bz)],
        [],
        [conductivity[None], material, right_side, k_near],
    )
    strip = (plane_strips(Y)[1], 8, bz)
    g_wide, g_near, g_far = kernel_call(
        g_kernel, [(bx, YA, bz), strip, strip], [], [right, g_near, g_far]
    )
    strip = (strip_tiles(diamond_strips(X)), NEAR, bz)
    k_wide, k_near, k_far = kernel_call(
        k_kernel, [(X, by, bz), strip, strip], [], [h, h_near, k_far, table]
    )
    g_near, g_far = trade(g_near, g_far, "gx")
    k_near, k_far = trade(k_near, k_far, "gy")

    pad0, full0, pad1, full1 = (X + 2, YB, bz), (X, YB, bz), (X1 + 2, Y1, bz), (X1, Y1, bz)
    wx0, wy0, wz0, inv0, tot0, wx1, wy1, wz1, inv1, h2 = kernel_call(
        faces_kernel,
        [pad0, full0, full0, full0, full0, pad1, full1, full1, full1, (xb, yb, bz)],
        [(X + 2, YA, bz), pad1, (X1, Y, bz)],
        [k_wide, k_near, k_far],
    )
    packed, g0, v0, v1, g1 = kernel_call(
        first_kernel,
        [(devices, 2 * yb, bz), (X, YA, bz), pad0, pad1, full1],
        [(X1, Y, bz), (xb, 8, bz)],
        [g_wide, g_near, g_far, wx0, wy0, wz0, inv0, wx1, wy1, wz1, inv1, h2],
    )
    got = everywhere(packed)
    level2 = (gx_count, gy_count * yb, bz)
    level3 = (gx_count, gy_count * yb // 2, bz)
    coarse_scratch = [
        level2, (gx_count + 2, gy_count + 2, yb, bz), (3, 16, bz), (3 * xb, 32, bz), pad1, (X1, by + 24, bz), pad0,
    ]
    packed, v0n, v1n, g1n, *levels = kernel_call(
        second_kernel,
        [(devices, yb, bz), pad0, pad1, full1] + [level2] * 4 + [level3] * 7,
        [level2, level2] + coarse_scratch + [pad0, (X1, Y, bz), (xb, 8, bz)],
        [got, g0, wx0, wy0, wz0, inv0, tot0, v0, wx1, wy1, wz1, inv1, v1, g1],
    )
    got = everywhere(packed)
    (out,) = kernel_call(
        third_kernel,
        [(bx, by, bz)],
        [level2] + coarse_scratch,
        [got, g0, wx0, wy0, wz0, inv0, v0n, wx1, wy1, wz1, inv1, v1n, g1n] + levels,
    )
    return out


def solution(mesh):
    return jax.shard_map(
        local,
        mesh=mesh,
        in_specs=(P("gx", "gy", None), P("gx", "gy", None), P()),
        out_specs=P("gx", "gy", None),
        check_vma=False,
    )
```

```python
import jax
import jax.numpy as jnp
from jax import lax
from jax.experimental import pallas as pl
from jax.experimental.pallas import tpu as pltpu
from jax.sharding import PartitionSpec as P

COARSE_SWEEPS = 6
OMEGA = 0.8
KEEP = 1.0 - OMEGA
HALO = 12
NEAR = 8
FAR = HALO - NEAR
BASE = 8
UNPACK = 8
F32 = jnp.float32


def near_partner(index, count):
    return index ^ 1 if index ^ 1 < count else index


def far_partner(index, count):
    return (index - 1 ^ 1) + 1


def route(axis, far):
    gx_count, gy_count = lax.axis_size("gx"), lax.axis_size("gy")
    pairs = []
    for x in range(gx_count):
        for y in range(gy_count):
            if axis == "gx":
                if not far:
                    a, b = near_partner(x, gx_count), y
                elif 0 < x < gx_count - 1:
                    a, b = far_partner(x, gx_count), y
                else:
                    a, b = x, near_partner(y, gy_count)
            else:
                if not far:
                    a, b = x, near_partner(y, gy_count)
                elif 0 < y < gy_count - 1:
                    a, b = x, far_partner(y, gy_count)
                else:
                    a, b = near_partner(x, gx_count), y
            pairs.append((x * gy_count + y, a * gy_count + b))
    return pairs


def trade(to_near, to_far, axis):
    from_far = lax.ppermute(to_far, ("gx", "gy"), route(axis, True))
    from_near = lax.ppermute(to_near, ("gx", "gy"), route(axis, False))
    return from_near, from_far


def everywhere(copies):
    return lax.all_to_all(copies, ("gy", "gx"), 0, 0)


def is_odd(axis):
    return lax.axis_index(axis) % 2 == 1


def has_below(axis):
    return lax.axis_index(axis) > 0


def has_above(axis):
    return lax.axis_index(axis) < lax.axis_size(axis) - 1


def below(near, far, axis):
    return jnp.where(has_below(axis), jnp.where(is_odd(axis), near, far), 0.0)


def above(near, far, axis):
    return jnp.where(has_above(axis), jnp.where(is_odd(axis), far, near), 0.0)


def roll(value, shift, axis):
    return pltpu.roll(value, shift % value.shape[axis], axis=axis)


def lanes_of(value):
    return lax.broadcasted_iota(jnp.int32, value.shape, value.ndim - 1)


def rows_of(value):
    return lax.broadcasted_iota(jnp.int32, value.shape, value.ndim - 2)


def lane_row(width):
    return lax.broadcasted_iota(jnp.int32, (1, width), 1)


def pick_lanes(value, index):
    flat = value.reshape(-1, value.shape[-1])
    index = jnp.broadcast_to(index, flat.shape)
    return jnp.take_along_axis(flat, index, axis=1).reshape(value.shape)


def add_partner(value, apart):
    return value + pick_lanes(value, lane_row(value.shape[-1]) ^ apart)


def shift_up(value):
    return jnp.concatenate([value[1:], jnp.zeros_like(value[:1])], axis=0)


def shift_down(value):
    return jnp.concatenate([jnp.zeros_like(value[:1]), value[:-1]], axis=0)


def next_x(value, step):
    turned = roll(value, -step, 2)
    return jnp.where(lanes_of(value) < value.shape[-1] - step, turned, shift_up(turned))


def prev_x(value, step):
    turned = roll(value, step, 2)
    return jnp.where(lanes_of(value) >= step, turned, shift_down(turned))


def whole_faces(h, span, xstep, zstep):
    in_span = lanes_of(h) % span
    row = rows_of(h)
    not_last_z, not_first_z = in_span < span - zstep, in_span >= zstep
    not_last_y, not_first_y = row < h.shape[1] - 1, row >= 1
    wx = h + next_x(h, xstep)
    wy = h + jnp.where(not_last_y, roll(h, -1, 1), 0.0)
    wz = h + jnp.where(not_last_z, roll(h, -zstep, 2), 0.0)
    back = h + prev_x(h, xstep)
    back = back + (h + jnp.where(not_first_y, roll(h, 1, 1), 0.0))
    back = back + (h + jnp.where(not_first_z, roll(h, zstep, 2), 0.0))
    total = wx + wy + wz + back
    return wx, jnp.where(not_last_y, wy, 0.0), jnp.where(not_last_z, wz, 0.0), OMEGA / total


def whole_spread(v, wx, wy, wz, xstep, zstep):
    return (
        (wx * next_x(v, xstep) + prev_x(wx * v, xstep))
        + (wy * roll(v, -1, 1) + roll(wy * v, 1, 1))
        + (wz * roll(v, -zstep, 2) + roll(wz * v, zstep, 2))
    )


def coarse_faces(h, span, xstep, zstep):
    wx, wy, wz, inverse = whole_faces(h, span, xstep, zstep)
    return wx, prev_x(wx, xstep), wy, roll(wy, 1, 1), wz, roll(wz, zstep, 2), inverse


def coarse_spread(v, wx, wx_back, wy, wy_back, wz, wz_back, zstep):
    turned = roll(v, v.shape[-1] // 2, 2)
    low = lanes_of(v) < v.shape[-1] // 2
    after = jnp.where(low, turned, shift_up(turned))
    before = jnp.where(low, shift_down(turned), turned)
    return (
        (wx * after + wx_back * before)
        + (wy * roll(v, -1, 1) + wy_back * roll(v, 1, 1))
        + (wz * roll(v, -zstep, 2) + wz_back * roll(v, zstep, 2))
    )


def read(array, start, size, top, rows, dx=0, dy=0):
    ref, planes_off, rows_off = array
    return ref[pl.ds(start + planes_off + dx, size), pl.ds(top + rows_off + dy, rows), :]


def write(array, start, top, value):
    ref, planes_off, rows_off = array
    ref[pl.ds(start + planes_off, value.shape[0]), pl.ds(top + rows_off, value.shape[1]), :] = value


def slabs(first, last, size, body):
    if first + size == last:
        body(first)
        return

    def step(i, carry):
        body(first + i * size)
        return carry

    lax.fori_loop(0, (last - first) // size, step, 0)


def faces(h, window, step):
    here = read(h, *window)
    lane = lanes_of(here)
    width = here.shape[-1]
    not_last = lane < width - step
    wx = here + read(h, *window, dx=1)
    wy = here + read(h, *window, dy=1)
    wz = here + jnp.where(not_last, roll(here, -step, 2), 0.0)
    back = (here + read(h, *window, dx=-1)) + (here + read(h, *window, dy=-1))
    back = back + (here + jnp.where(lane >= step, roll(here, step, 2), 0.0))
    total = (wx + wy + wz) + back
    inverse = jnp.where(here > 0.0, OMEGA / total, 0.0)
    return here, wx, wy, jnp.where(not_last, wz, 0.0), total, inverse


def spread(v, weights, window, step):
    wx, wy, wz = weights
    here = read(v, *window)
    wz = read(wz, *window)
    return here, (
        (read(wx, *window) * read(v, *window, dx=1) + read(wx, *window, dx=-1) * read(v, *window, dx=-1))
        + (read(wy, *window) * read(v, *window, dy=1) + read(wy, *window, dy=-1) * read(v, *window, dy=-1))
        + (wz * roll(here, -step, 2) + roll(wz * here, step, 2))
    )


def diamond(planes, rows, reach):
    groups = {}
    for distance in range(0, reach + 2, 2):
        rest = reach - max(distance - 1, 0)
        wide = -(-(rows - 2 * HALO + 2 * rest) // 8) * 8
        top = HALO - (wide - (rows - 2 * HALO)) // 2
        first, last = groups.get((top, wide), (distance, distance))
        groups[(top, wide)] = (first, distance)
    found = []
    for (top, wide), (first, last) in groups.items():
        if first == 0:
            found.append((HALO - last, planes - 2 * HALO + 2 * last, top, wide))
        else:
            size = last - first + 2
            found.append((HALO - last, size, top, wide))
            found.append((planes - HALO + first - 2, size, top, wide))
    return found


def halve_rows(value, buffer):
    count, rows, _ = value.shape
    buffer[0:count, 0:rows, :] = value
    return (
        buffer[0:count, pl.ds(0, rows // 2, stride=2), :] + buffer[0:count, pl.ds(1, rows // 2, stride=2), :]
    )


def halve_planes(value):
    pairs = value.reshape((value.shape[0] // 2, 2) + value.shape[1:])
    return pairs[:, 0] + pairs[:, 1]


def sum_blocks(value, buffer, step):
    return add_partner(halve_rows(halve_planes(value), buffer), step)


def double_rows(ref, start, value):
    count, rows, _ = value.shape
    ref[pl.ds(start, count), pl.ds(0, rows, stride=2), :] = value
    ref[pl.ds(start, count), pl.ds(1, rows, stride=2), :] = value


def double_planes(value):
    wide = jnp.broadcast_to(value[:, None], (value.shape[0], 2) + value.shape[1:])
    return wide.reshape((2 * value.shape[0],) + value.shape[1:])


def pack_block(values, buffer):
    blocks, rows, width = values[0].shape
    span = width // blocks
    for n, value in enumerate(values):
        buffer[:, n * rows : (n + 1) * rows, :] = value
    used = rows * len(values)
    lane = lane_row(width)
    first = (lane % span) * blocks
    packed = None
    for x in range(blocks):
        picked = (pick_lanes(buffer[x], first) + pick_lanes(buffer[x], first + blocks // 2))[:used]
        packed = picked if packed is None else jnp.where(lanes_of(picked) // span == x, picked, packed)
    return packed


def send_to_all(packed, chunk):
    copies = min(packed.shape[0], 32)

    def copy_out(i):
        packed[pl.ds(i, copies)] = jnp.broadcast_to(chunk[None], (copies,) + chunk.shape)

    slabs(0, packed.shape[0], copies, copy_out)


def sum_whole_blocks(value, buffer):
    halved = halve_rows(value, buffer)
    lane = lane_row(value.shape[-1])
    span = value.shape[-1] // 4
    return (halved + pick_lanes(halved, lane ^ 1)) + (
        pick_lanes(halved, lane ^ span) + pick_lanes(halved, lane ^ span ^ 1)
    )


def coarse_cycle(g2, level2, level3, buffer):
    wx2, wy2, wz2, inv2 = level2
    *w3, inv3 = level3
    span = g2.shape[-1] // 4
    v2 = inv2 * g2
    r2 = KEEP * g2 + whole_spread(v2, wx2, wy2, wz2, span, 1)
    g3 = 0.125 * sum_whole_blocks(r2, buffer)
    v3 = inv3 * g3
    for _ in range(COARSE_SWEEPS - 1):
        v3 = KEEP * v3 + inv3 * (g3 + coarse_spread(v3, *w3, 2))
    double_rows(buffer, 0, v3)
    u2 = v2 + buffer[...]
    return KEEP * u2 + inv2 * (g2 + whole_spread(u2, wx2, wy2, wz2, span, 1))


def spread_out(e2, wide, around, doubled, planes):
    count, rows, width = e2.shape
    blocks = lax.axis_size("gy")
    block = rows // blocks
    span = width // 4
    for edge in (0, count + 1):
        wide[edge] = jnp.zeros(wide.shape[1:], F32)
    for edge in (0, blocks + 1):
        wide[:, edge] = jnp.zeros((count + 2,) + wide.shape[2:], F32)
    for y in range(blocks):
        wide[1 : count + 1, y + 1] = e2[:, y * block : (y + 1) * block]
    gx, gy = lax.axis_index("gx"), lax.axis_index("gy")
    for x in range(3):
        for y in range(3):
            around[x, y * block : (y + 1) * block, :] = wide[gx + x, gy + y]
    lane = lane_row(width)
    kept = 3 * block
    for j in planes:
        value = pick_lanes(around[j // 4], (j % 4) * span + lane // 4)[:kept]
        doubled[j, pl.ds(0, kept, stride=2), :] = value
        doubled[j, pl.ds(1, kept, stride=2), :] = value


def row_starts(axis, block):
    odd = is_odd(axis)
    low = (0, 0, NEAR)
    high = (block - NEAR, block - FAR, block - HALO)
    to_near = [jnp.where(odd, a, b) for a, b in zip(low, high)]
    to_far = [jnp.where(odd, b, a) for a, b in zip(low, high)]
    return to_near, to_far


def diamond_strips(planes):
    full = (HALO - NEAR + 1, planes - HALO + NEAR - 1)
    far = HALO - FAR + 1
    half = planes // 2 - far
    return full, (1, full[1], full[0] - 1), (far, far + half, half)


def strip_tiles(strips):
    (first, last), (_, _, edge), (_, _, half) = strips
    return last - first + edge + half


def pack_rows(source, starts, strips, target):
    (first, last), *halves = strips
    at = last - first
    target[0:at] = source[first:last, pl.ds(starts[0], NEAR), :]
    for start, (one, two, count) in zip(starts[1:], halves):
        if count:
            target[at : at + count, 0:FAR, :] = source[one : one + count, pl.ds(start, FAR), :]
            target[at : at + count, FAR:NEAR, :] = source[two : two + count, pl.ds(start, FAR), :]
        at += count


def unpack_rows(target, planes_off, top, bottom, strips, near, far):
    (first, last), *halves = strips
    for choose, rows in ((below, (top - NEAR, top - FAR, top - HALO)), (above, (bottom, bottom, bottom + NEAR))):
        at = last - first
        target[planes_off + first : planes_off + last, rows[0] : rows[0] + NEAR, :] = choose(
            near[0:at], far[0:at], "gy"
        )
        for row, (one, two, count) in zip(rows[1:], halves):
            if count:
                both = choose(near[at : at + count], far[at : at + count], "gy")
                for plane, value in ((planes_off + one, both[:, 0:FAR]), (planes_off + two, both[:, FAR:NEAR])):
                    target[plane : plane + count, row : row + FAR, :] = value
            at += count


def own_kernel(cond, material, right_in, near, table, h, h_near, right):
    table[...] = jnp.zeros(table.shape, F32)
    table[0:1, 0 : cond.shape[1]] = 0.5 * cond[...]
    h[...] = look_up(material[...], table)
    first = jnp.where(is_odd("gx"), near.shape[0] - HALO, 0)
    h_near[...] = look_up(near[pl.ds(first, HALO)], table)
    right[...] = right_in[...]


def look_up(ids, table):
    planes, rows, width = ids.shape
    ids = ids.reshape(planes * rows, width)
    values = jnp.broadcast_to(table[0:1, :], ids.shape)
    return jnp.take_along_axis(values, ids, axis=1).reshape(planes, rows, width)


def k_kernel(h, h_near, far, table, wide, k_near, k_far):
    block = h.shape[0]
    first = jnp.where(is_odd("gx"), 0, block - HALO)
    h_far = look_up(far[pl.ds(first, HALO)], table)
    wide[0:HALO] = below(h_near[...], h_far, "gx")
    wide[HALO : HALO + block] = h[...]
    wide[HALO + block :] = above(h_near[...], h_far, "gx")
    strips = diamond_strips(wide.shape[0])
    to_near, to_far = row_starts("gy", wide.shape[1])
    pack_rows(wide, to_near, strips, k_near)
    pack_rows(wide, to_far, strips, k_far)


def plane_strips(rows):
    strips, at = [], 0
    for distance in range(1, HALO):
        cut = HALO - -(-(HALO - 1 - distance) // 4) * 4
        tiles = (rows - 2 * cut) // 8
        strips.append((distance, cut, tiles, at))
        at += tiles
    return strips, at


def g_kernel(right, near, far, wide, g_near, g_far):
    block, rows, _ = right.shape
    top = BASE // 2
    wide[:, top + HALO : top + HALO + rows, :] = right[...]
    wide[:, top : top + HALO, :] = below(near[:, rows - HALO :], far[:, rows - HALO :], "gy")
    wide[:, top + HALO + rows : top + 2 * HALO + rows, :] = above(near[:, :HALO], far[:, :HALO], "gy")
    odd = is_odd("gx")
    strips, _ = plane_strips(rows + 2 * HALO)
    for distance, cut, tiles, at in strips:
        low, high = distance - 1, block - distance
        for target, plane in ((g_near, jnp.where(odd, low, high)), (g_far, jnp.where(odd, high, low))):
            for tile in range(tiles):
                target[at + tile] = wide[plane, top + cut + 8 * tile : top + cut + 8 * tile + 8, :]


def faces_kernel(
    k_wide, k_near, k_far,
    wx0, wy0, wz0, inv0, tot0, wx1, wy1, wz1, inv1, h2,
    h0, h1, buf0,
):
    top = BASE // 2
    planes, rows, _ = k_wide.shape
    h0[1 : planes + 1, top + HALO : top + HALO + rows, :] = k_wide[...]
    unpack_rows(h0, 1, top + HALO, top + HALO + rows, diamond_strips(planes), k_near, k_far)
    rows = rows + 2 * HALO

    aH0, aWX0, aH1, aWX1 = (h0, 1, top), (wx0, 1, BASE), (h1, 1, BASE), (wx1, 1, BASE)
    for window in diamond(planes, rows, HALO - 1):
        start, _, above_rows, _ = window
        _, wx, wy, wz, total, inverse = faces(aH0, window, 1)
        write(aWX0, start, above_rows, wx)
        for ref, value in ((wy0, wy), (wz0, wz), (tot0, total), (inv0, inverse)):
            write((ref, 0, BASE), start, above_rows, value)
    write(aH1, 0, 0, sum_blocks(read(aH0, 0, planes, 0, rows), buf0, 1) * (1.0 / 32.0))

    planes1, rows1 = planes // 2, -(-rows // 16) * 8
    _, wx, wy, wz, _, inverse = faces(aH1, (0, planes1, 0, rows1), 2)
    write(aWX1, 0, 0, wx)
    for ref, value in ((wy1, wy), (wz1, wz), (inv1, inverse)):
        write((ref, 0, BASE), 0, 0, value)
    low = HALO // 2
    own = read(aH1, low, planes1 - HALO, low, rows // 2 - HALO)
    h2[...] = halve_rows(halve_planes(own), buf0) * (1.0 / 32.0)


def first_kernel(
    g_wide, g_near, g_far, wx0, wy0, wz0, inv0, wx1, wy1, wz1, inv1, h2,
    packed, g0, v0, v1, g1,
    buf0, bufp,
):
    top = BASE // 2
    planes, _, width = g0.shape
    block, rows = g_wide.shape[0], g_wide.shape[1] - BASE
    g0[HALO : HALO + block] = g_wide[...]
    strips, _ = plane_strips(rows)
    for distance, cut, tiles, at in strips:
        for choose, plane in ((below, HALO - distance), (above, planes - HALO - 1 + distance)):
            value = choose(g_near[at : at + tiles], g_far[at : at + tiles], "gx")
            g0[plane, top + cut : top + cut + 8 * tiles, :] = value.reshape(8 * tiles, width)

    aG0, aV0, aV1, aG1 = (g0, 0, top), (v0, 1, BASE), (v1, 1, BASE), (g1, 0, BASE)
    w0 = (wx0, 1, BASE), (wy0, 0, BASE), (wz0, 0, BASE)
    w1 = (wx1, 1, BASE), (wy1, 0, BASE), (wz1, 0, BASE)
    for window in diamond(planes, rows, HALO - 1):
        write(aV0, window[0], window[2], read((inv0, 0, BASE), *window) * read(aG0, *window))
    for window in diamond(planes, rows, HALO - 2):
        start, _, above_rows, _ = window
        _, around = spread(aV0, w0, window, 1)
        r = KEEP * read(aG0, *window) + around
        write(aG1, start // 2, above_rows // 2, sum_blocks(r, buf0.at[start // 2 :], 1) * 0.125)

    planes1, rows1 = planes // 2, -(-rows // 16) * 8
    window = (0, planes1, 0, rows1)
    write(aV1, 0, 0, read((inv1, 0, BASE), *window) * read(aG1, *window))
    low = HALO // 2
    window = (low, planes1 - HALO, low, rows // 2 - HALO)
    _, around = spread(aV1, w1, window, 2)
    g2 = halve_rows(halve_planes(KEEP * read(aG1, *window) + around), buf0) * 0.125
    send_to_all(packed, pack_block([g2, h2[...]], bufp))


def second_kernel(
    got, g0, wx0, wy0, wz0, inv0, tot0, v0, wx1, wy1, wz1, inv1, v1, g1,
    packed, v0n, v1n, g1n, *rest,
):
    levels, (g2, h2, buf2, wide, around, doubled, u1, e0, u0, v0m, buf0, bufp) = rest[:11], rest[11:]
    count, rows2, width = g2.shape
    gy_count = lax.axis_size("gy")
    block2 = rows2 // gy_count

    def unpack(i):
        for x in range(UNPACK):
            for y in range(gy_count):
                both = got[y * count + i + x]
                g2[i + x, y * block2 : (y + 1) * block2, :] = both[:block2]
                h2[i + x, y * block2 : (y + 1) * block2, :] = both[block2:]

    slabs(0, count, UNPACK, unpack)

    span = width // 4
    h = h2[...]
    level2 = whole_faces(h, span, span, 1)
    h3 = sum_whole_blocks(h, buf2) * (1.0 / 32.0)
    level3 = coarse_faces(h3, span, 2 * span, 2)
    for ref, value in zip(levels, level2 + level3):
        ref[...] = value
    spread_out(coarse_cycle(g2[...], level2, level3, buf2), wide, around, doubled, range(1, 11))

    top = BASE // 2
    planes = g0.shape[0]
    block = planes - 2 * HALO
    aG0 = (g0, 0, top)
    w0 = (wx0, 1, BASE), (wy0, 0, BASE), (wz0, 0, BASE)
    aINV0, aTOT0, aV0 = (inv0, 0, BASE), (tot0, 0, BASE), (v0, 1, BASE)
    w1 = (wx1, 1, BASE), (wy1, 0, BASE), (wz1, 0, BASE)
    aINV1, aG1, aV1 = (inv1, 0, BASE), (g1, 0, BASE), (v1, 1, BASE)

    low, block1 = HALO // 2, block // 2
    aU1 = (u1, 1, BASE)
    window = (0, planes // 2, 0, planes // 4 // 8 * 8 + 16)
    e1 = doubled[1 : 1 + planes // 4, 2 : 2 + window[3], :]
    write(aU1, 0, 0, read(aV1, *window) + double_planes(e1))
    window = (low - 4, block1 + 8, low - 4, block1 + 8)
    here, around = spread(aU1, w1, window, 2)
    swept = KEEP * here + read(aINV1, *window) * (read(aG1, *window) + around)
    double_rows(e0, low - 4, swept)

    rows = block + 16
    aU0 = (u0, 1, BASE - (HALO - 7))
    aE0 = (e0, 0, -(2 * low - 8))
    aV0M = (v0m, 1, BASE - (HALO - 6))
    aV0N = (v0n, 1, BASE - (HALO - 5))
    size = block + 16

    def correct(i):
        window = (i, size, HALO - 7, rows)
        e = double_planes(read(aE0, i // 2, size // 2, HALO - 7, rows))
        write(aU0, i, HALO - 7, read(aV0, *window) + e)

    slabs(HALO - 8, planes - HALO + 8, size, correct)

    def sweep(source, target, margin, size):
        def body(i):
            window = (i, size, HALO - margin, rows)
            here, around = spread(source, w0, window, 1)
            value = KEEP * here + read(aINV0, *window) * (read(aG0, *window) + around)
            write(target, i, HALO - margin, value)

        slabs(HALO - margin, planes - HALO + margin, size, body)

    sweep(aU0, aV0M, 6, block + 12)
    sweep(aV0M, aV0N, 5, block + 10)

    aG1N, aV1N = (g1n, 0, BASE - (low - 2)), (v1n, 1, BASE - (low - 2))
    window = (HALO - 4, block + 8, HALO - 4, block + 8)
    here, around = spread(aV0N, w0, window, 1)
    r = (read(aG0, *window) - read(aTOT0, *window) * here) + around
    write(aG1N, low - 2, low - 2, sum_blocks(r, buf0, 1) * 0.125)

    window = (low - 2, block1 + 4, low - 2, block1 + 4)
    write(aV1N, low - 2, low - 2, read(aINV1, *window) * read(aG1N, *window))
    window = (low, block1, low, block1)
    _, around = spread(aV1N, w1, window, 2)
    g2 = halve_rows(halve_planes(KEEP * read(aG1N, *window) + around), buf0) * 0.125
    send_to_all(packed, pack_block([g2], bufp))


def third_kernel(
    got, g0, wx0, wy0, wz0, inv0, v0n, wx1, wy1, wz1, inv1, v1n, g1n, *rest,
):
    levels, (out, g2, buf2, wide, around, doubled, u1, e0, u0) = rest[:11], rest[11:]
    count, rows2, width = g2.shape
    gy_count = lax.axis_size("gy")
    block2 = rows2 // gy_count

    def unpack(i):
        for x in range(UNPACK):
            for y in range(gy_count):
                g2[i + x, y * block2 : (y + 1) * block2, :] = got[y * count + i + x]

    slabs(0, count, UNPACK, unpack)
    values = [ref[...] for ref in levels]
    spread_out(coarse_cycle(g2[...], values[:4], values[4:], buf2), wide, around, doubled, range(3, 9))

    top = BASE // 2
    planes = g0.shape[0]
    block = planes - 2 * HALO
    aG0, aINV0 = (g0, 0, top), (inv0, 0, BASE)
    w0 = (wx0, 1, BASE), (wy0, 0, BASE), (wz0, 0, BASE)
    w1 = (wx1, 1, BASE), (wy1, 0, BASE), (wz1, 0, BASE)
    low, block1 = HALO // 2, block // 2
    aINV1 = (inv1, 0, BASE)
    aG1N, aV1N = (g1n, 0, BASE - (low - 2)), (v1n, 1, BASE - (low - 2))
    aV0N = (v0n, 1, BASE - (HALO - 5))

    aU1 = (u1, 1, BASE - (low - 2))
    window = (low - 2, block1 + 4, low - 2, block1 + 4)
    e1 = doubled[low // 2 : low // 2 + block1 // 2 + 2, low : low + block1 + 4, :]
    write(aU1, low - 2, low - 2, read(aV1N, *window) + double_planes(e1))
    window = (low - 1, block1 + 2, low - 1, block1 + 2)
    here, around = spread(aU1, w1, window, 2)
    swept = KEEP * here + read(aINV1, *window) * (read(aG1N, *window) + around)
    double_rows(e0, low - 1, swept)

    aU0 = (u0, 1, BASE - (HALO - 1))
    aE0 = (e0, 0, -(2 * low - 2))
    size = block + 4
    rows = block + 2

    def correct(i):
        window = (i, size, HALO - 1, rows)
        e = double_planes(read(aE0, i // 2, size // 2, HALO - 1, rows))
        write(aU0, i, HALO - 1, read(aV0N, *window) + e)

    slabs(HALO - 2, planes - HALO + 2, size, correct)

    def sweep(i):
        window = (i, size, HALO, block)
        here, around = spread(aU0, w0, window, 1)
        out[pl.ds(i - HALO, size)] = KEEP * here + read(aINV0, *window) * (read(aG0, *window) + around)

    size = block
    slabs(HALO, planes - HALO, size, sweep)


def kernel_call(body, outs, scratch, args):
    def size(shape):
        total = 4
        for length in shape:
            total *= length
        return total

    shapes = [a.shape for a in args] + list(outs) + list(scratch)
    limit = sum(size(s) for s in shapes) + (8 << 20)
    return pl.pallas_call(
        body,
        out_shape=[jax.ShapeDtypeStruct(s, F32) for s in outs],
        in_specs=[pl.BlockSpec(memory_space=pltpu.VMEM)] * len(args),
        out_specs=[pl.BlockSpec(memory_space=pltpu.VMEM)] * len(outs),
        scratch_shapes=[pltpu.VMEM(s, F32) for s in scratch],
        compiler_params=pltpu.CompilerParams(vmem_limit_bytes=limit),
    )(*args)


def local(right_side, material, conductivity):
    bx, by, bz = right_side.shape
    gx_count, gy_count = lax.axis_size("gx"), lax.axis_size("gy")
    devices = gx_count * gy_count

    X, Y = bx + 2 * HALO, by + 2 * HALO
    YA = Y + BASE
    YB = Y + 2 * BASE
    X1, Y1 = X // 2, -(-Y // 16) * 8 + 2 * BASE
    xb, yb = bx // 4, by // 4

    k_near, k_far = trade(material, material, "gx")
    g_near, g_far = trade(right_side, right_side, "gy")
    table, h, h_near, right = kernel_call(
        own_kernel,
        [(8, bz), (bx, by, bz), (HALO, by, bz), (bx, by, bz)],
        [],
        [conductivity[None], material, right_side, k_near],
    )
    strip = (plane_strips(Y)[1], 8, bz)
    g_wide, g_near, g_far = kernel_call(
        g_kernel, [(bx, YA, bz), strip, strip], [], [right, g_near, g_far]
    )
    strip = (strip_tiles(diamond_strips(X)), NEAR, bz)
    k_wide, k_near, k_far = kernel_call(
        k_kernel, [(X, by, bz), strip, strip], [], [h, h_near, k_far, table]
    )
    g_near, g_far = trade(g_near, g_far, "gx")
    k_near, k_far = trade(k_near, k_far, "gy")

    pad0, full0, pad1, full1 = (X + 2, YB, bz), (X, YB, bz), (X1 + 2, Y1, bz), (X1, Y1, bz)
    wx0, wy0, wz0, inv0, tot0, wx1, wy1, wz1, inv1, h2 = kernel_call(
        faces_kernel,
        [pad0, full0, full0, full0, full0, pad1, full1, full1, full1, (xb, yb, bz)],
        [(X + 2, YA, bz), pad1, (X1, Y, bz)],
        [k_wide, k_near, k_far],
    )
    packed, g0, v0, v1, g1 = kernel_call(
        first_kernel,
        [(devices, 2 * yb, bz), (X, YA, bz), pad0, pad1, full1],
        [(X1, Y, bz), (xb, 8, bz)],
        [g_wide, g_near, g_far, wx0, wy0, wz0, inv0, wx1, wy1, wz1, inv1, h2],
    )
    got = everywhere(packed)
    level2 = (gx_count, gy_count * yb, bz)
    level3 = (gx_count, gy_count * yb // 2, bz)
    coarse_scratch = [
        level2, (gx_count + 2, gy_count + 2, yb, bz), (3, 16, bz), (3 * xb, 32, bz), pad1, (X1, by + 24, bz), pad0,
    ]
    packed, v0n, v1n, g1n, *levels = kernel_call(
        second_kernel,
        [(devices, yb, bz), pad0, pad1, full1] + [level2] * 4 + [level3] * 7,
        [level2, level2] + coarse_scratch + [pad0, (X1, Y, bz), (xb, 8, bz)],
        [got, g0, wx0, wy0, wz0, inv0, tot0, v0, wx1, wy1, wz1, inv1, v1, g1],
    )
    got = everywhere(packed)
    (out,) = kernel_call(
        third_kernel,
        [(bx, by, bz)],
        [level2] + coarse_scratch,
        [got, g0, wx0, wy0, wz0, inv0, v0n, wx1, wy1, wz1, inv1, v1n, g1n] + levels,
    )
    return out


def solution(mesh):
    return jax.shard_map(
        local,
        mesh=mesh,
        in_specs=(P("gx", "gy", None), P("gx", "gy", None), P()),
        out_specs=P("gx", "gy", None),
        check_vma=False,
    )
```

```python
import jax
import jax.numpy as jnp
from jax import lax
from jax.experimental import pallas as pl
from jax.experimental.pallas import tpu as pltpu
from jax.sharding import PartitionSpec as P

COARSE_SWEEPS = 6
OMEGA = 0.8
KEEP = 1.0 - OMEGA
HALO = 12
NEAR = 8
FAR = HALO - NEAR
BASE = 8
UNPACK = 8
F32 = jnp.float32


def near_partner(index, count):
    return index ^ 1 if index ^ 1 < count else index


def far_partner(index, count):
    return (index - 1 ^ 1) + 1


def route(axis, far):
    gx_count, gy_count = lax.axis_size("gx"), lax.axis_size("gy")
    pairs = []
    for x in range(gx_count):
        for y in range(gy_count):
            if axis == "gx":
                if not far:
                    a, b = near_partner(x, gx_count), y
                elif 0 < x < gx_count - 1:
                    a, b = far_partner(x, gx_count), y
                else:
                    a, b = x, near_partner(y, gy_count)
            else:
                if not far:
                    a, b = x, near_partner(y, gy_count)
                elif 0 < y < gy_count - 1:
                    a, b = x, far_partner(y, gy_count)
                else:
                    a, b = near_partner(x, gx_count), y
            pairs.append((x * gy_count + y, a * gy_count + b))
    return pairs


def trade(to_near, to_far, axis):
    from_far = lax.ppermute(to_far, ("gx", "gy"), route(axis, True))
    from_near = lax.ppermute(to_near, ("gx", "gy"), route(axis, False))
    return from_near, from_far


def everywhere(copies):
    return lax.all_to_all(copies, ("gy", "gx"), 0, 0)


def is_odd(axis):
    return lax.axis_index(axis) % 2 == 1


def has_below(axis):
    return lax.axis_index(axis) > 0


def has_above(axis):
    return lax.axis_index(axis) < lax.axis_size(axis) - 1


def below(near, far, axis):
    return jnp.where(has_below(axis), jnp.where(is_odd(axis), near, far), 0.0)


def above(near, far, axis):
    return jnp.where(has_above(axis), jnp.where(is_odd(axis), far, near), 0.0)


def roll(value, shift, axis):
    return pltpu.roll(value, shift % value.shape[axis], axis=axis)


def lanes_of(value):
    return lax.broadcasted_iota(jnp.int32, value.shape, value.ndim - 1)


def rows_of(value):
    return lax.broadcasted_iota(jnp.int32, value.shape, value.ndim - 2)


def lane_row(width):
    return lax.broadcasted_iota(jnp.int32, (1, width), 1)


def pick_lanes(value, index):
    flat = value.reshape(-1, value.shape[-1])
    index = jnp.broadcast_to(index, flat.shape)
    return jnp.take_along_axis(flat, index, axis=1).reshape(value.shape)


def add_partner(value, apart):
    return value + pick_lanes(value, lane_row(value.shape[-1]) ^ apart)


def shift_up(value):
    return jnp.concatenate([value[1:], jnp.zeros_like(value[:1])], axis=0)


def shift_down(value):
    return jnp.concatenate([jnp.zeros_like(value[:1]), value[:-1]], axis=0)


def next_x(value, step):
    turned = roll(value, -step, 2)
    return jnp.where(lanes_of(value) < value.shape[-1] - step, turned, shift_up(turned))


def prev_x(value, step):
    turned = roll(value, step, 2)
    return jnp.where(lanes_of(value) >= step, turned, shift_down(turned))


def whole_faces(h, span, xstep, zstep):
    in_span = lanes_of(h) % span
    row = rows_of(h)
    not_last_z, not_first_z = in_span < span - zstep, in_span >= zstep
    not_last_y, not_first_y = row < h.shape[1] - 1, row >= 1
    wx = h + next_x(h, xstep)
    wy = h + jnp.where(not_last_y, roll(h, -1, 1), 0.0)
    wz = h + jnp.where(not_last_z, roll(h, -zstep, 2), 0.0)
    back = h + prev_x(h, xstep)
    back = back + (h + jnp.where(not_first_y, roll(h, 1, 1), 0.0))
    back = back + (h + jnp.where(not_first_z, roll(h, zstep, 2), 0.0))
    total = wx + wy + wz + back
    return wx, jnp.where(not_last_y, wy, 0.0), jnp.where(not_last_z, wz, 0.0), OMEGA / total


def whole_spread(v, wx, wy, wz, xstep, zstep):
    return (
        (wx * next_x(v, xstep) + prev_x(wx * v, xstep))
        + (wy * roll(v, -1, 1) + roll(wy * v, 1, 1))
        + (wz * roll(v, -zstep, 2) + roll(wz * v, zstep, 2))
    )


def coarse_faces(h, span, xstep, zstep):
    wx, wy, wz, inverse = whole_faces(h, span, xstep, zstep)
    return wx, prev_x(wx, xstep), wy, roll(wy, 1, 1), wz, roll(wz, zstep, 2), inverse


def coarse_spread(v, wx, wx_back, wy, wy_back, wz, wz_back, zstep):
    turned = roll(v, v.shape[-1] // 2, 2)
    low = lanes_of(v) < v.shape[-1] // 2
    after = jnp.where(low, turned, shift_up(turned))
    before = jnp.where(low, shift_down(turned), turned)
    return (
        (wx * after + wx_back * before)
        + (wy * roll(v, -1, 1) + wy_back * roll(v, 1, 1))
        + (wz * roll(v, -zstep, 2) + wz_back * roll(v, zstep, 2))
    )


def read(array, start, size, top, rows, dx=0, dy=0):
    ref, planes_off, rows_off = array
    return ref[pl.ds(start + planes_off + dx, size), pl.ds(top + rows_off + dy, rows), :]


def write(array, start, top, value):
    ref, planes_off, rows_off = array
    ref[pl.ds(start + planes_off, value.shape[0]), pl.ds(top + rows_off, value.shape[1]), :] = value


def slabs(first, last, size, body):
    if first + size == last:
        body(first)
        return

    def step(i, carry):
        body(first + i * size)
        return carry

    lax.fori_loop(0, (last - first) // size, step, 0)


def faces(h, window, step):
    here = read(h, *window)
    lane = lanes_of(here)
    width = here.shape[-1]
    not_last = lane < width - step
    wx = here + read(h, *window, dx=1)
    wy = here + read(h, *window, dy=1)
    wz = here + jnp.where(not_last, roll(here, -step, 2), 0.0)
    back = (here + read(h, *window, dx=-1)) + (here + read(h, *window, dy=-1))
    back = back + (here + jnp.where(lane >= step, roll(here, step, 2), 0.0))
    total = (wx + wy + wz) + back
    inverse = jnp.where(here > 0.0, OMEGA / total, 0.0)
    return here, wx, wy, jnp.where(not_last, wz, 0.0), total, inverse


def spread(v, weights, window, step):
    wx, wy, wz = weights
    here = read(v, *window)
    wz = read(wz, *window)
    return here, (
        (read(wx, *window) * read(v, *window, dx=1) + read(wx, *window, dx=-1) * read(v, *window, dx=-1))
        + (read(wy, *window) * read(v, *window, dy=1) + read(wy, *window, dy=-1) * read(v, *window, dy=-1))
        + (wz * roll(here, -step, 2) + roll(wz * here, step, 2))
    )


def diamond(planes, rows, reach):
    groups = {}
    for distance in range(0, reach + 2, 2):
        rest = reach - max(distance - 1, 0)
        wide = -(-(rows - 2 * HALO + 2 * rest) // 8) * 8
        top = HALO - (wide - (rows - 2 * HALO)) // 2
        first, last = groups.get((top, wide), (distance, distance))
        groups[(top, wide)] = (first, distance)
    found = []
    for (top, wide), (first, last) in groups.items():
        if first == 0:
            found.append((HALO - last, planes - 2 * HALO + 2 * last, top, wide))
        else:
            size = last - first + 2
            found.append((HALO - last, size, top, wide))
            found.append((planes - HALO + first - 2, size, top, wide))
    return found


def halve_rows(value, buffer):
    count, rows, _ = value.shape
    buffer[0:count, 0:rows, :] = value
    return (
        buffer[0:count, pl.ds(0, rows // 2, stride=2), :] + buffer[0:count, pl.ds(1, rows // 2, stride=2), :]
    )


def halve_planes(value):
    pairs = value.reshape((value.shape[0] // 2, 2) + value.shape[1:])
    return pairs[:, 0] + pairs[:, 1]


def sum_blocks(value, buffer, step):
    return add_partner(halve_rows(halve_planes(value), buffer), step)


def double_rows(ref, start, value):
    count, rows, _ = value.shape
    ref[pl.ds(start, count), pl.ds(0, rows, stride=2), :] = value
    ref[pl.ds(start, count), pl.ds(1, rows, stride=2), :] = value


def double_planes(value):
    wide = jnp.broadcast_to(value[:, None], (value.shape[0], 2) + value.shape[1:])
    return wide.reshape((2 * value.shape[0],) + value.shape[1:])


def pack_block(values, buffer):
    blocks, rows, width = values[0].shape
    span = width // blocks
    for n, value in enumerate(values):
        buffer[:, n * rows : (n + 1) * rows, :] = value
    used = rows * len(values)
    lane = lane_row(width)
    first = (lane % span) * blocks
    packed = None
    for x in range(blocks):
        picked = (pick_lanes(buffer[x], first) + pick_lanes(buffer[x], first + blocks // 2))[:used]
        packed = picked if packed is None else jnp.where(lanes_of(picked) // span == x, picked, packed)
    return packed


def send_to_all(packed, chunk):
    copies = min(packed.shape[0], 32)

    def copy_out(i):
        packed[pl.ds(i, copies)] = jnp.broadcast_to(chunk[None], (copies,) + chunk.shape)

    slabs(0, packed.shape[0], copies, copy_out)


def sum_whole_blocks(value, buffer):
    halved = halve_rows(value, buffer)
    lane = lane_row(value.shape[-1])
    span = value.shape[-1] // 4
    return (halved + pick_lanes(halved, lane ^ 1)) + (
        pick_lanes(halved, lane ^ span) + pick_lanes(halved, lane ^ span ^ 1)
    )


def coarse_cycle(g2, level2, level3, buffer):
    wx2, wy2, wz2, inv2 = level2
    *w3, inv3 = level3
    span = g2.shape[-1] // 4
    v2 = inv2 * g2
    r2 = KEEP * g2 + whole_spread(v2, wx2, wy2, wz2, span, 1)
    g3 = 0.125 * sum_whole_blocks(r2, buffer)
    v3 = inv3 * g3
    for _ in range(COARSE_SWEEPS - 1):
        v3 = KEEP * v3 + inv3 * (g3 + coarse_spread(v3, *w3, 2))
    double_rows(buffer, 0, v3)
    u2 = v2 + buffer[...]
    return KEEP * u2 + inv2 * (g2 + whole_spread(u2, wx2, wy2, wz2, span, 1))


def spread_out(e2, wide, around, doubled, planes):
    count, rows, width = e2.shape
    blocks = lax.axis_size("gy")
    block = rows // blocks
    span = width // 4
    for edge in (0, count + 1):
        wide[edge] = jnp.zeros(wide.shape[1:], F32)
    for edge in (0, blocks + 1):
        wide[:, edge] = jnp.zeros((count + 2,) + wide.shape[2:], F32)
    for y in range(blocks):
        wide[1 : count + 1, y + 1] = e2[:, y * block : (y + 1) * block]
    gx, gy = lax.axis_index("gx"), lax.axis_index("gy")
    for x in range(3):
        for y in range(3):
            around[x, y * block : (y + 1) * block, :] = wide[gx + x, gy + y]
    lane = lane_row(width)
    kept = 3 * block
    for j in planes:
        value = pick_lanes(around[j // 4], (j % 4) * span + lane // 4)[:kept]
        doubled[j, pl.ds(0, kept, stride=2), :] = value
        doubled[j, pl.ds(1, kept, stride=2), :] = value


def row_starts(axis, block):
    odd = is_odd(axis)
    low = (0, 0, NEAR)
    high = (block - NEAR, block - FAR, block - HALO)
    to_near = [jnp.where(odd, a, b) for a, b in zip(low, high)]
    to_far = [jnp.where(odd, b, a) for a, b in zip(low, high)]
    return to_near, to_far


def diamond_strips(planes):
    full = (HALO - NEAR + 1, planes - HALO + NEAR - 1)
    far = HALO - FAR + 1
    half = planes // 2 - far
    return full, (1, full[1], full[0] - 1), (far, far + half, half)


def strip_tiles(strips):
    (first, last), (_, _, edge), (_, _, half) = strips
    return last - first + edge + half


def pack_rows(source, starts, strips, target):
    (first, last), *halves = strips
    at = last - first
    target[0:at] = source[first:last, pl.ds(starts[0], NEAR), :]
    for start, (one, two, count) in zip(starts[1:], halves):
        if count:
            target[at : at + count, 0:FAR, :] = source[one : one + count, pl.ds(start, FAR), :]
            target[at : at + count, FAR:NEAR, :] = source[two : two + count, pl.ds(start, FAR), :]
        at += count


def unpack_rows(target, planes_off, top, bottom, strips, near, far):
    (first, last), *halves = strips
    for choose, rows in ((below, (top - NEAR, top - FAR, top - HALO)), (above, (bottom, bottom, bottom + NEAR))):
        at = last - first
        target[planes_off + first : planes_off + last, rows[0] : rows[0] + NEAR, :] = choose(
            near[0:at], far[0:at], "gy"
        )
        for row, (one, two, count) in zip(rows[1:], halves):
            if count:
                both = choose(near[at : at + count], far[at : at + count], "gy")
                for plane, value in ((planes_off + one, both[:, 0:FAR]), (planes_off + two, both[:, FAR:NEAR])):
                    target[plane : plane + count, row : row + FAR, :] = value
            at += count


def own_kernel(cond, material, right_in, near, table, h, h_near, right):
    table[...] = jnp.zeros(table.shape, F32)
    table[0:1, 0 : cond.shape[1]] = 0.5 * cond[...]
    h[...] = look_up(material[...], table)
    first = jnp.where(is_odd("gx"), near.shape[0] - HALO, 0)
    h_near[...] = look_up(near[pl.ds(first, HALO)], table)
    right[...] = right_in[...]


def look_up(ids, table):
    planes, rows, width = ids.shape
    ids = ids.reshape(planes * rows, width)
    values = jnp.broadcast_to(table[0:1, :], ids.shape)
    return jnp.take_along_axis(values, ids, axis=1).reshape(planes, rows, width)


def k_kernel(h, h_near, far, table, wide, k_near, k_far):
    block = h.shape[0]
    first = jnp.where(is_odd("gx"), 0, block - HALO)
    h_far = look_up(far[pl.ds(first, HALO)], table)
    wide[0:HALO] = below(h_near[...], h_far, "gx")
    wide[HALO : HALO + block] = h[...]
    wide[HALO + block :] = above(h_near[...], h_far, "gx")
    strips = diamond_strips(wide.shape[0])
    to_near, to_far = row_starts("gy", wide.shape[1])
    pack_rows(wide, to_near, strips, k_near)
    pack_rows(wide, to_far, strips, k_far)


def plane_strips(rows):
    strips, at = [], 0
    for distance in range(1, HALO):
        cut = HALO - -(-(HALO - 1 - distance) // 4) * 4
        tiles = (rows - 2 * cut) // 8
        strips.append((distance, cut, tiles, at))
        at += tiles
    return strips, at


def g_kernel(right, near, far, wide, g_near, g_far):
    block, rows, _ = right.shape
    top = BASE // 2
    wide[:, top + HALO : top + HALO + rows, :] = right[...]
    wide[:, top : top + HALO, :] = below(near[:, rows - HALO :], far[:, rows - HALO :], "gy")
    wide[:, top + HALO + rows : top + 2 * HALO + rows, :] = above(near[:, :HALO], far[:, :HALO], "gy")
    odd = is_odd("gx")
    strips, _ = plane_strips(rows + 2 * HALO)
    for distance, cut, tiles, at in strips:
        low, high = distance - 1, block - distance
        for target, plane in ((g_near, jnp.where(odd, low, high)), (g_far, jnp.where(odd, high, low))):
            for tile in range(tiles):
                target[at + tile] = wide[plane, top + cut + 8 * tile : top + cut + 8 * tile + 8, :]


def faces_kernel(
    k_wide, k_near, k_far,
    wx0, wy0, wz0, inv0, tot0, wx1, wy1, wz1, inv1, h2,
    h0, h1, buf0,
):
    top = BASE // 2
    planes, rows, _ = k_wide.shape
    h0[1 : planes + 1, top + HALO : top + HALO + rows, :] = k_wide[...]
    unpack_rows(h0, 1, top + HALO, top + HALO + rows, diamond_strips(planes), k_near, k_far)
    rows = rows + 2 * HALO

    aH0, aWX0, aH1, aWX1 = (h0, 1, top), (wx0, 1, BASE), (h1, 1, BASE), (wx1, 1, BASE)
    for window in diamond(planes, rows, HALO - 1):
        start, _, above_rows, _ = window
        _, wx, wy, wz, total, inverse = faces(aH0, window, 1)
        write(aWX0, start, above_rows, wx)
        for ref, value in ((wy0, wy), (wz0, wz), (tot0, total), (inv0, inverse)):
            write((ref, 0, BASE), start, above_rows, value)
    write(aH1, 0, 0, sum_blocks(read(aH0, 0, planes, 0, rows), buf0, 1) * (1.0 / 32.0))

    planes1, rows1 = planes // 2, -(-rows // 16) * 8
    _, wx, wy, wz, _, inverse = faces(aH1, (0, planes1, 0, rows1), 2)
    write(aWX1, 0, 0, wx)
    for ref, value in ((wy1, wy), (wz1, wz), (inv1, inverse)):
        write((ref, 0, BASE), 0, 0, value)
    low = HALO // 2
    own = read(aH1, low, planes1 - HALO, low, rows // 2 - HALO)
    h2[...] = halve_rows(halve_planes(own), buf0) * (1.0 / 32.0)


def first_kernel(
    g_wide, g_near, g_far, wx0, wy0, wz0, inv0, wx1, wy1, wz1, inv1, h2,
    packed, g0, v0, v1, g1,
    buf0, bufp,
):
    top = BASE // 2
    planes, _, width = g0.shape
    block, rows = g_wide.shape[0], g_wide.shape[1] - BASE
    g0[HALO : HALO + block] = g_wide[...]
    strips, _ = plane_strips(rows)
    for distance, cut, tiles, at in strips:
        for choose, plane in ((below, HALO - distance), (above, planes - HALO - 1 + distance)):
            value = choose(g_near[at : at + tiles], g_far[at : at + tiles], "gx")
            g0[plane, top + cut : top + cut + 8 * tiles, :] = value.reshape(8 * tiles, width)

    aG0, aV0, aV1, aG1 = (g0, 0, top), (v0, 1, BASE), (v1, 1, BASE), (g1, 0, BASE)
    w0 = (wx0, 1, BASE), (wy0, 0, BASE), (wz0, 0, BASE)
    w1 = (wx1, 1, BASE), (wy1, 0, BASE), (wz1, 0, BASE)
    for window in diamond(planes, rows, HALO - 1):
        write(aV0, window[0], window[2], read((inv0, 0, BASE), *window) * read(aG0, *window))
    for window in diamond(planes, rows, HALO - 2):
        start, _, above_rows, _ = window
        _, around = spread(aV0, w0, window, 1)
        r = KEEP * read(aG0, *window) + around
        write(aG1, start // 2, above_rows // 2, sum_blocks(r, buf0.at[start // 2 :], 1) * 0.125)

    planes1, rows1 = planes // 2, -(-rows // 16) * 8
    window = (0, planes1, 0, rows1)
    write(aV1, 0, 0, read((inv1, 0, BASE), *window) * read(aG1, *window))
    low = HALO // 2
    window = (low, planes1 - HALO, low, rows // 2 - HALO)
    _, around = spread(aV1, w1, window, 2)
    g2 = halve_rows(halve_planes(KEEP * read(aG1, *window) + around), buf0) * 0.125
    send_to_all(packed, pack_block([g2, h2[...]], bufp))


def second_kernel(
    got, g0, wx0, wy0, wz0, inv0, tot0, v0, wx1, wy1, wz1, inv1, v1, g1,
    packed, v0n, v1n, g1n, *rest,
):
    levels, (g2, h2, buf2, wide, around, doubled, u1, e0, u0, v0m, buf0, bufp) = rest[:11], rest[11:]
    count, rows2, width = g2.shape
    gy_count = lax.axis_size("gy")
    block2 = rows2 // gy_count

    def unpack(i):
        for x in range(UNPACK):
            for y in range(gy_count):
                both = got[y * count + i + x]
                g2[i + x, y * block2 : (y + 1) * block2, :] = both[:block2]
                h2[i + x, y * block2 : (y + 1) * block2, :] = both[block2:]

    slabs(0, count, UNPACK, unpack)

    span = width // 4
    h = h2[...]
    level2 = whole_faces(h, span, span, 1)
    h3 = sum_whole_blocks(h, buf2) * (1.0 / 32.0)
    level3 = coarse_faces(h3, span, 2 * span, 2)
    for ref, value in zip(levels, level2 + level3):
        ref[...] = value
    spread_out(coarse_cycle(g2[...], level2, level3, buf2), wide, around, doubled, range(1, 11))

    top = BASE // 2
    planes = g0.shape[0]
    block = planes - 2 * HALO
    aG0 = (g0, 0, top)
    w0 = (wx0, 1, BASE), (wy0, 0, BASE), (wz0, 0, BASE)
    aINV0, aTOT0, aV0 = (inv0, 0, BASE), (tot0, 0, BASE), (v0, 1, BASE)
    w1 = (wx1, 1, BASE), (wy1, 0, BASE), (wz1, 0, BASE)
    aINV1, aG1, aV1 = (inv1, 0, BASE), (g1, 0, BASE), (v1, 1, BASE)

    low, block1 = HALO // 2, block // 2
    aU1 = (u1, 1, BASE)
    window = (0, planes // 2, 0, planes // 4 // 8 * 8 + 16)
    e1 = doubled[1 : 1 + planes // 4, 2 : 2 + window[3], :]
    write(aU1, 0, 0, read(aV1, *window) + double_planes(e1))
    window = (low - 4, block1 + 8, low - 4, block1 + 8)
    here, around = spread(aU1, w1, window, 2)
    swept = KEEP * here + read(aINV1, *window) * (read(aG1, *window) + around)
    double_rows(e0, low - 4, swept)

    rows = block + 16
    aU0 = (u0, 1, BASE - (HALO - 7))
    aE0 = (e0, 0, -(2 * low - 8))
    aV0M = (v0m, 1, BASE // 2)
    aV0N = (v0n, 1, BASE // 2)
    size = block + 16

    def correct(i):
        window = (i, size, HALO - 7, rows)
        e = double_planes(read(aE0, i // 2, size // 2, HALO - 7, rows))
        write(aU0, i, HALO - 7, read(aV0, *window) + e)

    slabs(HALO - 8, planes - HALO + 8, size, correct)

    def sweep(source, target, margin):
        for window in diamond(planes, planes, margin):
            here, around = spread(source, w0, window, 1)
            value = KEEP * here + read(aINV0, *window) * (read(aG0, *window) + around)
            write(target, window[0], window[2], value)

    sweep(aU0, aV0M, 6)
    sweep(aV0M, aV0N, 5)

    aG1N, aV1N = (g1n, 0, BASE - (low - 2)), (v1n, 1, BASE - (low - 2))
    window = (HALO - 4, block + 8, HALO - 4, block + 8)
    here, around = spread(aV0N, w0, window, 1)
    r = (read(aG0, *window) - read(aTOT0, *window) * here) + around
    write(aG1N, low - 2, low - 2, sum_blocks(r, buf0, 1) * 0.125)

    window = (low - 2, block1 + 4, low - 2, block1 + 4)
    write(aV1N, low - 2, low - 2, read(aINV1, *window) * read(aG1N, *window))
    window = (low, block1, low, block1)
    _, around = spread(aV1N, w1, window, 2)
    g2 = halve_rows(halve_planes(KEEP * read(aG1N, *window) + around), buf0) * 0.125
    send_to_all(packed, pack_block([g2], bufp))


def third_kernel(
    got, g0, wx0, wy0, wz0, inv0, v0n, wx1, wy1, wz1, inv1, v1n, g1n, *rest,
):
    levels, (out, g2, buf2, wide, around, doubled, u1, e0, u0) = rest[:11], rest[11:]
    count, rows2, width = g2.shape
    gy_count = lax.axis_size("gy")
    block2 = rows2 // gy_count

    def unpack(i):
        for x in range(UNPACK):
            for y in range(gy_count):
                g2[i + x, y * block2 : (y + 1) * block2, :] = got[y * count + i + x]

    slabs(0, count, UNPACK, unpack)
    values = [ref[...] for ref in levels]
    spread_out(coarse_cycle(g2[...], values[:4], values[4:], buf2), wide, around, doubled, range(3, 9))

    top = BASE // 2
    planes = g0.shape[0]
    block = planes - 2 * HALO
    aG0, aINV0 = (g0, 0, top), (inv0, 0, BASE)
    w0 = (wx0, 1, BASE), (wy0, 0, BASE), (wz0, 0, BASE)
    w1 = (wx1, 1, BASE), (wy1, 0, BASE), (wz1, 0, BASE)
    low, block1 = HALO // 2, block // 2
    aINV1 = (inv1, 0, BASE)
    aG1N, aV1N = (g1n, 0, BASE - (low - 2)), (v1n, 1, BASE - (low - 2))
    aV0N = (v0n, 1, BASE // 2)

    aU1 = (u1, 1, BASE - (low - 2))
    window = (low - 2, block1 + 4, low - 2, block1 + 4)
    e1 = doubled[low // 2 : low // 2 + block1 // 2 + 2, low : low + block1 + 4, :]
    write(aU1, low - 2, low - 2, read(aV1N, *window) + double_planes(e1))
    window = (low - 1, block1 + 2, low - 1, block1 + 2)
    here, around = spread(aU1, w1, window, 2)
    swept = KEEP * here + read(aINV1, *window) * (read(aG1N, *window) + around)
    double_rows(e0, low - 1, swept)

    aU0 = (u0, 1, BASE - (HALO - 1))
    aE0 = (e0, 0, -(2 * low - 2))
    size = block + 4
    rows = block + 2

    def correct(i):
        window = (i, size, HALO - 1, rows)
        e = double_planes(read(aE0, i // 2, size // 2, HALO - 1, rows))
        write(aU0, i, HALO - 1, read(aV0N, *window) + e)

    slabs(HALO - 2, planes - HALO + 2, size, correct)

    def sweep(i):
        window = (i, size, HALO, block)
        here, around = spread(aU0, w0, window, 1)
        out[pl.ds(i - HALO, size)] = KEEP * here + read(aINV0, *window) * (read(aG0, *window) + around)

    size = block
    slabs(HALO, planes - HALO, size, sweep)


def kernel_call(body, outs, scratch, args):
    def size(shape):
        total = 4
        for length in shape:
            total *= length
        return total

    shapes = [a.shape for a in args] + list(outs) + list(scratch)
    limit = sum(size(s) for s in shapes) + (8 << 20)
    return pl.pallas_call(
        body,
        out_shape=[jax.ShapeDtypeStruct(s, F32) for s in outs],
        in_specs=[pl.BlockSpec(memory_space=pltpu.VMEM)] * len(args),
        out_specs=[pl.BlockSpec(memory_space=pltpu.VMEM)] * len(outs),
        scratch_shapes=[pltpu.VMEM(s, F32) for s in scratch],
        compiler_params=pltpu.CompilerParams(vmem_limit_bytes=limit),
    )(*args)


def local(right_side, material, conductivity):
    bx, by, bz = right_side.shape
    gx_count, gy_count = lax.axis_size("gx"), lax.axis_size("gy")
    devices = gx_count * gy_count

    X, Y = bx + 2 * HALO, by + 2 * HALO
    YA = Y + BASE
    YB = Y + 2 * BASE
    X1, Y1 = X // 2, -(-Y // 16) * 8 + 2 * BASE
    xb, yb = bx // 4, by // 4

    k_near, k_far = trade(material, material, "gx")
    g_near, g_far = trade(right_side, right_side, "gy")
    table, h, h_near, right = kernel_call(
        own_kernel,
        [(8, bz), (bx, by, bz), (HALO, by, bz), (bx, by, bz)],
        [],
        [conductivity[None], material, right_side, k_near],
    )
    strip = (plane_strips(Y)[1], 8, bz)
    g_wide, g_near, g_far = kernel_call(
        g_kernel, [(bx, YA, bz), strip, strip], [], [right, g_near, g_far]
    )
    strip = (strip_tiles(diamond_strips(X)), NEAR, bz)
    k_wide, k_near, k_far = kernel_call(
        k_kernel, [(X, by, bz), strip, strip], [], [h, h_near, k_far, table]
    )
    g_near, g_far = trade(g_near, g_far, "gx")
    k_near, k_far = trade(k_near, k_far, "gy")

    pad0, full0, pad1, full1 = (X + 2, YB, bz), (X, YB, bz), (X1 + 2, Y1, bz), (X1, Y1, bz)
    wx0, wy0, wz0, inv0, tot0, wx1, wy1, wz1, inv1, h2 = kernel_call(
        faces_kernel,
        [pad0, full0, full0, full0, full0, pad1, full1, full1, full1, (xb, yb, bz)],
        [(X + 2, YA, bz), pad1, (X1, Y, bz)],
        [k_wide, k_near, k_far],
    )
    packed, g0, v0, v1, g1 = kernel_call(
        first_kernel,
        [(devices, 2 * yb, bz), (X, YA, bz), pad0, pad1, full1],
        [(X1, Y, bz), (xb, 8, bz)],
        [g_wide, g_near, g_far, wx0, wy0, wz0, inv0, wx1, wy1, wz1, inv1, h2],
    )
    got = everywhere(packed)
    level2 = (gx_count, gy_count * yb, bz)
    level3 = (gx_count, gy_count * yb // 2, bz)
    coarse_scratch = [
        level2, (gx_count + 2, gy_count + 2, yb, bz), (3, 16, bz), (3 * xb, 32, bz), pad1, (X1, by + 24, bz), pad0,
    ]
    packed, v0n, v1n, g1n, *levels = kernel_call(
        second_kernel,
        [(devices, yb, bz), pad0, pad1, full1] + [level2] * 4 + [level3] * 7,
        [level2, level2] + coarse_scratch + [pad0, (X1, Y, bz), (xb, 8, bz)],
        [got, g0, wx0, wy0, wz0, inv0, tot0, v0, wx1, wy1, wz1, inv1, v1, g1],
    )
    got = everywhere(packed)
    (out,) = kernel_call(
        third_kernel,
        [(bx, by, bz)],
        [level2] + coarse_scratch,
        [got, g0, wx0, wy0, wz0, inv0, v0n, wx1, wy1, wz1, inv1, v1n, g1n] + levels,
    )
    return out


def solution(mesh):
    return jax.shard_map(
        local,
        mesh=mesh,
        in_specs=(P("gx", "gy", None), P("gx", "gy", None), P()),
        out_specs=P("gx", "gy", None),
        check_vma=False,
    )
```
